32 devices in a mesh: space: 4 (over z), rep: 8 (over y, x, core).
Axes of the slice: x: 2, y: 2, z: 4, core: 2. Of those that a mesh axis runs over, the one named last changes fastest.
Arguments:
- features: bfloat16 [8, 20, 96, 1024], P('rep', 'space'), may hold values from -4 to 4.5
- labels: int32 [8, 20, 96], P('rep', 'space'), may hold values from 0 to 2
- w_in: bfloat16 [29, 1024, 256], replicated, may hold values from -0.0625 to 0.0625
- w_proj: bfloat16 [1280, 256], replicated, may hold values from -0.15625 to 0.15625
- w_cls: bfloat16 [256, 3], replicated, may hold values from -0.375 to 0.375
- class_weight: float32 [3], replicated, may hold values from 0.5 to 4
- matching: int32 [8], replicated, may hold values from 0 to 7, as said below
Outputs:
- avg_in: float32 [8, 29696, 256], P('rep', 'space')
- avg_proj: float32 [8, 1280, 256], P('rep', 'space')
- avg_cls: float32 [8, 256, 3], P('rep', 'space')
The draws below stay inside these ranges and needn't reach their ends.
Inputs may be any that keep to these rules, and one draw needn't show every extreme that they name: matching[i] = i XOR matching[0] with matching[0] nonzero, so replicas are matched in pairs.
All inputs are finite; a program needn't handle non-finite values.
Results may differ from the reference program's by a relative error of at most 0.025.
The reference program's roundings to bfloat16 on the way count: a program that leaves them out, or rounds other values in their place, can miss the bound.
Values may be sent and summed in bfloat16 or wider, within the bound.
No kernel may reach another device: no remote copies, remote signals or barrier semaphores. Data moves between devices by JAX's collectives and lax.ppermute only.
A program may use at most 256 MiB of HBM per device.

```python
import math
import jax
import jax.numpy as jnp
from jax import lax

COLS = 96
C_IN = 1024
C_OUT = 256
CLS = 3
ROWS = 20
REPLICAS = 8
N_SPACE = 4


def draw_features(key, part):
    key_noise = jax.random.fold_in(key, 11)
    key_level = jax.random.fold_in(key, 12)
    shape = (REPLICAS, ROWS, COLS, C_IN)
    position = jnp.arange(ROWS, dtype=jnp.float32) / max(ROWS - 1, 1)
    level = jax.random.uniform(key_level, (REPLICAS, 1, 1, C_IN), jnp.float32, 0.03, 0.12)
    noise = jnp.clip(2.0 * jax.random.normal(key_noise, shape, jnp.float32), -4.0, 4.0)
    ramp = 1.0 + 2.0 * position
    return (noise + level * ramp[None, :, None, None]).astype(jnp.bfloat16)


def draw_matching(key, part):
    pair_bits = jax.random.randint(jax.random.fold_in(key, 21), (), 1, REPLICAS, dtype=jnp.int32)
    return jnp.bitwise_xor(jnp.arange(REPLICAS, dtype=jnp.int32), pair_bits)


def set_ends(result, rng, low, top_value):
    shape = result.shape
    index_at = [jax.random.randint(jax.random.fold_in(rng, axis), (), 0, shape[axis]) for axis in range(len(shape))]
    result = result.at[tuple(index_at)].set(low)
    longest = shape.index(max(shape))
    index_at[longest] = (index_at[longest] + 1) % shape[longest]
    return result.at[tuple(index_at)].set(top_value)


def scatter_about(rng, shape, width, bound, kind=jnp.bfloat16):
    values = width * jax.random.normal(rng, shape, jnp.float32)
    return jnp.clip(values, min=-bound, max=bound).astype(kind)


def setup_inputs(seed: int = 0) -> dict:
    seeds = jax.random.split(jax.random.key(seed), 8)
    features = draw_features(jax.random.fold_in(seeds[7], 71), 0)
    labels = set_ends(jax.random.randint(seeds[1], (REPLICAS, ROWS, COLS), 0, CLS), jax.random.fold_in(seeds[1], 1), 0, CLS - 1).astype(jnp.int32)
    w_in = scatter_about(seeds[2], (29, C_IN, C_OUT), (9 * C_IN) ** -0.5, 0.0625)
    w_proj = scatter_about(seeds[3], (5 * C_OUT, C_OUT), (5 * C_OUT) ** -0.5, 0.15625)
    w_cls = scatter_about(seeds[4], (C_OUT, CLS), C_OUT ** -0.5, 0.375)
    class_weight = jnp.clip(jnp.exp(jax.random.uniform(seeds[5], (CLS,), jnp.float32, math.log(0.5), math.log(4.0))), 0.5, 4.0)
    matching = draw_matching(jax.random.fold_in(seeds[7], 71), 0)
    return dict(features=features, labels=labels, w_in=w_in, w_proj=w_proj, w_cls=w_cls, class_weight=class_weight, matching=matching)


loss_scale = 1024.0


def shifted(values, offset, along):
    length = values.shape[along]
    extent = abs(offset)
    if extent >= length:
        return jnp.zeros_like(values)
    padding = [(0, 0)] * values.ndim
    padding[along] = (extent, extent)
    return lax.slice_in_dim(jnp.pad(values, padding), extent + offset, extent + offset + length, axis=along)


def block_terms(left, right):
    a = left.reshape(N_SPACE, -1, left.shape[-1]).astype(jnp.float32)
    b = right.reshape(N_SPACE, -1, right.shape[-1]).astype(jnp.float32)
    partial_value = jnp.einsum("spc,spo->sco", a, b, precision=lax.Precision.HIGHEST).astype(jnp.bfloat16)
    return jnp.sum(partial_value.astype(jnp.float32), axis=0)


def one_replica(inputs, w_in, w_proj, w_cls, class_weight):
    field_map, label_map = inputs
    height, col_count, in_width = field_map.shape
    out_width = w_proj.shape[1]
    pixels = height * col_count
    flat_rows = field_map.reshape(pixels, in_width)
    mean_in = (jnp.sum(field_map, axis=(0, 1), dtype=jnp.float32) / pixels).astype(jnp.bfloat16)
    pre_list = [jnp.dot(flat_rows, w_in[0], preferred_element_type=jnp.float32)]
    for k in range(1, 4):
        dilation = 12 * k
        pre_act = jnp.zeros((height, col_count, out_width), jnp.float32)
        for i in range(3):
            row_block = shifted(field_map, (i - 1) * dilation, 0).reshape(pixels, in_width)
            for j in range(3):
                product = jnp.dot(row_block, w_in[1 + 9 * (k - 1) + 3 * i + j], preferred_element_type=jnp.float32)
                pre_act = pre_act + shifted(product.reshape(height, col_count, out_width), (j - 1) * dilation, 1)
        pre_list.append(pre_act.reshape(pixels, out_width))
    pool_pre = jnp.dot(mean_in[None, :], w_in[28], preferred_element_type=jnp.float32)
    act_list = [jax.nn.relu(p).astype(jnp.bfloat16) for p in pre_list]
    pool_act = jnp.broadcast_to(jax.nn.relu(pool_pre).astype(jnp.bfloat16), (pixels, out_width))
    concat = jnp.concatenate(act_list + [pool_act], axis=1)
    y_pre = jnp.dot(concat, w_proj, preferred_element_type=jnp.float32)
    y_act = jax.nn.relu(y_pre).astype(jnp.bfloat16)
    logits = jnp.dot(y_act, w_cls, preferred_element_type=jnp.float32)
    exp_logits = jnp.exp(logits)
    softmax_out = exp_logits / jnp.sum(exp_logits, axis=1, keepdims=True)
    onehot = (label_map.reshape(pixels)[:, None] == jnp.arange(logits.shape[1], dtype=jnp.int32)[None, :]).astype(jnp.float32)
    weight = jnp.sum(onehot * class_weight[None, :], axis=1)
    d_logits = ((softmax_out - onehot) * weight[:, None] * (loss_scale / pixels)).astype(jnp.bfloat16)
    g_cls = block_terms(y_act, d_logits)
    d_y = (jnp.dot(d_logits, w_cls.T, preferred_element_type=jnp.float32) * (y_pre > 0)).astype(jnp.bfloat16)
    g_proj = block_terms(concat, d_y)
    d_cat = jnp.dot(d_y, w_proj.T, preferred_element_type=jnp.float32)
    grad_list = []
    d_first = (d_cat[:, :out_width] * (pre_list[0] > 0)).astype(jnp.bfloat16)
    grad_list.append(block_terms(flat_rows, d_first))
    for k in range(1, 4):
        dilation = 12 * k
        d_branch = (d_cat[:, k * out_width:(k + 1) * out_width] * (pre_list[k] > 0)).astype(jnp.bfloat16)
        d_branch = d_branch.reshape(height, col_count, out_width)
        for i in range(3):
            row_block = shifted(field_map, (i - 1) * dilation, 0)
            for j in range(3):
                grad_list.append(block_terms(row_block, shifted(d_branch, -(j - 1) * dilation, 1)))
    pool_grad = d_cat[:, 4 * out_width:] * (pool_pre > 0)
    s_pool = jnp.sum(pool_grad.reshape(N_SPACE, -1, out_width), axis=1)
    partial_value = (mean_in.astype(jnp.float32)[None, :, None] * s_pool[:, None, :]).astype(jnp.bfloat16)
    grad_list.append(jnp.sum(partial_value.astype(jnp.float32), axis=0))
    g_in = jnp.stack(grad_list).reshape(-1, out_width)
    return (g_in.astype(jnp.bfloat16), g_proj.astype(jnp.bfloat16), g_cls.astype(jnp.bfloat16))


def reference(features, labels, w_in, w_proj, w_cls, class_weight, matching):
    g_in, g_proj, g_cls = lax.map(lambda inputs: one_replica(inputs, w_in, w_proj, w_cls, class_weight), (features, labels))

    def average(grad):
        return (grad.astype(jnp.float32) + grad[matching].astype(jnp.float32)) * 0.5

    return (average(g_in), average(g_proj), average(g_cls))
```

```python
import functools

import jax
import jax.numpy as jnp
import numpy as np
from jax import lax
from jax.experimental import pallas as pl
from jax.experimental.pallas import tpu as pltpu
from jax.sharding import PartitionSpec as P

LOSS_SCALE = 1024.0
RATE = 12
EDGE = 40
BF16 = jnp.bfloat16
F32 = jnp.float32
VMEM_LIMIT = 60 * 1024 * 1024


def nn(a, b):
    return lax.dot_general(a, b, (((1,), (0,)), ((), ())), preferred_element_type=F32)


def nt(a, b):
    return lax.dot_general(a, b, (((1,), (1,)), ((), ())), preferred_element_type=F32)


def identity(size):
    rows = lax.broadcasted_iota(jnp.int32, (size, size), 0)
    cols = lax.broadcasted_iota(jnp.int32, (size, size), 1)
    return (rows == cols).astype(F32).astype(BF16)


class Plan:
    def __init__(self, n, reps, rows, cols, c_in, c_out, classes):
        self.n, self.reps, self.rows, self.cols = n, reps, rows, cols
        self.c_in, self.c_out, self.classes = c_in, c_out, classes
        self.height = rows * n
        self.pix = rows * cols
        self.total = self.pix * n
        self.shifted = [k for k in (1, 2, 3) if RATE * k < self.height]
        self.direct = [k for k in range(4) if k not in self.shifted]
        self.n_sh = len(self.shifted)
        self.units = 29
        self.unit_rows = c_in // n
        self.proj_rows = 5 * c_out // n
        self.cls_rows = c_out // n
        tables = [self.table(s) for s in range(n)]
        self.n_slots = max(t[1] for t in tables)
        self.tables = np.array([t[0] for t in tables], np.int32)

    def tap(self, t):
        if t == 0:
            return (0, 1, 1)
        if t == 28:
            return None
        k, rest = (t - 1) // 9 + 1, (t - 1) % 9
        a, b = rest // 3, rest % 3
        if a != 1 and k not in self.shifted:
            return "zero"
        return (k, a, b)

    def table(self, s):
        units = []
        for local in range(self.units):
            unit = s * self.units + local
            units.append((unit % self.n, unit // self.n, local))
        units.sort()
        slots = {}
        order, chan, slot, shift, low, high, kind = [], [], [], [], [], [], []
        for c, t, local in units:
            tap = self.tap(t)
            order.append(local)
            chan.append(c)
            if tap is None or tap == "zero":
                slot.append(0)
                shift.append(0)
                low.append(0)
                high.append(0)
                kind.append(1 if tap is None else 0)
                continue
            k, a, b = tap
            slot.append(slots.setdefault((k, b), len(slots)))
            move = (a - 1) * RATE * k
            shift.append(move)
            valid = [
                j for j in range(self.n)
                if any(0 <= self.rows * j + i - move < self.height for i in range(self.rows))
            ]
            low.append(valid[0])
            high.append(valid[-1] + 1)
            kind.append(0)
        flags = [slots.get((k, b), -1) for k in range(4) for b in range(3)]
        return order + chan + slot + shift + low + high + kind + flags + [s], len(slots)


def block_kernel(plan, n_cand, aliased, meta, *refs):
    rows, cols, c_in, c_out = plan.rows, plan.cols, plan.c_in, plan.c_out
    pix = plan.pix
    cands = refs[:n_cand]
    w_hbm = refs[n_cand]
    refs = refs[n_cand + 1 + (3 if aliased else 0):]
    xt_out, cat_out, s_out = refs[:3]
    xbuf, wbuf, xtb, catb, sb, pad_a, pad_b, sem_x, sem_w, sem_o, sem_s = refs[3:]
    step = pl.program_id(0)

    @pl.when(step == 0)
    def _():
        pad_a[:, :EDGE, :] = jnp.zeros((rows, EDGE, c_out), F32)
        pad_b[:, cols:, :] = jnp.zeros((rows, EDGE, c_out), F32)

    @pl.when(meta[step, 0] == 1)
    def _():
        source, block, field = meta[step, 1], meta[step, 2], meta[step, 3]

        def weights(first, count, slot):
            return pltpu.make_async_copy(
                w_hbm.at[pl.ds(first, count)], wbuf.at[slot, pl.ds(0, count)], sem_w.at[slot]
            )

        for c in range(n_cand):
            @pl.when(source == c)
            def _(c=c):
                pltpu.make_async_copy(cands[c], xbuf, sem_x).start()
        weights(0, 1, 0).start()
        pltpu.make_async_copy(cands[0], xbuf, sem_x).wait()

        flat = xbuf[...].reshape(pix, c_in)
        eye = identity(256)
        for c in range(c_in // 256):
            xtb[c * 256:(c + 1) * 256, :] = nt(eye, flat[:, c * 256:(c + 1) * 256]).astype(BF16)
        xt_copy = pltpu.make_async_copy(xtb, xt_out.at[field, block], sem_o.at[0])
        xt_copy.start()

        def in_field(move):
            first = block * rows + move
            return jnp.logical_and(first + rows - 1 >= 0, first < plan.height)

        def taps(k, slot):
            r = RATE * k
            width = -(-(cols - r) // 16) * 16
            low = r // 16 * 16
            left = nn(xbuf[:, :width, :].reshape(rows * width, c_in), wbuf[slot, 0])
            pad_a[:, EDGE:EDGE + width, :] = left.reshape(rows, width, c_out)
            right = nn(xbuf[:, low:, :].reshape(rows * (cols - low), c_in), wbuf[slot, 2])
            pad_b[:, low:cols, :] = right.reshape(rows, cols - low, c_out)
            mid = nn(xbuf[...].reshape(pix, c_in), wbuf[slot, 1])
            return (
                mid.reshape(rows, cols, c_out)
                + pad_a[:, EDGE - r:EDGE - r + cols, :]
                + pad_b[:, r:r + cols, :]
            )

        def relu_to(k, value):
            at = plan.direct.index(k)
            catb[:, at * c_out:(at + 1) * c_out] = (
                jnp.maximum(value, 0.0).astype(BF16).reshape(pix, c_out)
            )

        def shifted_copy(at):
            return pltpu.make_async_copy(
                sb.at[at], s_out.at[at, field, pl.ds(block * rows, rows)], sem_s.at[at]
            )

        weights(1 if 1 in plan.shifted else 4, 3, 1).start()
        weights(0, 1, 0).wait()
        relu_to(0, nn(xbuf[...].reshape(pix, c_in), wbuf[0, 0]))
        slot = 1
        for k in (1, 2, 3):
            base = 1 + 9 * (k - 1)
            if k in plan.shifted:
                at = 3 * plan.shifted.index(k)

                def one(a, _, k=k, at=at, base=base, slot=slot):
                    now = lax.rem(a + slot, 2)

                    @pl.when(a < 2)
                    def _():
                        weights(base + 3 * (a + 1), 3, 1 - now).start()

                    if k < 3:
                        after = base + 9 + (0 if k + 1 in plan.shifted else 3)

                        @pl.when(a == 2)
                        def _():
                            weights(after, 3, 1 - now).start()

                    weights(base, 3, now).wait()

                    @pl.when(in_field((1 - a) * RATE * k))
                    def _():
                        sb[at + a] = taps(k, now)
                        shifted_copy(at + a).start()

                    return 0

                lax.fori_loop(0, 3, one, 0)
                slot = (slot + 3) % 2
            else:
                if k < 3:
                    after = base + 9 + (0 if k + 1 in plan.shifted else 3)
                    weights(after, 3, 1 - slot).start()
                weights(base, 3, slot).wait()
                relu_to(k, taps(k, slot))
                slot = 1 - slot

        cat_copy = pltpu.make_async_copy(catb, cat_out.at[field, block], sem_o.at[1])
        cat_copy.start()
        xt_copy.wait()
        cat_copy.wait()
        for at, k in enumerate(plan.shifted):
            for a in range(3):
                @pl.when(in_field((1 - a) * RATE * k))
                def _(at=at, a=a):
                    shifted_copy(3 * at + a).wait()


def run_blocks(plan, slots, w_in, state):
    arrays, meta = [], []
    for cands, (valid, source, block, field) in slots:
        meta.append(jnp.stack([
            jnp.asarray(v, jnp.int32) for v in (valid, source + len(arrays), block, field)
        ]))
        arrays.extend(cands)
    meta = jnp.stack(meta)
    n, rows, cols, pix = plan.n, plan.rows, plan.cols, plan.pix
    c_in, c_out, n_sh = plan.c_in, plan.c_out, plan.n_sh
    shapes = [
        jax.ShapeDtypeStruct((2, n, c_in, pix), BF16),
        jax.ShapeDtypeStruct((2, n, pix, len(plan.direct) * c_out), BF16),
        jax.ShapeDtypeStruct((3 * n_sh, 2, n * rows, cols, c_out), F32),
    ]
    aliased = state is not None
    operands = [*arrays, w_in] + (list(state) if aliased else [])
    aliases = {1 + len(arrays) + 1 + i: i for i in range(3)} if aliased else {}
    flops = len(slots) * 2 * pix * c_in * c_out * (10 + 6 * n_sh)
    return pl.pallas_call(
        functools.partial(block_kernel, plan, len(arrays), aliased),
        grid_spec=pltpu.PrefetchScalarGridSpec(
            num_scalar_prefetch=1,
            grid=(len(slots),),
            in_specs=[pl.BlockSpec(memory_space=pl.ANY)] * len(operands),
            out_specs=[pl.BlockSpec(memory_space=pl.ANY)] * 3,
            scratch_shapes=[
                pltpu.VMEM((rows, cols, c_in), BF16),
                pltpu.VMEM((2, 3, c_in, c_out), BF16),
                pltpu.VMEM((c_in, pix), BF16),
                pltpu.VMEM((pix, len(plan.direct) * c_out), BF16),
                pltpu.VMEM((3 * n_sh, rows, cols, c_out), F32),
                pltpu.VMEM((rows, EDGE + cols, c_out), F32),
                pltpu.VMEM((rows, cols + EDGE, c_out), F32),
                pltpu.SemaphoreType.DMA,
                pltpu.SemaphoreType.DMA((2,)),
                pltpu.SemaphoreType.DMA((2,)),
                pltpu.SemaphoreType.DMA((3 * n_sh,)),
            ],
        ),
        out_shape=shapes,
        input_output_aliases=aliases,
        compiler_params=pltpu.CompilerParams(
            dimension_semantics=("arbitrary",), vmem_limit_bytes=VMEM_LIMIT
        ),
        cost_estimate=pl.CostEstimate(
            flops=flops, bytes_accessed=len(slots) * 14_000_000, transcendentals=0
        ),
        name="block_forward",
    )(meta, *operands)


def field_kernel(plan, last, tab, *refs):
    n, rows, cols, pix = plan.n, plan.rows, plan.cols, plan.pix
    c_in, c_out, n_sh = plan.c_in, plan.c_out, plan.n_sh
    units = plan.units
    n_rows_in = 2 * n_sh * rows
    cat_ref = refs[0]
    mid_refs = refs[1:1 + n_sh]
    s_refs = refs[1 + n_sh:1 + n_sh + n_rows_in]
    refs = refs[1 + n_sh + n_rows_in:]
    lab_ref, mean_ref, meanb_ref, w28_ref, wproj_ref, wcls_ref, cw_ref, xt_ref = refs[:8]
    refs = refs[8:]
    if last:
        prev_g, prev_p, prev_c = refs[:3]
        refs = refs[3:]
    g_out, p_out, c_out_ref = refs[:3]
    dbuf, pad, gpt, gp, gc, sdy, spool, pact, cat5, acc = refs[3:]
    step = pl.program_id(0)
    edge_rows = rows - 1
    flags = 7 * units

    def finish(value, prev):
        grad = value.astype(BF16)
        if not last:
            return grad
        return (prev.astype(F32) + grad.astype(F32)) * 0.5

    @pl.when(step == 0)
    def _():
        zero = jnp.zeros((edge_rows, cols, c_out), BF16)
        for slot in range(plan.n_slots):
            dbuf[slot, :edge_rows] = zero
            dbuf[slot, edge_rows + plan.height:] = zero
        pad[:, :EDGE, :] = jnp.zeros((rows, EDGE, c_out), F32)
        pad[:, EDGE + cols:, :] = jnp.zeros((rows, EDGE, c_out), F32)
        gpt[...] = jnp.zeros_like(gpt)
        gc[...] = jnp.zeros_like(gc)
        sdy[...] = jnp.zeros_like(sdy)
        pool_pre = nn(mean_ref[...], w28_ref[0])
        pact[...] = jnp.maximum(pool_pre, 0.0)

    @pl.when(step < n)
    def _():
        block = step
        for k in range(4):
            part = slice(k * c_out, (k + 1) * c_out)
            if k in plan.shifted:
                at = plan.shifted.index(k)
                r = RATE * k
                pre = mid_refs[at]
                for i in range(rows):
                    h = block * rows + i
                    line = pre[i]
                    for side, src in ((0, h - r), (1, h + r)):
                        ok = jnp.logical_and(src >= 0, src < plan.height)
                        ref = s_refs[(2 * at + side) * rows + i]
                        line = line + jnp.where(ok, ref[...], 0.0)
                    cat5[i * cols:(i + 1) * cols, part] = jnp.maximum(line, 0.0).astype(BF16)
            else:
                at = plan.direct.index(k)
                cat5[:, part] = cat_ref[:, at * c_out:(at + 1) * c_out]
        cat5[:, 4 * c_out:] = jnp.broadcast_to(pact[0:1, :].astype(BF16), (pix, c_out))
        cat = cat5[...]
        y_pre = nn(cat, wproj_ref[...])
        y_act = jnp.maximum(y_pre, 0.0).astype(BF16)
        logits = nn(y_act, wcls_ref[...])
        lane = lax.broadcasted_iota(jnp.int32, (pix, 128), 1)
        live = lane < plan.classes
        expo = jnp.where(live, jnp.exp(logits), 0.0)
        prob = expo / jnp.sum(expo, axis=1, keepdims=True)
        label = lab_ref[...]
        onehot = jnp.where(label == lane.astype(F32), 1.0, 0.0)
        weight = jnp.zeros((pix, 128), F32)
        for c in range(plan.classes):
            weight = jnp.where(label == float(c), cw_ref[c], weight)
        d_logits = jnp.where(
            live, (prob - onehot) * weight * (LOSS_SCALE / plan.total), 0.0
        ).astype(BF16)
        d_y = jnp.where(y_pre > 0, nt(d_logits, wcls_ref[...]), 0.0).astype(BF16)
        sdy[0:1, :] += jnp.sum(d_y.astype(F32), axis=0, keepdims=True)
        eye = identity(c_out)
        gpt[...] += nn(nt(eye, d_y).astype(BF16), cat)
        gc[...] += nn(nt(eye, y_act).astype(BF16), d_logits)
        for k in range(4):
            want = [tab[flags + 3 * k + b] for b in range(3)]
            part = slice(k * c_out, (k + 1) * c_out)

            @pl.when((want[0] >= 0) | (want[1] >= 0) | (want[2] >= 0))
            def _(k=k, want=want, part=part):
                d_cat = nt(d_y, wproj_ref[part, :])
                d_k = jnp.where(cat5[:, part] > 0, d_cat, 0.0).astype(BF16)
                if k > 0:
                    pad[:, EDGE:EDGE + cols, :] = d_k.astype(F32).reshape(rows, cols, c_out)
                at = pl.ds(block * rows + edge_rows, rows)
                for b in range(3):
                    if k == 0 and b != 1:
                        continue

                    @pl.when(want[b] >= 0)
                    def _(b=b):
                        slot = jnp.maximum(want[b], 0)
                        if b == 1:
                            dbuf[slot, at] = d_k.reshape(rows, cols, c_out)
                        else:
                            first = EDGE + (1 - b) * RATE * k
                            dbuf[slot, at] = pad[:, first:first + cols, :].astype(BF16)

    @pl.when(step == n - 1)
    def _():
        pool = wproj_ref[4 * c_out:, :]
        rest = sdy[...]
        total = jnp.zeros(sdy.shape, F32)
        for _i in range(3):
            head = rest.astype(BF16)
            total = total + nt(head, pool)
            rest = rest - head.astype(F32)
        pool_pre = nn(mean_ref[...], w28_ref[0])
        spool[...] = jnp.where(pool_pre > 0, total[0:1, :], 0.0)
        for c in range(5):
            gp[c * c_out:(c + 1) * c_out, :] = gpt[:, c * c_out:(c + 1) * c_out].T
        index = tab[flags + 12]
        first = pl.multiple_of(index * plan.proj_rows, plan.proj_rows)
        mine = gp[pl.ds(first, plan.proj_rows), :]
        p_out[...] = finish(mine, prev_p[...] if last else None)
        first = pl.multiple_of(index * plan.cls_rows, plan.cls_rows)
        mine = gc[pl.ds(first, plan.cls_rows), :]
        c_out_ref[...] = finish(mine, prev_c[...] if last else None)

    @pl.when(step >= n)
    def _():
        unit = step - n
        slot, move = tab[2 * units + unit], tab[3 * units + unit]
        low, high = tab[4 * units + unit], tab[5 * units + unit]
        acc[...] = jnp.zeros_like(acc)
        for j in range(n):
            @pl.when(jnp.logical_and(low <= j, j < high))
            def _(j=j):
                first = j * rows - move + edge_rows
                right = dbuf[slot, pl.ds(first, rows)].reshape(pix, c_out)
                acc[...] += nn(xt_ref[j], right)

        @pl.when(tab[6 * units + unit] == 1)
        def _():
            mean = meanb_ref[...]
            for c in range(c_out // 128):
                part = slice(c * 128, (c + 1) * 128)
                acc[:, part] = mean * spool[0:1, part]

        g_out[...] = finish(acc[...], prev_g[...] if last else None)


def run_field(plan, field, tab, state, labels, mean, meanb, w_in, w_proj, wcls, cw, prev):
    n, rows, cols, pix = plan.n, plan.rows, plan.cols, plan.pix
    c_in, c_out, n_sh = plan.c_in, plan.c_out, plan.n_sh
    units, unit_rows = plan.units, plan.unit_rows
    xt, cat, s = state
    last = prev is not None

    def blk(i):
        return jnp.minimum(i, n - 1)

    def unit(i):
        return jnp.maximum(i - n, 0)

    in_specs = [
        pl.BlockSpec(
            (None, None, pix, len(plan.direct) * c_out), lambda i, t: (field, blk(i), 0, 0)
        ),
    ]
    operands = [cat]
    for at in range(n_sh):
        in_specs.append(pl.BlockSpec(
            (None, None, rows, cols, c_out),
            lambda i, t, at=at: (3 * at + 1, field, blk(i), 0, 0),
        ))
        operands.append(s)
    for at, k in enumerate(plan.shifted):
        for side in range(2):
            move = (2 * side - 1) * RATE * k
            for row in range(rows):
                def index(i, t, at=at, side=side, move=move, row=row):
                    h = jnp.clip(blk(i) * rows + row + move, 0, plan.height - 1)
                    return (3 * at + 2 * side, field, h, 0, 0)
                in_specs.append(pl.BlockSpec((None, None, None, cols, c_out), index))
                operands.append(s)
    in_specs += [
        pl.BlockSpec((None, pix, 128), lambda i, t: (blk(i), 0, 0)),
        pl.BlockSpec((16, c_in), lambda i, t: (0, 0)),
        pl.BlockSpec((unit_rows, 128), lambda i, t: (t[units + unit(i)], 0)),
        pl.BlockSpec((1, c_in, c_out), lambda i, t: (28, 0, 0)),
        pl.BlockSpec((5 * c_out, c_out), lambda i, t: (0, 0)),
        pl.BlockSpec((c_out, 128), lambda i, t: (0, 0)),
        pl.BlockSpec(memory_space=pltpu.SMEM),
        pl.BlockSpec((None, n, unit_rows, pix), lambda i, t: (field, 0, t[units + unit(i)], 0)),
    ]
    operands += [labels, mean, meanb, w_in, w_proj, wcls, cw, xt]
    out_specs = [
        pl.BlockSpec((unit_rows, c_out), lambda i, t: (t[unit(i)], 0)),
        pl.BlockSpec((plan.proj_rows, c_out), lambda i, t: (0, 0)),
        pl.BlockSpec((plan.cls_rows, 128), lambda i, t: (0, 0)),
    ]
    if last:
        in_specs += out_specs
        operands += list(prev)
    kind = F32 if last else BF16
    return pl.pallas_call(
        functools.partial(field_kernel, plan, last),
        grid_spec=pltpu.PrefetchScalarGridSpec(
            num_scalar_prefetch=1,
            grid=(n + units,),
            in_specs=in_specs,
            out_specs=out_specs,
            scratch_shapes=[
                pltpu.VMEM((plan.n_slots, plan.height + 2 * (rows - 1), cols, c_out), BF16),
                pltpu.VMEM((rows, cols + 2 * EDGE, c_out), F32),
                pltpu.VMEM((c_out, 5 * c_out), F32),
                pltpu.VMEM((5 * c_out, c_out), F32),
                pltpu.VMEM((c_out, 128), F32),
                pltpu.VMEM((16, c_out), F32),
                pltpu.VMEM((16, c_out), F32),
                pltpu.VMEM((16, c_out), F32),
                pltpu.VMEM((pix, 5 * c_out), BF16),
                pltpu.VMEM((unit_rows, c_out), F32),
            ],
        ),
        out_shape=[
            jax.ShapeDtypeStruct((units * unit_rows, c_out), kind),
            jax.ShapeDtypeStruct((plan.proj_rows, c_out), kind),
            jax.ShapeDtypeStruct((plan.cls_rows, 128), kind),
        ],
        compiler_params=pltpu.CompilerParams(
            dimension_semantics=("arbitrary",), vmem_limit_bytes=VMEM_LIMIT
        ),
        cost_estimate=pl.CostEstimate(
            flops=10_000_000_000, bytes_accessed=25_000_000, transcendentals=0
        ),
        name="field_grads",
    )(tab, *operands)


def per_device(plan, features, labels, w_in, w_proj, w_cls, class_weight, matching):
    n, reps, rows, pix = plan.n, plan.reps, plan.rows, plan.pix
    c_in = plan.c_in
    x = features[0]
    here = lax.axis_index("space")
    tab = jnp.asarray(plan.tables)[here]
    wcls = jnp.pad(w_cls, ((0, 0), (0, 128 - plan.classes)))
    sums = jnp.sum(x, axis=(0, 1), dtype=F32)
    aux = jnp.concatenate([sums, labels[0].reshape(pix).astype(F32)])

    def along(value, way, step):
        pairs = [
            (i, i + way) for i in range(n)
            if 0 <= i + way < n and 0 <= i - way * (step - 1) < n
        ]
        return lax.ppermute(value, "space", pairs)

    def branch(bits, x, aux, tab, wcls, w_in, w_proj, class_weight):
        def partner(value, valid):
            pairs = [
                (s * reps + r, s * reps + (r ^ bits))
                for s in range(n) if valid(s) for r in range(reps)
            ]
            return lax.ppermute(value, ("space", "rep"), pairs)

        both = jnp.stack([aux, partner(aux, lambda s: True)])
        up = down = x
        stages = [[([x], (1, 0, here, 0))]]
        pair_slots = [([partner(x, lambda s: True)], (1, 0, here, 1))]
        for t in range(1, n):
            up, down = along(up, 1, t), along(down, -1, t)
            has_up = (here >= t).astype(jnp.int32)
            has_down = (here + t < n).astype(jnp.int32)
            part_up = partner(up, lambda s: s >= t)
            part_down = partner(down, lambda s: s + t < n)

            def slots(first, second, field):
                if 2 * t < n:
                    return [
                        ([first], (has_up, 0, here - t, field)),
                        ([second], (has_down, 0, here + t, field)),
                    ]
                block = jnp.where(has_up == 1, here - t, here + t)
                return [([first, second], (has_up | has_down, 1 - has_up, block, field))]

            stages.append(slots(up, down, 0) + pair_slots)
            pair_slots = slots(part_up, part_down, 1)
        every = lax.all_gather(both, "space", axis=0)
        means = (jnp.sum(every[:, :, :c_in], axis=0) / plan.total).astype(BF16)
        label_cols = jnp.broadcast_to(every[:, :, c_in:, None], (n, 2, pix, 128))
        mean_rows = jnp.broadcast_to(means[:, None, :], (2, 16, c_in))
        mean_cols = jnp.broadcast_to(means.astype(F32)[:, :, None], (2, c_in, 128))
        state = None
        for stage in stages:
            state = run_blocks(plan, stage, w_in, state)
        field = functools.partial(
            run_field, w_in=w_in, w_proj=w_proj, wcls=wcls, cw=class_weight
        )
        grads = field(
            plan, 0, tab, state, label_cols[:, 0], mean_rows[0], mean_cols[0], prev=None
        )
        state, grads = lax.optimization_barrier((state, grads))
        state = run_blocks(plan, pair_slots, w_in, state)
        out = field(
            plan, 1, tab, state, label_cols[:, 1], mean_rows[1], mean_cols[1], prev=grads
        )
        return tuple(out)

    branches = [functools.partial(branch, bits) for bits in range(1, reps)]
    avg_in, avg_proj, avg_cls = lax.switch(
        matching[0] - 1, branches, x, aux, tab, wcls, w_in, w_proj, class_weight
    )
    return avg_in[None], avg_proj[None], avg_cls[None, :, :plan.classes]


def solution(mesh):
    n, reps = mesh.shape["space"], mesh.shape["rep"]

    def build(features, labels, w_in, w_proj, w_cls, class_weight, matching):
        _, rows, cols, c_in = features.shape
        plan = Plan(n, reps, rows // n, cols, c_in, w_proj.shape[1], w_cls.shape[1])
        return jax.shard_map(
            functools.partial(per_device, plan),
            mesh=mesh,
            in_specs=(P("rep", "space", None, None), P("rep", "space", None), P(), P(), P(), P(), P()),
            out_specs=(P("rep", "space", None), P("rep", "space", None), P("rep", "space", None)),
            check_vma=False,
        )(features, labels, w_in, w_proj, w_cls, class_weight, matching)

    return build
```

```python
import functools

import jax
import jax.numpy as jnp
import numpy as np
from jax import lax
from jax.experimental import pallas as pl
from jax.experimental.pallas import tpu as pltpu
from jax.sharding import PartitionSpec as P

LOSS_SCALE = 1024.0
RATE = 12
EDGE = 40
BF16 = jnp.bfloat16
F32 = jnp.float32
VMEM_LIMIT = 60 * 1024 * 1024


def nn(a, b):
    return lax.dot_general(a, b, (((1,), (0,)), ((), ())), preferred_element_type=F32)


def nt(a, b):
    return lax.dot_general(a, b, (((1,), (1,)), ((), ())), preferred_element_type=F32)


def identity(size):
    rows = lax.broadcasted_iota(jnp.int32, (size, size), 0)
    cols = lax.broadcasted_iota(jnp.int32, (size, size), 1)
    return (rows == cols).astype(F32).astype(BF16)


class Plan:
    def __init__(self, n, reps, rows, cols, c_in, c_out, classes):
        self.n, self.reps, self.rows, self.cols = n, reps, rows, cols
        self.c_in, self.c_out, self.classes = c_in, c_out, classes
        self.height = rows * n
        self.pix = rows * cols
        self.total = self.pix * n
        self.shifted = [k for k in (1, 2, 3) if RATE * k < self.height]
        self.direct = [k for k in range(4) if k not in self.shifted]
        self.n_sh = len(self.shifted)
        row = lambda k, a: [1 + 9 * (k - 1) + 3 * a + b for b in range(3)]
        still = [row(k, 1) for k in self.direct[1:]]
        self.loads = [[0] + (still[0] if still else [])] + still[1:]
        for k in self.shifted:
            self.loads += [row(k, a) for a in range(3)]
        self.units = 29
        self.unit_rows = c_in // n
        self.proj_rows = 5 * c_out // n
        self.cls_rows = c_out // n
        tables = [self.table(s) for s in range(n)]
        self.n_slots = max(t[1] for t in tables)
        self.tables = np.array([t[0] for t in tables], np.int32)

    def tap(self, t):
        if t == 0:
            return (0, 1, 1)
        if t == 28:
            return None
        k, rest = (t - 1) // 9 + 1, (t - 1) % 9
        a, b = rest // 3, rest % 3
        if a != 1 and k not in self.shifted:
            return "zero"
        return (k, a, b)

    def table(self, s):
        units = []
        for local in range(self.units):
            unit = s * self.units + local
            units.append((unit % self.n, unit // self.n, local))
        units.sort()
        slots = {}
        order, chan, slot, shift, low, high, kind = [], [], [], [], [], [], []
        for c, t, local in units:
            tap = self.tap(t)
            order.append(local)
            chan.append(c)
            if tap is None or tap == "zero":
                slot.append(0)
                shift.append(0)
                low.append(0)
                high.append(0)
                kind.append(1 if tap is None else 0)
                continue
            k, a, b = tap
            slot.append(slots.setdefault((k, b), len(slots)))
            move = (a - 1) * RATE * k
            shift.append(move)
            valid = [
                j for j in range(self.n)
                if any(0 <= self.rows * j + i - move < self.height for i in range(self.rows))
            ]
            low.append(valid[0])
            high.append(valid[-1] + 1)
            kind.append(0)
        flags = [slots.get((k, b), -1) for k in range(4) for b in range(3)]
        return order + chan + slot + shift + low + high + kind + flags + [s], len(slots)


def block_kernel(plan, n_cand, aliased, meta, *refs):
    rows, cols, c_in, c_out = plan.rows, plan.cols, plan.c_in, plan.c_out
    pix = plan.pix
    cands = refs[:n_cand]
    w_hbm = refs[n_cand]
    refs = refs[n_cand + 1 + (3 if aliased else 0):]
    xt_out, cat_out, s_out = refs[:3]
    xbuf, wbuf, xtb, catb, sb, res, sem_x, sem_w, sem_o, sem_s = refs[3:]
    step = pl.program_id(0)
    source, block, field = meta[step, 0], meta[step, 1], meta[step, 2]

    for c in range(n_cand):
        @pl.when(source == c)
        def _(c=c):
            pltpu.make_async_copy(cands[c], xbuf, sem_x).start()

    def weights(group, taps):
        return [
            pltpu.make_async_copy(
                w_hbm.at[tap], wbuf.at[group, :, pl.ds(i * c_out, c_out)], sem_w.at[group]
            )
            for i, tap in enumerate(taps)
        ]

    @pl.when(step == 0)
    def _():
        for group, taps in enumerate(plan.loads):
            for copy in weights(group, taps):
                copy.start()
        res[:, :EDGE, :] = jnp.zeros((rows, EDGE, res.shape[2]), F32)
        res[:, EDGE + cols:, :] = jnp.zeros((rows, EDGE, res.shape[2]), F32)

    pltpu.make_async_copy(cands[0], xbuf, sem_x).wait()
    eye = identity(256)
    for c in range(c_in // 256):
        part = slice(c * 256, (c + 1) * 256)
        xtb[part, :] = nt(eye, xbuf[:, part]).astype(BF16)
    xt_copy = pltpu.make_async_copy(xtb, xt_out.at[field, block], sem_o.at[0])
    xt_copy.start()

    def in_field(move):
        first = block * rows + move
        return jnp.logical_and(first + rows - 1 >= 0, first < plan.height)

    def loaded(group, taps):
        @pl.when(step == 0)
        def _():
            for copy in weights(group, taps):
                copy.wait()

    def columns(k, first):
        r = RATE * k
        part = [slice(first + i * c_out, first + (i + 1) * c_out) for i in range(3)]
        return (
            res[:, EDGE - r:EDGE - r + cols, part[0]]
            + res[:, EDGE:EDGE + cols, part[1]]
            + res[:, EDGE + r:EDGE + r + cols, part[2]]
        )

    def relu_to(k, value):
        at = plan.direct.index(k)
        catb[:, at * c_out:(at + 1) * c_out] = (
            jnp.maximum(value, 0.0).astype(BF16).reshape(pix, c_out)
        )

    def shifted_copy(at):
        return pltpu.make_async_copy(
            sb.at[at], s_out.at[at, field, pl.ds(block * rows, rows)], sem_s.at[at]
        )

    group = 0
    first = c_out
    loaded(0, plan.loads[0])
    width = len(plan.loads[0]) * c_out
    res[:, EDGE:EDGE + cols, :width] = nn(xbuf[...], wbuf[0, :, :width]).reshape(
        rows, cols, width
    )
    relu_to(0, res[:, EDGE:EDGE + cols, :c_out])
    group = 1
    for k in plan.direct[1:]:
        if first + 3 * c_out > width:
            loaded(group, plan.loads[group])
            width, first = 3 * c_out, 0
            res[:, EDGE:EDGE + cols, :width] = nn(xbuf[...], wbuf[group, :, :width]).reshape(
                rows, cols, width
            )
            group += 1
        relu_to(k, columns(k, first))
        first += 3 * c_out
    cat_copy = pltpu.make_async_copy(catb, cat_out.at[field, block], sem_o.at[1])
    cat_copy.start()
    width = 3 * c_out
    for at, k in enumerate(plan.shifted):
        for a in range(3):
            loaded(group + 3 * at + a, plan.loads[group + 3 * at + a])

        def one(a, _, k=k, at=at, base=group + 3 * at):
            @pl.when(in_field((1 - a) * RATE * k))
            def _():
                res[:, EDGE:EDGE + cols, :width] = nn(
                    xbuf[...], wbuf[base + a, :, :width]
                ).reshape(rows, cols, width)
                sb[3 * at + a] = columns(k, 0)
                shifted_copy(3 * at + a).start()
            return 0

        lax.fori_loop(0, 3, one, 0)
    xt_copy.wait()
    cat_copy.wait()
    for at, k in enumerate(plan.shifted):
        for a in range(3):
            @pl.when(in_field((1 - a) * RATE * k))
            def _(at=at, a=a):
                shifted_copy(3 * at + a).wait()


def run_blocks(plan, slots, w_in, state):
    arrays, meta = [], []
    for cands, (source, block, field) in slots:
        meta.append(jnp.stack([
            jnp.asarray(v, jnp.int32) for v in (source + len(arrays), block, field)
        ]))
        arrays.extend(cands)
    meta = jnp.stack(meta)
    n, rows, cols, pix = plan.n, plan.rows, plan.cols, plan.pix
    c_in, c_out, n_sh = plan.c_in, plan.c_out, plan.n_sh
    shapes = [
        jax.ShapeDtypeStruct((2, n, c_in, pix), BF16),
        jax.ShapeDtypeStruct((2, n, pix, len(plan.direct) * c_out), BF16),
        jax.ShapeDtypeStruct((3 * n_sh, 2, n * rows, cols, c_out), F32),
    ]
    aliased = state is not None
    operands = [*arrays, w_in] + (list(state) if aliased else [])
    aliases = {1 + len(arrays) + 1 + i: i for i in range(3)} if aliased else {}
    widest = max(len(g) for g in plan.loads) * c_out
    return pl.pallas_call(
        functools.partial(block_kernel, plan, len(arrays), aliased),
        grid_spec=pltpu.PrefetchScalarGridSpec(
            num_scalar_prefetch=1,
            grid=(len(slots),),
            in_specs=[pl.BlockSpec(memory_space=pl.ANY)] * len(operands),
            out_specs=[pl.BlockSpec(memory_space=pl.ANY)] * 3,
            scratch_shapes=[
                pltpu.VMEM((pix, c_in), BF16),
                pltpu.VMEM((len(plan.loads), c_in, widest), BF16),
                pltpu.VMEM((c_in, pix), BF16),
                pltpu.VMEM((pix, len(plan.direct) * c_out), BF16),
                pltpu.VMEM((3 * n_sh, rows, cols, c_out), F32),
                pltpu.VMEM((rows, cols + 2 * EDGE, widest), F32),
                pltpu.SemaphoreType.DMA,
                pltpu.SemaphoreType.DMA((len(plan.loads),)),
                pltpu.SemaphoreType.DMA((2,)),
                pltpu.SemaphoreType.DMA((3 * n_sh,)),
            ],
        ),
        out_shape=shapes,
        input_output_aliases=aliases,
        compiler_params=pltpu.CompilerParams(
            dimension_semantics=("arbitrary",), vmem_limit_bytes=VMEM_LIMIT
        ),
        cost_estimate=pl.CostEstimate(
            flops=len(slots) * 2 * pix * c_in * c_out * (10 + 6 * n_sh),
            bytes_accessed=10_000_000 + len(slots) * 5_000_000,
            transcendentals=0,
        ),
        name="block_forward",
    )(meta, *operands)


def chain_kernel(plan, tab, *refs):
    n, rows, cols, pix = plan.n, plan.rows, plan.cols, plan.pix
    c_out, n_sh = plan.c_out, plan.n_sh
    n_rows_in = 2 * n_sh * rows
    cat_ref = refs[0]
    mid_refs = refs[1:1 + n_sh]
    s_refs = refs[1 + n_sh:1 + n_sh + n_rows_in]
    refs = refs[1 + n_sh + n_rows_in:]
    lab_ref, mean_ref, w28_ref, wproj_ref, wcls_ref, cw_ref = refs[:6]
    d_out, p_out, c_ref_out, spool = refs[6:10]
    gpt, gp, gc, sdy, pact, cat5 = refs[10:]
    step = pl.program_id(0)
    flags = 7 * plan.units

    @pl.when(step == 0)
    def _():
        gpt[...] = jnp.zeros_like(gpt)
        gc[...] = jnp.zeros_like(gc)
        sdy[...] = jnp.zeros_like(sdy)
        pact[...] = nn(mean_ref[...], w28_ref[0])

    block = step
    for k in range(4):
        part = slice(k * c_out, (k + 1) * c_out)
        if k in plan.shifted:
            at = plan.shifted.index(k)
            r = RATE * k
            pre = mid_refs[at]
            for i in range(rows):
                h = block * rows + i
                line = pre[i]
                for side, src in ((0, h - r), (1, h + r)):
                    ok = jnp.logical_and(src >= 0, src < plan.height)
                    ref = s_refs[(2 * at + side) * rows + i]
                    line = line + jnp.where(ok, ref[...], 0.0)
                cat5[i * cols:(i + 1) * cols, part] = jnp.maximum(line, 0.0).astype(BF16)
        else:
            at = plan.direct.index(k)
            cat5[:, part] = cat_ref[:, at * c_out:(at + 1) * c_out]
    pool_act = jnp.maximum(pact[0:1, :], 0.0).astype(BF16)
    cat5[:, 4 * c_out:] = jnp.broadcast_to(pool_act, (pix, c_out))
    y_pre = nn(cat5[...], wproj_ref[...])
    y_act = jnp.maximum(y_pre, 0.0).astype(BF16)
    logits = nn(y_act, wcls_ref[...])
    lane = lax.broadcasted_iota(jnp.int32, (pix, 128), 1)
    live = lane < plan.classes
    expo = jnp.where(live, jnp.exp(logits), 0.0)
    prob = expo / jnp.sum(expo, axis=1, keepdims=True)
    label = lab_ref[...]
    onehot = jnp.where(label == lane.astype(F32), 1.0, 0.0)
    weight = jnp.zeros((pix, 128), F32)
    for c in range(plan.classes):
        weight = jnp.where(label == float(c), cw_ref[c], weight)
    d_logits = jnp.where(
        live, (prob - onehot) * weight * (LOSS_SCALE / plan.total), 0.0
    ).astype(BF16)
    d_y = jnp.where(y_pre > 0, nt(d_logits, wcls_ref[...]), 0.0).astype(BF16)
    sdy[0:1, :] += jnp.sum(d_y.astype(F32), axis=0, keepdims=True)
    eye = identity(c_out)
    gpt[...] += nn(nt(eye, d_y).astype(BF16), cat5[...])
    gc[...] += nn(nt(eye, y_act).astype(BF16), d_logits)
    for k in range(4):
        want = [tab[flags + 3 * k + b] for b in range(3)]
        part = slice(k * c_out, (k + 1) * c_out)

        @pl.when((want[0] >= 0) | (want[1] >= 0) | (want[2] >= 0))
        def _(part=part):
            d_cat = nt(d_y, wproj_ref[part, :])
            d_out[:, part] = jnp.where(cat5[:, part] > 0, d_cat, 0.0).astype(BF16)

    @pl.when(step == n - 1)
    def _():
        pool = wproj_ref[4 * c_out:, :]
        rest = sdy[...]
        total = jnp.zeros(sdy.shape, F32)
        for _i in range(3):
            head = rest.astype(BF16)
            total = total + nt(head, pool)
            rest = rest - head.astype(F32)
        spool[...] = jnp.where(pact[0:1, :] > 0, total[0:8, :], 0.0)
        for c in range(5):
            gp[c * c_out:(c + 1) * c_out, :] = gpt[:, c * c_out:(c + 1) * c_out].T
        index = tab[flags + 12]
        first = pl.multiple_of(index * plan.proj_rows, plan.proj_rows)
        p_out[...] = gp[pl.ds(first, plan.proj_rows), :]
        first = pl.multiple_of(index * plan.cls_rows, plan.cls_rows)
        c_ref_out[...] = gc[pl.ds(first, plan.cls_rows), :]


def run_chain(plan, field, tab, state, labels, mean, w_in, w_proj, wcls, cw):
    n, rows, cols, pix = plan.n, plan.rows, plan.cols, plan.pix
    c_in, c_out, n_sh = plan.c_in, plan.c_out, plan.n_sh
    _, cat, s = state
    in_specs = [
        pl.BlockSpec((None, None, pix, len(plan.direct) * c_out), lambda i, t: (field, i, 0, 0)),
    ]
    operands = [cat]
    for at in range(n_sh):
        in_specs.append(pl.BlockSpec(
            (None, None, rows, cols, c_out), lambda i, t, at=at: (3 * at + 1, field, i, 0, 0),
        ))
        operands.append(s)
    for at, k in enumerate(plan.shifted):
        for side in range(2):
            move = (2 * side - 1) * RATE * k
            for row in range(rows):
                def index(i, t, at=at, side=side, move=move, row=row):
                    h = jnp.clip(i * rows + row + move, 0, plan.height - 1)
                    return (3 * at + 2 * side, field, h, 0, 0)
                in_specs.append(pl.BlockSpec((None, None, None, cols, c_out), index))
                operands.append(s)
    in_specs += [
        pl.BlockSpec((None, pix, 128), lambda i, t: (i, 0, 0)),
        pl.BlockSpec((16, c_in), lambda i, t: (0, 0)),
        pl.BlockSpec((1, c_in, c_out), lambda i, t: (28, 0, 0)),
        pl.BlockSpec((5 * c_out, c_out), lambda i, t: (0, 0)),
        pl.BlockSpec((c_out, 128), lambda i, t: (0, 0)),
        pl.BlockSpec(memory_space=pltpu.SMEM),
    ]
    operands += [labels, mean, w_in, w_proj, wcls, cw]
    return pl.pallas_call(
        functools.partial(chain_kernel, plan),
        grid_spec=pltpu.PrefetchScalarGridSpec(
            num_scalar_prefetch=1,
            grid=(n,),
            in_specs=in_specs,
            out_specs=[
                pl.BlockSpec((None, pix, 4 * c_out), lambda i, t: (i, 0, 0)),
                pl.BlockSpec((plan.proj_rows, c_out), lambda i, t: (0, 0)),
                pl.BlockSpec((plan.cls_rows, 128), lambda i, t: (0, 0)),
                pl.BlockSpec((8, c_out), lambda i, t: (0, 0)),
            ],
            scratch_shapes=[
                pltpu.VMEM((c_out, 5 * c_out), F32),
                pltpu.VMEM((5 * c_out, c_out), F32),
                pltpu.VMEM((c_out, 128), F32),
                pltpu.VMEM((16, c_out), F32),
                pltpu.VMEM((16, c_out), F32),
                pltpu.VMEM((pix, 5 * c_out), BF16),
            ],
        ),
        out_shape=[
            jax.ShapeDtypeStruct((n, pix, 4 * c_out), BF16),
            jax.ShapeDtypeStruct((plan.proj_rows, c_out), F32),
            jax.ShapeDtypeStruct((plan.cls_rows, 128), F32),
            jax.ShapeDtypeStruct((8, c_out), F32),
        ],
        compiler_params=pltpu.CompilerParams(
            dimension_semantics=("arbitrary",), vmem_limit_bytes=VMEM_LIMIT
        ),
        cost_estimate=pl.CostEstimate(
            flops=5_000_000_000, bytes_accessed=15_000_000, transcendentals=0
        ),
        name="loss_chain",
    )(tab, *operands)


def grads_kernel(plan, last, tab, *refs):
    n, rows, cols, pix = plan.n, plan.rows, plan.cols, plan.pix
    c_out, units = plan.c_out, plan.units
    d_ref, spool, meanb_ref, xt_ref = refs[:4]
    prev_g = refs[4] if last else None
    g_out, dbuf, pad, acc = refs[4 + last:]
    step = pl.program_id(0)
    edge_rows = rows - 1
    flags = 7 * units

    @pl.when(step == 0)
    def _():
        zero = jnp.zeros((edge_rows, cols, c_out), BF16)
        for slot in range(plan.n_slots):
            dbuf[slot, :edge_rows] = zero
            dbuf[slot, edge_rows + plan.height:] = zero
        pad[:, :EDGE, :] = jnp.zeros((rows, EDGE, c_out), F32)
        pad[:, EDGE + cols:, :] = jnp.zeros((rows, EDGE, c_out), F32)

    @pl.when(step < n)
    def _():
        for k in range(4):
            want = [tab[flags + 3 * k + b] for b in range(3)]
            part = slice(k * c_out, (k + 1) * c_out)

            @pl.when((want[0] >= 0) | (want[1] >= 0) | (want[2] >= 0))
            def _(k=k, want=want, part=part):
                d_k = d_ref[:, part].reshape(rows, cols, c_out)
                if k > 0:
                    pad[:, EDGE:EDGE + cols, :] = d_k.astype(F32)
                at = pl.ds(step * rows + edge_rows, rows)
                for b in range(3):
                    if k == 0 and b != 1:
                        continue

                    @pl.when(want[b] >= 0)
                    def _(b=b):
                        slot = jnp.maximum(want[b], 0)
                        if b == 1:
                            dbuf[slot, at] = d_k
                        else:
                            first = EDGE + (1 - b) * RATE * k
                            dbuf[slot, at] = pad[:, first:first + cols, :].astype(BF16)

    @pl.when(step >= n)
    def _():
        unit = step - n
        slot, move = tab[2 * units + unit], tab[3 * units + unit]
        low, high = tab[4 * units + unit], tab[5 * units + unit]
        acc[...] = jnp.zeros_like(acc)
        for j in range(n):
            @pl.when(jnp.logical_and(low <= j, j < high))
            def _(j=j):
                first = j * rows - move + edge_rows
                right = dbuf[slot, pl.ds(first, rows)].reshape(pix, c_out)
                acc[...] += nn(xt_ref[j], right)

        @pl.when(tab[6 * units + unit] == 1)
        def _():
            mean = meanb_ref[...]
            for c in range(c_out // 128):
                part = slice(c * 128, (c + 1) * 128)
                acc[:, part] = mean * spool[0:1, part]

        grad = acc[...].astype(BF16)
        if last:
            grad = (prev_g[...].astype(F32) + grad.astype(F32)) * 0.5
        g_out[...] = grad


def run_grads(plan, field, tab, state, d, spool, meanb, prev):
    n, rows, cols, pix = plan.n, plan.rows, plan.cols, plan.pix
    c_out, units, unit_rows = plan.c_out, plan.units, plan.unit_rows
    last = prev is not None

    def unit(i):
        return jnp.maximum(i - n, 0)

    in_specs = [
        pl.BlockSpec((None, pix, 4 * c_out), lambda i, t: (jnp.minimum(i, n - 1), 0, 0)),
        pl.BlockSpec((8, c_out), lambda i, t: (0, 0)),
        pl.BlockSpec((unit_rows, 128), lambda i, t: (t[units + unit(i)], 0)),
        pl.BlockSpec((None, n, unit_rows, pix), lambda i, t: (field, 0, t[units + unit(i)], 0)),
    ]
    operands = [d, spool, meanb, state[0]]
    out_spec = pl.BlockSpec((unit_rows, c_out), lambda i, t: (t[unit(i)], 0))
    if last:
        in_specs.append(out_spec)
        operands.append(prev)
    return pl.pallas_call(
        functools.partial(grads_kernel, plan, last),
        grid_spec=pltpu.PrefetchScalarGridSpec(
            num_scalar_prefetch=1,
            grid=(n + units,),
            in_specs=in_specs,
            out_specs=out_spec,
            scratch_shapes=[
                pltpu.VMEM((plan.n_slots, plan.height + 2 * (rows - 1), cols, c_out), BF16),
                pltpu.VMEM((rows, cols + 2 * EDGE, c_out), F32),
                pltpu.VMEM((unit_rows, c_out), F32),
            ],
        ),
        out_shape=jax.ShapeDtypeStruct((units * unit_rows, c_out), F32 if last else BF16),
        compiler_params=pltpu.CompilerParams(
            dimension_semantics=("arbitrary",), vmem_limit_bytes=VMEM_LIMIT
        ),
        cost_estimate=pl.CostEstimate(
            flops=6_000_000_000, bytes_accessed=15_000_000, transcendentals=0
        ),
        name="tap_grads",
    )(tab, *operands)


def per_device(plan, features, labels, w_in, w_proj, w_cls, class_weight, matching):
    n, reps, rows, pix, c_in = plan.n, plan.reps, plan.rows, plan.pix, plan.c_in
    x = features[0].reshape(pix, c_in)
    here = lax.axis_index("space")
    bits = [
        jnp.bitwise_and(jnp.right_shift(matching[0], b), 1) == 1
        for b in range(reps.bit_length() - 1)
    ]

    def along(value, way, step):
        pairs = [
            (i, i + way) for i in range(n)
            if 0 <= i + way < n and 0 <= i - way * (step - 1) < n
        ]
        return lax.ppermute(value, "space", pairs)

    def partner(value):
        hops = []
        for b, on in enumerate(bits):
            moved = lax.ppermute(value, "rep", [(r, r ^ (1 << b)) for r in range(reps)])
            hops.insert(0, moved)
            if b + 1 < len(bits):
                value = jnp.where(on, moved, value)
        return hops

    top = jnp.int32(0)
    for b in range(len(bits)):
        top = jnp.where(bits[b], len(bits) - 1 - b, top)

    order = np.array(
        [sorted(range(n), key=lambda j: (abs(j - s), j)) for s in range(n)], np.int32
    )
    ups, downs, items = [x], [x], [x]
    for t in range(1, n):
        ups.append(along(ups[-1], 1, t))
        downs.append(along(downs[-1], -1, t))
    for q in range(1, n):
        value = None
        for s in range(n):
            j = int(order[s, q])
            arrived = ups[s - j] if j < s else downs[j - s]
            value = arrived if value is None else jnp.where(here == s, arrived, value)
        items.append(value)
    blocks = jnp.asarray(order)[here]
    pair_items = [partner(value) for value in items]

    sums = jnp.sum(x, axis=0, dtype=F32)
    aux = jnp.concatenate([sums, labels[0].reshape(pix).astype(F32)])
    other = partner(aux)
    aux_p = other[0]
    for at in range(1, len(other)):
        aux_p = jnp.where(top == at, other[at], aux_p)
    every = lax.all_gather(jnp.stack([aux, aux_p]), "space", axis=0)
    means = (jnp.sum(every[:, :, :c_in], axis=0) / plan.total).astype(BF16)
    label_cols = jnp.broadcast_to(every[:, :, c_in:, None], (n, 2, pix, 128))
    mean_rows = jnp.broadcast_to(means[:, None, :], (2, 16, c_in))
    mean_cols = jnp.broadcast_to(means.astype(F32)[:, :, None], (2, c_in, 128))
    tab = jnp.asarray(plan.tables)[here]
    wcls = jnp.pad(w_cls, ((0, 0), (0, 128 - plan.classes)))

    state = None
    for q in range(n):
        slots = [([items[q]], (0, blocks[q], 0))]
        if q:
            slots.append((pair_items[q - 1], (top, blocks[q - 1], 1)))
        state = run_blocks(plan, slots, w_in, state)

    def finish(field, state, prev):
        d, g_proj, g_cls, spool = run_chain(
            plan, field, tab, state, label_cols[:, field], mean_rows[field],
            w_in, w_proj, wcls, class_weight,
        )
        return run_grads(plan, field, tab, state, d, spool, mean_cols[field], prev), g_proj, g_cls

    def mean_of(a, b):
        return (a.astype(BF16).astype(F32) + b.astype(BF16).astype(F32)) * 0.5

    own_in, own_proj, own_cls = finish(0, state, None)
    state, own_in = lax.optimization_barrier((state, own_in))
    state = run_blocks(plan, [(pair_items[n - 1], (top, blocks[n - 1], 1))], w_in, state)
    avg_in, pair_proj, pair_cls = finish(1, state, own_in)
    avg_proj = mean_of(own_proj, pair_proj)
    avg_cls = mean_of(own_cls, pair_cls)[:, :plan.classes]
    return avg_in[None], avg_proj[None], avg_cls[None]


def solution(mesh):
    n, reps = mesh.shape["space"], mesh.shape["rep"]

    def build(features, labels, w_in, w_proj, w_cls, class_weight, matching):
        _, rows, cols, c_in = features.shape
        plan = Plan(n, reps, rows // n, cols, c_in, w_proj.shape[1], w_cls.shape[1])
        return jax.shard_map(
            functools.partial(per_device, plan),
            mesh=mesh,
            in_specs=(P("rep", "space", None, None), P("rep", "space", None), P(), P(), P(), P(), P()),
            out_specs=(P("rep", "space", None), P("rep", "space", None), P("rep", "space", None)),
            check_vma=False,
        )(features, labels, w_in, w_proj, w_cls, class_weight, matching)

    return build
```

```python
import functools

import jax
import jax.numpy as jnp
import numpy as np
from jax import lax
from jax.experimental import pallas as pl
from jax.experimental.pallas import tpu as pltpu
from jax.sharding import PartitionSpec as P

LOSS_SCALE = 1024.0
RATE = 12
EDGE = 40
EXTRA = 16
BF16 = jnp.bfloat16
F32 = jnp.float32
BLOCK_VMEM = 32 * 1024 * 1024
FIELD_VMEM = 44 * 1024 * 1024


def nn(a, b):
    return lax.dot_general(a, b, (((1,), (0,)), ((), ())), preferred_element_type=F32)


def nt(a, b):
    return lax.dot_general(a, b, (((1,), (1,)), ((), ())), preferred_element_type=F32)


def identity(size):
    rows = lax.broadcasted_iota(jnp.int32, (size, size), 0)
    cols = lax.broadcasted_iota(jnp.int32, (size, size), 1)
    return (rows == cols).astype(F32).astype(BF16)


class Plan:
    def __init__(self, n, reps, rows, cols, c_in, c_out, classes):
        self.n, self.reps, self.rows, self.cols = n, reps, rows, cols
        self.c_in, self.c_out, self.classes = c_in, c_out, classes
        self.height = rows * n
        self.pix = rows * cols
        self.total = self.pix * n
        self.shifted = [k for k in (1, 2, 3) if RATE * k < self.height]
        self.direct = [k for k in range(4) if k not in self.shifted]
        self.n_sh = len(self.shifted)
        row = lambda k, a: [1 + 9 * (k - 1) + 3 * a + b for b in range(3)]
        still = [row(k, 1) for k in self.direct[1:]]
        self.loads = [[0] + (still[0] if still else [])] + still[1:]
        for k in self.shifted:
            self.loads += [row(k, a) for a in range(3)]
        self.units = 29
        self.unit_rows = c_in // n
        self.proj_rows = 5 * c_out // n
        self.cls_rows = c_out // n
        tables = [self.table(s) for s in range(n)]
        self.n_slots = max(t[1] for t in tables)
        self.depth = max(t[2] for t in tables)
        self.tables = np.array([
            sum((c + [[0] * 6] * (self.depth - len(c)) for c in t[0]), []) for t in tables
        ], np.int32).reshape(n, -1)
        self.flags = self.tables.shape[1]
        self.tables = np.concatenate([
            self.tables,
            np.array([[len(c) for c in t[0]] + t[3] + [s] for s, t in enumerate(tables)], np.int32),
        ], axis=1)

    def tap(self, t):
        if t == 0:
            return (0, 1, 1)
        if t == 28:
            return None
        k, rest = (t - 1) // 9 + 1, (t - 1) % 9
        a, b = rest // 3, rest % 3
        if a != 1 and k not in self.shifted:
            return "zero"
        return (k, a, b)

    def table(self, s):
        parts = [[] for _ in range(self.n)]
        slots = {}
        for local in range(self.units):
            unit = s * self.units + local
            c, tap = unit % self.n, self.tap(unit // self.n)
            if tap is None or tap == "zero":
                parts[c].append([0, 0, 0, 0, 1 if tap is None else 2, local])
                continue
            k, a, b = tap
            move = (a - 1) * RATE * k
            valid = [
                j for j in range(self.n)
                if any(0 <= self.rows * j + i - move < self.height for i in range(self.rows))
            ]
            slot = slots.setdefault((k, b), len(slots))
            parts[c].append([slot, move, valid[0], valid[-1] + 1, 0, local])
        want = [slots.get((k, b), -1) for k in range(4) for b in range(3)]
        return parts, len(slots), max(len(c) for c in parts), want


def pack_kernel(pix, x_ref, lab_ref, out_ref):
    x = x_ref[...]
    out_ref[:pix, :] = x
    total = jnp.sum(x.astype(F32), axis=0, keepdims=True)
    head = total.astype(BF16).astype(F32)
    mid = (total - head).astype(BF16).astype(F32)
    row = lax.broadcasted_iota(jnp.int32, (EXTRA, x.shape[1]), 0)
    extra = jnp.zeros((EXTRA, x.shape[1]), F32)
    for at, value in enumerate((head, mid, total - head - mid, lab_ref[...])):
        extra = jnp.where(row == at, value, extra)
    out_ref[pix:, :] = extra.astype(BF16)


def block_kernel(plan, n_cand, aliased, meta, *refs):
    rows, cols, c_in, c_out = plan.rows, plan.cols, plan.c_in, plan.c_out
    pix = plan.pix
    cands = refs[:n_cand]
    w_hbm = refs[n_cand]
    refs = refs[n_cand + 1 + (4 if aliased else 0):]
    xt_out, cat_out, s_out, aux_out = refs[:4]
    xin, wbuf, xtb, catb, sb, res, sem_x, sem_w, sem_o, sem_s = refs[4:]
    xbuf = xin.at[pl.ds(0, pix)]
    step = pl.program_id(0)
    source, block, field = meta[step, 0], meta[step, 1], meta[step, 2]

    for c in range(n_cand):
        @pl.when(source == c)
        def _(c=c):
            pltpu.make_async_copy(cands[c], xin, sem_x).start()

    def weights(group, taps):
        return [
            pltpu.make_async_copy(
                w_hbm.at[tap], wbuf.at[group, :, pl.ds(i * c_out, c_out)], sem_w.at[group, i]
            )
            for i, tap in enumerate(taps)
        ]

    @pl.when(step == 0)
    def _():
        for group, taps in enumerate(plan.loads):
            for copy in weights(group, taps):
                copy.start()
        res[:, :EDGE, :] = jnp.zeros((rows, EDGE, res.shape[2]), F32)
        res[:, EDGE + cols:, :] = jnp.zeros((rows, EDGE, res.shape[2]), F32)

    pltpu.make_async_copy(cands[0], xin, sem_x).wait()
    aux_copy = pltpu.make_async_copy(
        xin.at[pl.ds(pix, EXTRA)], aux_out.at[field, block], sem_o.at[2]
    )
    aux_copy.start()
    eye = identity(256)
    for c in range(c_in // 256):
        part = slice(c * 256, (c + 1) * 256)
        xtb[part, :] = nt(eye, xbuf[:, part]).astype(BF16)
    xt_copy = pltpu.make_async_copy(xtb, xt_out.at[field, block], sem_o.at[0])
    xt_copy.start()

    def in_field(move):
        first = block * rows + move
        return jnp.logical_and(first + rows - 1 >= 0, first < plan.height)

    def loaded(group, taps):
        @pl.when(step == 0)
        def _():
            for copy in weights(group, taps):
                copy.wait()

    def columns(k, first):
        r = RATE * k
        part = [slice(first + i * c_out, first + (i + 1) * c_out) for i in range(3)]
        return (
            res[:, EDGE - r:EDGE - r + cols, part[0]]
            + res[:, EDGE:EDGE + cols, part[1]]
            + res[:, EDGE + r:EDGE + r + cols, part[2]]
        )

    def relu_to(k, value):
        at = plan.direct.index(k)
        catb[:, at * c_out:(at + 1) * c_out] = (
            jnp.maximum(value, 0.0).astype(BF16).reshape(pix, c_out)
        )

    def shifted_copy(at):
        return pltpu.make_async_copy(
            sb.at[at], s_out.at[at, field, pl.ds(block * rows, rows)], sem_s.at[at]
        )

    group = 0
    first = c_out
    loaded(0, plan.loads[0])
    width = len(plan.loads[0]) * c_out
    res[:, EDGE:EDGE + cols, :width] = nn(xbuf[...], wbuf[0, :, :width]).reshape(
        rows, cols, width
    )
    relu_to(0, res[:, EDGE:EDGE + cols, :c_out])
    group = 1
    for k in plan.direct[1:]:
        if first + 3 * c_out > width:
            loaded(group, plan.loads[group])
            width, first = 3 * c_out, 0
            res[:, EDGE:EDGE + cols, :width] = nn(xbuf[...], wbuf[group, :, :width]).reshape(
                rows, cols, width
            )
            group += 1
        relu_to(k, columns(k, first))
        first += 3 * c_out
    cat_copy = pltpu.make_async_copy(catb, cat_out.at[field, block], sem_o.at[1])
    cat_copy.start()
    width = 3 * c_out
    for at, k in enumerate(plan.shifted):
        for a in range(3):
            loaded(group + 3 * at + a, plan.loads[group + 3 * at + a])

        def one(a, _, k=k, at=at, base=group + 3 * at):
            @pl.when(in_field((1 - a) * RATE * k))
            def _():
                res[:, EDGE:EDGE + cols, :width] = nn(
                    xbuf[...], wbuf[base + a, :, :width]
                ).reshape(rows, cols, width)
                sb[3 * at + a] = columns(k, 0)
                shifted_copy(3 * at + a).start()
            return 0

        lax.fori_loop(0, 3, one, 0)
    aux_copy.wait()
    xt_copy.wait()
    cat_copy.wait()
    for at, k in enumerate(plan.shifted):
        for a in range(3):
            @pl.when(in_field((1 - a) * RATE * k))
            def _(at=at, a=a):
                shifted_copy(3 * at + a).wait()


def run_blocks(plan, slots, w_in, state):
    arrays, meta = [], []
    for cands, (source, block, field) in slots:
        meta.append(jnp.stack([
            jnp.asarray(v, jnp.int32) for v in (source + len(arrays), block, field)
        ]))
        arrays.extend(cands)
    meta = jnp.stack(meta)
    n, rows, cols, pix = plan.n, plan.rows, plan.cols, plan.pix
    c_in, c_out, n_sh = plan.c_in, plan.c_out, plan.n_sh
    shapes = [
        jax.ShapeDtypeStruct((2, n, c_in, pix), BF16),
        jax.ShapeDtypeStruct((2, n, pix, len(plan.direct) * c_out), BF16),
        jax.ShapeDtypeStruct((3 * n_sh, 2, n * rows, cols, c_out), F32),
        jax.ShapeDtypeStruct((2, n, EXTRA, c_in), BF16),
    ]
    aliased = state is not None
    operands = [*arrays, w_in] + (list(state) if aliased else [])
    aliases = {1 + len(arrays) + 1 + i: i for i in range(4)} if aliased else {}
    widest = max(len(g) for g in plan.loads) * c_out
    return pl.pallas_call(
        functools.partial(block_kernel, plan, len(arrays), aliased),
        grid_spec=pltpu.PrefetchScalarGridSpec(
            num_scalar_prefetch=1,
            grid=(len(slots),),
            in_specs=[pl.BlockSpec(memory_space=pl.ANY)] * len(operands),
            out_specs=[pl.BlockSpec(memory_space=pl.ANY)] * 4,
            scratch_shapes=[
                pltpu.VMEM((pix + EXTRA, c_in), BF16),
                pltpu.VMEM((len(plan.loads), c_in, widest), BF16),
                pltpu.VMEM((c_in, pix), BF16),
                pltpu.VMEM((pix, len(plan.direct) * c_out), BF16),
                pltpu.VMEM((3 * n_sh, rows, cols, c_out), F32),
                pltpu.VMEM((rows, cols + 2 * EDGE, widest), F32),
                pltpu.SemaphoreType.DMA,
                pltpu.SemaphoreType.DMA((len(plan.loads), 4)),
                pltpu.SemaphoreType.DMA((3,)),
                pltpu.SemaphoreType.DMA((3 * n_sh,)),
            ],
        ),
        out_shape=shapes,
        input_output_aliases=aliases,
        compiler_params=pltpu.CompilerParams(
            dimension_semantics=("arbitrary",), vmem_limit_bytes=BLOCK_VMEM
        ),
        cost_estimate=pl.CostEstimate(
            flops=len(slots) * 2 * pix * c_in * c_out * (10 + 6 * n_sh),
            bytes_accessed=20_000_000 + len(slots) * 20_000_000,
            transcendentals=0,
        ),
        name="block_forward",
    )(meta, *operands)


def field_kernel(plan, last, tab, *refs):
    n, rows, cols, pix = plan.n, plan.rows, plan.cols, plan.pix
    c_in, c_out, n_sh = plan.c_in, plan.c_out, plan.n_sh
    n_rows_in = 2 * n_sh * rows
    unit_rows, depth, flags = plan.unit_rows, plan.depth, plan.flags
    cat_ref = refs[0]
    mid_refs = refs[1:1 + n_sh]
    s_refs = refs[1 + n_sh:1 + n_sh + n_rows_in]
    refs = refs[1 + n_sh + n_rows_in:]
    aux_ref, all_ref, w28_ref, wproj_ref, wcls_ref, cw_ref, xt_ref = refs[:7]
    refs = refs[7:]
    if last:
        prev_g, prev_p, prev_c = refs[:3]
        refs = refs[3:]
    g_out, p_out, c_ref_out = refs[:3]
    dbuf, pad, mean, gpt, gp, gc, sdy, spool, pact, cat5, acc, stage, sems = refs[3:]
    step = pl.program_id(0)
    edge_rows = rows - 1

    def finish(value, prev):
        grad = value.astype(BF16)
        if not last:
            return grad
        return (prev.astype(F32) + grad.astype(F32)) * 0.5

    @pl.when(step == 0)
    def _():
        zero = jnp.zeros((edge_rows, cols, c_out), BF16)
        for slot in range(plan.n_slots):
            dbuf[slot, :edge_rows] = zero
            dbuf[slot, edge_rows + plan.height:] = zero
        pad[:, :EDGE, :] = jnp.zeros((rows, EDGE, c_out), F32)
        pad[:, EDGE + cols:, :] = jnp.zeros((rows, EDGE, c_out), F32)
        gpt[...] = jnp.zeros_like(gpt)
        gc[...] = jnp.zeros_like(gc)
        sdy[...] = jnp.zeros_like(sdy)
        total = jnp.zeros((1, c_in), F32)
        for j in range(n):
            extra = all_ref[j].astype(F32)
            total = total + ((extra[2:3] + extra[1:2]) + extra[0:1])
        mean_in = (total / plan.total).astype(BF16)
        mean[...] = jnp.broadcast_to(mean_in.astype(F32), (16, c_in))
        pact[...] = nn(mean[...].astype(BF16), w28_ref[0])

    @pl.when(step < n)
    def _():
        block = step
        for k in range(4):
            part = slice(k * c_out, (k + 1) * c_out)
            if k in plan.shifted:
                at = plan.shifted.index(k)
                r = RATE * k
                pre = mid_refs[at]
                for i in range(rows):
                    h = block * rows + i
                    line = pre[i]
                    for side, src in ((0, h - r), (1, h + r)):
                        ok = jnp.logical_and(src >= 0, src < plan.height)
                        ref = s_refs[(2 * at + side) * rows + i]
                        line = line + jnp.where(ok, ref[...], 0.0)
                    cat5[i * cols:(i + 1) * cols, part] = jnp.maximum(line, 0.0).astype(BF16)
            else:
                at = plan.direct.index(k)
                cat5[:, part] = cat_ref[:, at * c_out:(at + 1) * c_out]
        pool_act = jnp.maximum(pact[0:1, :], 0.0).astype(BF16)
        cat5[:, 4 * c_out:] = jnp.broadcast_to(pool_act, (pix, c_out))
        y_pre = nn(cat5[...], wproj_ref[...])
        y_act = jnp.maximum(y_pre, 0.0).astype(BF16)
        logits = nn(y_act, wcls_ref[...])
        lane = lax.broadcasted_iota(jnp.int32, (pix, 128), 1)
        live = lane < plan.classes
        expo = jnp.where(live, jnp.exp(logits), 0.0)
        prob = expo / jnp.sum(expo, axis=1, keepdims=True)
        names = aux_ref[3:4, :512].astype(F32)
        label = jnp.broadcast_to(names, (128, 512)).T[:pix]
        onehot = jnp.where(label == lane.astype(F32), 1.0, 0.0)
        weight = jnp.zeros((pix, 128), F32)
        for c in range(plan.classes):
            weight = jnp.where(label == float(c), cw_ref[c], weight)
        d_logits = jnp.where(
            live, (prob - onehot) * weight * (LOSS_SCALE / plan.total), 0.0
        ).astype(BF16)
        d_y = jnp.where(y_pre > 0, nt(d_logits, wcls_ref[...]), 0.0).astype(BF16)
        sdy[0:1, :] += jnp.sum(d_y.astype(F32), axis=0, keepdims=True)
        gpt[...] += nn(nt(identity(c_out), d_y).astype(BF16), cat5[...])
        gc[...] += nn(nt(identity(128), d_logits).astype(BF16), y_act)
        for k in range(4):
            want = [tab[flags + n + 3 * k + b] for b in range(3)]
            part = slice(k * c_out, (k + 1) * c_out)

            @pl.when((want[0] >= 0) | (want[1] >= 0) | (want[2] >= 0))
            def _(k=k, want=want, part=part):
                d_cat = nt(d_y, wproj_ref[part, :])
                d_k = jnp.where(cat5[:, part] > 0, d_cat, 0.0).astype(BF16)
                d_k = d_k.reshape(rows, cols, c_out)
                if k > 0:
                    pad[:, EDGE:EDGE + cols, :] = d_k.astype(F32)
                at = pl.ds(block * rows + edge_rows, rows)
                for b in range(3):
                    if k == 0 and b != 1:
                        continue

                    @pl.when(want[b] >= 0)
                    def _(b=b):
                        slot = jnp.maximum(want[b], 0)
                        if b == 1:
                            dbuf[slot, at] = d_k
                        else:
                            first = EDGE + (1 - b) * RATE * k
                            dbuf[slot, at] = pad[:, first:first + cols, :].astype(BF16)

    @pl.when(step == n - 1)
    def _():
        pool = wproj_ref[4 * c_out:, :]
        rest = sdy[...]
        total = jnp.zeros(sdy.shape, F32)
        for _i in range(3):
            head = rest.astype(BF16)
            total = total + nt(head, pool)
            rest = rest - head.astype(F32)
        spool[...] = jnp.where(pact[...] > 0, jnp.broadcast_to(total[0:1, :], total.shape), 0.0)
        for c in range(5):
            gp[c * c_out:(c + 1) * c_out, :] = gpt[:, c * c_out:(c + 1) * c_out].T
        index = tab[flags + n + 12]
        first = pl.multiple_of(index * plan.proj_rows, plan.proj_rows)
        p_out[...] = finish(gp[pl.ds(first, plan.proj_rows), :], prev_p[...] if last else None)
        gp[:c_out, :128] = gc[...].T
        first = pl.multiple_of(index * plan.cls_rows, plan.cls_rows)
        c_ref_out[...] = finish(
            gp[pl.ds(first, plan.cls_rows), :128], prev_c[...] if last else None
        )

    def out_copy(part, slot, t):
        row = tab[(part * depth + t) * 6 + 5] * unit_rows
        return pltpu.make_async_copy(
            stage.at[slot, t],
            g_out.at[pl.ds(pl.multiple_of(row, unit_rows), unit_rows)],
            sems.at[slot, t],
        )

    @pl.when(step >= n)
    def _():
        part = step - n
        parity = lax.rem(part, 2)

        def one(t, _):
            base = (part * depth + t) * 6
            slot, move, low, high = tab[base], tab[base + 1], tab[base + 2], tab[base + 3]
            kind = tab[base + 4]

            def term(j):
                first = j * rows - move + edge_rows
                return nn(xt_ref[j], dbuf[slot, pl.ds(first, rows)].reshape(pix, c_out))

            whole = jnp.logical_and(low == 0, high == n)

            @pl.when(whole)
            def _():
                total = term(0)
                for j in range(1, n):
                    total = total + term(j)
                acc[...] = total

            @pl.when(jnp.logical_not(whole))
            def _():
                acc[...] = jnp.zeros_like(acc)

                def add(j, _):
                    acc[...] += term(j)
                    return 0

                lax.fori_loop(low, high, add, 0)

            @pl.when(kind == 1)
            def _():
                first = pl.multiple_of(part * unit_rows, unit_rows)
                row = mean[0:1, pl.ds(first, unit_rows)]
                column = jnp.broadcast_to(row, (128, unit_rows)).T
                for c in range(c_out // 128):
                    lanes = slice(c * 128, (c + 1) * 128)
                    acc[:, lanes] = column * spool[0:1, lanes]

            if last:
                stage[parity, t] = finish(acc[...], prev_g[t])
                out_copy(part, parity, t).start()
            else:
                g_out[t] = finish(acc[...], None)
            return 0

        lax.fori_loop(0, tab[flags + part], one, 0)

        if last:
            def drain(which, slot):
                def one(t, _):
                    out_copy(which, slot, t).wait()
                    return 0
                lax.fori_loop(0, tab[flags + which], one, 0)

            @pl.when(part > 0)
            def _():
                drain(part - 1, 1 - parity)

            @pl.when(part == n - 1)
            def _():
                drain(part, parity)


def run_field(plan, field, tab, state, w_in, w_proj, wcls, cw, prev):
    n, rows, cols, pix = plan.n, plan.rows, plan.cols, plan.pix
    c_in, c_out, n_sh = plan.c_in, plan.c_out, plan.n_sh
    unit_rows, depth = plan.unit_rows, plan.depth
    last = prev is not None
    xt, cat, s, aux = state

    def blk(i):
        return jnp.minimum(i, n - 1)

    def part(i):
        return jnp.maximum(i - n, 0)

    in_specs = [
        pl.BlockSpec(
            (None, None, pix, len(plan.direct) * c_out), lambda i, t: (field, blk(i), 0, 0)
        ),
    ]
    operands = [cat]
    for at in range(n_sh):
        in_specs.append(pl.BlockSpec(
            (None, None, rows, cols, c_out),
            lambda i, t, at=at: (3 * at + 1, field, blk(i), 0, 0),
        ))
        operands.append(s)
    for at, k in enumerate(plan.shifted):
        for side in range(2):
            move = (2 * side - 1) * RATE * k
            for row in range(rows):
                def index(i, t, at=at, side=side, move=move, row=row):
                    h = jnp.clip(blk(i) * rows + row + move, 0, plan.height - 1)
                    return (3 * at + 2 * side, field, h, 0, 0)
                in_specs.append(pl.BlockSpec((None, None, None, cols, c_out), index))
                operands.append(s)
    in_specs += [
        pl.BlockSpec((None, None, EXTRA, c_in), lambda i, t: (field, blk(i), 0, 0)),
        pl.BlockSpec((None, n, EXTRA, c_in), lambda i, t: (field, 0, 0, 0)),
        pl.BlockSpec((1, c_in, c_out), lambda i, t: (28, 0, 0)),
        pl.BlockSpec((5 * c_out, c_out), lambda i, t: (0, 0)),
        pl.BlockSpec((c_out, 128), lambda i, t: (0, 0)),
        pl.BlockSpec(memory_space=pltpu.SMEM),
        pl.BlockSpec((None, n, unit_rows, pix), lambda i, t: (field, 0, part(i), 0)),
    ]
    operands += [aux, aux, w_in, w_proj, wcls, cw, xt]
    kind = F32 if last else BF16
    inner = pl.BlockSpec((None, depth, unit_rows, c_out), lambda i, t: (part(i), 0, 0, 0))
    small = [
        pl.BlockSpec((plan.proj_rows, c_out), lambda i, t: (0, 0)),
        pl.BlockSpec((plan.cls_rows, 128), lambda i, t: (0, 0)),
    ]
    if last:
        in_specs += [inner] + small
        operands += list(prev)
        main_spec = pl.BlockSpec(memory_space=pl.ANY)
        main_shape = jax.ShapeDtypeStruct((plan.units * unit_rows, c_out), F32)
    else:
        main_spec = inner
        main_shape = jax.ShapeDtypeStruct((n, depth, unit_rows, c_out), BF16)
    return pl.pallas_call(
        functools.partial(field_kernel, plan, last),
        grid_spec=pltpu.PrefetchScalarGridSpec(
            num_scalar_prefetch=1,
            grid=(2 * n,),
            in_specs=in_specs,
            out_specs=[main_spec] + small,
            scratch_shapes=[
                pltpu.VMEM((plan.n_slots, plan.height + 2 * (rows - 1), cols, c_out), BF16),
                pltpu.VMEM((rows, cols + 2 * EDGE, c_out), F32),
                pltpu.VMEM((16, c_in), F32),
                pltpu.VMEM((c_out, 5 * c_out), F32),
                pltpu.VMEM((5 * c_out, c_out), F32),
                pltpu.VMEM((128, c_out), F32),
                pltpu.VMEM((16, c_out), F32),
                pltpu.VMEM((16, c_out), F32),
                pltpu.VMEM((16, c_out), F32),
                pltpu.VMEM((pix, 5 * c_out), BF16),
                pltpu.VMEM((unit_rows, c_out), F32),
                pltpu.VMEM((2, depth if last else 1, unit_rows, c_out), F32),
                pltpu.SemaphoreType.DMA((2, depth)),
            ],
        ),
        out_shape=[
            main_shape,
            jax.ShapeDtypeStruct((plan.proj_rows, c_out), kind),
            jax.ShapeDtypeStruct((plan.cls_rows, 128), kind),
        ],
        compiler_params=pltpu.CompilerParams(
            dimension_semantics=("arbitrary",), vmem_limit_bytes=FIELD_VMEM
        ),
        cost_estimate=pl.CostEstimate(
            flops=10_000_000_000, bytes_accessed=90_000_000, transcendentals=0
        ),
        name="field_grads",
    )(tab, *operands)


def after(value, *others):
    return lax.optimization_barrier((value, *others))[0]


def per_device(plan, features, labels, w_in, w_proj, w_cls, class_weight, matching):
    n, reps, rows, pix, c_in = plan.n, plan.reps, plan.rows, plan.pix, plan.c_in
    names = jnp.pad(labels[0].reshape(1, pix).astype(F32), ((0, 0), (0, c_in - pix)))
    x = pl.pallas_call(
        functools.partial(pack_kernel, pix),
        out_shape=jax.ShapeDtypeStruct((pix + EXTRA, c_in), BF16),
        name="pack",
    )(features[0].reshape(pix, c_in), names)
    here = lax.axis_index("space")
    n_bits = reps.bit_length() - 1
    bits = [jnp.bitwise_and(jnp.right_shift(matching[0], b), 1) == 1 for b in range(n_bits)]
    top = jnp.int32(0)
    for b in range(n_bits):
        top = jnp.where(bits[b], n_bits - 1 - b, top)
    tab = jnp.asarray(plan.tables)[here]
    wcls = jnp.pad(w_cls, ((0, 0), (0, 128 - plan.classes)))

    def along(value, way, step):
        pairs = [
            (i, i + way) for i in range(n)
            if 0 <= i + way < n and 0 <= i - way * (step - 1) < n
        ]
        return lax.ppermute(value, "space", pairs)

    def hop(value, b):
        return lax.ppermute(value, "rep", [(r, r ^ (1 << b)) for r in range(reps)])

    order = np.array(
        [sorted(range(n), key=lambda j: (abs(j - s), j)) for s in range(n)], np.int32
    )
    blocks = jnp.asarray(order)[here]

    def arrival(q, ups, downs):
        value = None
        for s in range(n):
            j = int(order[s, q])
            arrived = ups[s - j] if j < s else downs[j - s]
            value = arrived if value is None else jnp.where(here == s, arrived, value)
        return value

    common = (w_in, w_proj, wcls, class_weight)
    ups, downs, items = [x], [x], [x]
    values, moves = {}, {q: [] for q in range(n)}
    state, grads = None, None

    def pair(q):
        return (moves[q], (top, blocks[q], 1))

    for t in range(1, n + n_bits - 1):
        q = t - 1
        if t < n:
            ups.append(along(ups[-1], 1, t))
            downs.append(along(downs[-1], -1, t))
        tie = []
        if q < n:
            moved = hop(items[q], 0)
            moves[q].insert(0, moved)
            values[q] = jnp.where(bits[0], moved, items[q])
            tie = [values[q]]
        sent = []
        for b in range(1, n_bits):
            if 0 <= t - b < n:
                moves[t - b].insert(0, hop(values[t - b], b))
                sent.append((t - b, b))
        if q < n:
            slots = [([after(items[q], *tie)], (0, blocks[q], 0))]
            if t >= n_bits:
                slots.append(pair(t - n_bits))
            state = run_blocks(plan, slots, w_in, state)
        if q == n:
            grads = tuple(run_field(plan, 0, tab, state, *common, None))
        for at, b in sent:
            if b + 1 < n_bits:
                values[at] = jnp.where(bits[b], moves[at][0], values[at])
        if t < n:
            items.append(arrival(t, ups, downs))
        live = (ups, downs, items, values, moves, state, grads)
        ups, downs, items, values, moves, state, grads = lax.optimization_barrier(live)
    if grads is None:
        grads = tuple(run_field(plan, 0, tab, state, *common, None))
        state, grads = lax.optimization_barrier((state, grads))
    done = max(0, n - n_bits + 1)
    state = run_blocks(plan, [pair(q) for q in range(done, n)], w_in, state)
    avg_in, avg_proj, avg_cls = run_field(plan, 1, tab, state, *common, grads)
    return avg_in[None], avg_proj[None], avg_cls[None, :, :plan.classes]


def solution(mesh):
    n, reps = mesh.shape["space"], mesh.shape["rep"]

    def build(features, labels, w_in, w_proj, w_cls, class_weight, matching):
        _, rows, cols, c_in = features.shape
        plan = Plan(n, reps, rows // n, cols, c_in, w_proj.shape[1], w_cls.shape[1])
        return jax.shard_map(
            functools.partial(per_device, plan),
            mesh=mesh,
            in_specs=(P("rep", "space", None, None), P("rep", "space", None), P(), P(), P(), P(), P()),
            out_specs=(P("rep", "space", None), P("rep", "space", None), P("rep", "space", None)),
            check_vma=False,
        )(features, labels, w_in, w_proj, w_cls, class_weight, matching)

    return build
```

```python
import functools

import jax
import jax.numpy as jnp
import numpy as np
from jax import lax
from jax.experimental import pallas as pl
from jax.experimental.pallas import tpu as pltpu
from jax.sharding import PartitionSpec as P

LOSS_SCALE = 1024.0
RATE = 12
EDGE = 40
EXTRA = 16
BF16 = jnp.bfloat16
F32 = jnp.float32
BLOCK_VMEM = 60 * 1024 * 1024
FIELD_VMEM = 60 * 1024 * 1024


def nn(a, b):
    return lax.dot_general(a, b, (((1,), (0,)), ((), ())), preferred_element_type=F32)


def nt(a, b):
    return lax.dot_general(a, b, (((1,), (1,)), ((), ())), preferred_element_type=F32)


def identity(size):
    rows = lax.broadcasted_iota(jnp.int32, (size, size), 0)
    cols = lax.broadcasted_iota(jnp.int32, (size, size), 1)
    return (rows == cols).astype(F32).astype(BF16)


class Plan:
    def __init__(self, n, reps, rows, cols, c_in, c_out, classes):
        self.n, self.reps, self.rows, self.cols = n, reps, rows, cols
        self.c_in, self.c_out, self.classes = c_in, c_out, classes
        self.height = rows * n
        self.pix = rows * cols
        self.total = self.pix * n
        self.shifted = [k for k in (1, 2, 3) if RATE * k < self.height]
        self.direct = [k for k in range(4) if k not in self.shifted]
        self.n_sh = len(self.shifted)
        row = lambda k, a: [1 + 9 * (k - 1) + 3 * a + b for b in range(3)]
        still = [row(k, 1) for k in self.direct[1:]]
        self.loads = [[0] + (still[0] if still else [])] + still[1:]
        for k in self.shifted:
            self.loads += [row(k, a) for a in range(3)]
        self.units = 29
        self.unit_rows = c_in // n
        self.proj_rows = 5 * c_out // n
        self.cls_rows = c_out // n
        starts = [self.proj_rows * s // 128 * 128 for s in range(n)]
        ends = [-(-self.proj_rows * (s + 1) // 128) * 128 for s in range(n)]
        self.window = max(e - b for b, e in zip(starts, ends))
        self.starts = [min(b, 5 * c_out - self.window) for b in starts]
        tables = [self.table(s) for s in range(n)]
        self.n_slots = max(t[1] for t in tables)
        self.depth = max(t[2] for t in tables)
        self.tables = np.array([
            sum((c + [[0] * 6] * (self.depth - len(c)) for c in t[0]), []) for t in tables
        ], np.int32).reshape(n, -1)
        self.flags = self.tables.shape[1]
        self.tables = np.concatenate([
            self.tables,
            np.array([
                [len(c) for c in t[0]] + t[3] + [s, self.starts[s]] for s, t in enumerate(tables)
            ], np.int32),
        ], axis=1)

    def tap(self, t):
        if t == 0:
            return (0, 1, 1)
        if t == 28:
            return None
        k, rest = (t - 1) // 9 + 1, (t - 1) % 9
        a, b = rest // 3, rest % 3
        if a != 1 and k not in self.shifted:
            return "zero"
        return (k, a, b)

    def table(self, s):
        parts = [[] for _ in range(self.n)]
        here = range(s * self.units, (s + 1) * self.units)
        slots = {}
        for k in range(4):
            for b in ((1,) if k == 0 else range(3)):
                if any(
                    isinstance(self.tap(u // self.n), tuple)
                    and (self.tap(u // self.n)[0], self.tap(u // self.n)[2]) == (k, b)
                    for u in here
                ):
                    slots[(k, b)] = len(slots)
        for unit in here:
            c, tap = unit % self.n, self.tap(unit // self.n)
            local = unit - s * self.units
            if tap is None or tap == "zero":
                parts[c].append([0, 0, 0, 0, 1 if tap is None else 2, local])
                continue
            k, a, b = tap
            move = (a - 1) * RATE * k
            valid = [
                j for j in range(self.n)
                if any(0 <= self.rows * j + i - move < self.height for i in range(self.rows))
            ]
            entry = [slots[(k, b)], move, valid[0], valid[-1] + 1, 0, local]
            if b == 2 and len(parts[c]) > 1 and all(
                e[4] == 0 and e[:4] == [entry[0] - back] + entry[1:4]
                for back, e in ((1, parts[c][-1]), (2, parts[c][-2]))
            ):
                parts[c][-2][4] = 3
                parts[c][-1][4] = 4
                entry[4] = 4
            parts[c].append(entry)
        want = [slots.get((k, b), -1) for k in range(4) for b in range(3)]
        return parts, len(slots), max(len(c) for c in parts), want


def pack_kernel(pix, x_ref, lab_ref, out_ref):
    x = x_ref[...]
    out_ref[:pix, :] = x
    total = jnp.sum(x.astype(F32), axis=0, keepdims=True)
    head = total.astype(BF16).astype(F32)
    mid = (total - head).astype(BF16).astype(F32)
    row = lax.broadcasted_iota(jnp.int32, (EXTRA, x.shape[1]), 0)
    extra = jnp.zeros((EXTRA, x.shape[1]), F32)
    for at, value in enumerate((head, mid, total - head - mid, lab_ref[...])):
        extra = jnp.where(row == at, value, extra)
    out_ref[pix:, :] = extra.astype(BF16)


def block_kernel(plan, n_cand, aliased, meta, *refs):
    rows, cols, c_in, c_out = plan.rows, plan.cols, plan.c_in, plan.c_out
    pix = plan.pix
    cands = refs[:n_cand]
    w_hbm = refs[n_cand]
    refs = refs[n_cand + 1 + (4 if aliased else 0):]
    xt_out, cat_out, s_out, aux_out = refs[:4]
    xin, wbuf, xtb, catb, sb, res, sem_x, sem_w, sem_o, sem_s = refs[4:]
    xbuf = xin.at[pl.ds(0, pix)]
    step = pl.program_id(0)
    source, block, field = meta[step, 0], meta[step, 1], meta[step, 2]

    for c in range(n_cand):
        @pl.when(source == c)
        def _(c=c):
            pltpu.make_async_copy(cands[c], xin, sem_x).start()

    def weights(group, taps):
        return [
            pltpu.make_async_copy(
                w_hbm.at[tap], wbuf.at[group, :, pl.ds(i * c_out, c_out)], sem_w.at[group, i]
            )
            for i, tap in enumerate(taps)
        ]

    @pl.when(step == 0)
    def _():
        for group, taps in enumerate(plan.loads):
            for copy in weights(group, taps):
                copy.start()
        res[:, :EDGE, :] = jnp.zeros((rows, EDGE, res.shape[2]), F32)
        res[:, EDGE + cols:, :] = jnp.zeros((rows, EDGE, res.shape[2]), F32)

    pltpu.make_async_copy(cands[0], xin, sem_x).wait()
    aux_copy = pltpu.make_async_copy(
        xin.at[pl.ds(pix, EXTRA)], aux_out.at[field, block], sem_o.at[2]
    )
    aux_copy.start()
    eye = identity(256)
    for c in range(c_in // 256):
        part = slice(c * 256, (c + 1) * 256)
        xtb[part, :] = nt(eye, xbuf[:, part]).astype(BF16)
    xt_copy = pltpu.make_async_copy(xtb, xt_out.at[field, block], sem_o.at[0])
    xt_copy.start()

    def in_field(move):
        first = block * rows + move
        return jnp.logical_and(first + rows - 1 >= 0, first < plan.height)

    def loaded(group, taps):
        @pl.when(step == 0)
        def _():
            for copy in weights(group, taps):
                copy.wait()

    def columns(k, first):
        r = RATE * k
        part = [slice(first + i * c_out, first + (i + 1) * c_out) for i in range(3)]
        return (
            res[:, EDGE - r:EDGE - r + cols, part[0]]
            + res[:, EDGE:EDGE + cols, part[1]]
            + res[:, EDGE + r:EDGE + r + cols, part[2]]
        )

    def relu_to(k, value):
        at = plan.direct.index(k)
        catb[:, at * c_out:(at + 1) * c_out] = (
            jnp.maximum(value, 0.0).astype(BF16).reshape(pix, c_out)
        )

    def shifted_copy(at):
        return pltpu.make_async_copy(
            sb.at[at], s_out.at[at, field, pl.ds(block * rows, rows)], sem_s.at[at]
        )

    group = 0
    first = c_out
    loaded(0, plan.loads[0])
    width = len(plan.loads[0]) * c_out
    res[:, EDGE:EDGE + cols, :width] = nn(xbuf[...], wbuf[0, :, :width]).reshape(
        rows, cols, width
    )
    relu_to(0, res[:, EDGE:EDGE + cols, :c_out])
    group = 1
    for k in plan.direct[1:]:
        if first + 3 * c_out > width:
            loaded(group, plan.loads[group])
            width, first = 3 * c_out, 0
            res[:, EDGE:EDGE + cols, :width] = nn(xbuf[...], wbuf[group, :, :width]).reshape(
                rows, cols, width
            )
            group += 1
        relu_to(k, columns(k, first))
        first += 3 * c_out
    cat_copy = pltpu.make_async_copy(catb, cat_out.at[field, block], sem_o.at[1])
    cat_copy.start()
    width = 3 * c_out
    for at, k in enumerate(plan.shifted):
        for a in range(3):
            loaded(group + 3 * at + a, plan.loads[group + 3 * at + a])

        def one(a, _, k=k, at=at, base=group + 3 * at):
            @pl.when(in_field((1 - a) * RATE * k))
            def _():
                res[:, EDGE:EDGE + cols, :width] = nn(
                    xbuf[...], wbuf[base + a, :, :width]
                ).reshape(rows, cols, width)
                sb[3 * at + a] = columns(k, 0)
                shifted_copy(3 * at + a).start()
            return 0

        lax.fori_loop(0, 3, one, 0)
    aux_copy.wait()
    xt_copy.wait()
    cat_copy.wait()
    for at, k in enumerate(plan.shifted):
        for a in range(3):
            @pl.when(in_field((1 - a) * RATE * k))
            def _(at=at, a=a):
                shifted_copy(3 * at + a).wait()


def run_blocks(plan, slots, w_in, state):
    arrays, meta = [], []
    for cands, (source, block, field) in slots:
        meta.append(jnp.stack([
            jnp.asarray(v, jnp.int32) for v in (source + len(arrays), block, field)
        ]))
        arrays.extend(cands)
    meta = jnp.stack(meta)
    n, rows, cols, pix = plan.n, plan.rows, plan.cols, plan.pix
    c_in, c_out, n_sh = plan.c_in, plan.c_out, plan.n_sh
    shapes = [
        jax.ShapeDtypeStruct((2, n, c_in, pix), BF16),
        jax.ShapeDtypeStruct((2, n, pix, len(plan.direct) * c_out), BF16),
        jax.ShapeDtypeStruct((3 * n_sh, 2, n * rows, cols, c_out), F32),
        jax.ShapeDtypeStruct((2, n, EXTRA, c_in), BF16),
    ]
    aliased = state is not None
    operands = [*arrays, w_in] + (list(state) if aliased else [])
    aliases = {1 + len(arrays) + 1 + i: i for i in range(4)} if aliased else {}
    widest = max(len(g) for g in plan.loads) * c_out
    return pl.pallas_call(
        functools.partial(block_kernel, plan, len(arrays), aliased),
        grid_spec=pltpu.PrefetchScalarGridSpec(
            num_scalar_prefetch=1,
            grid=(len(slots),),
            in_specs=[pl.BlockSpec(memory_space=pl.ANY)] * len(operands),
            out_specs=[pl.BlockSpec(memory_space=pl.ANY)] * 4,
            scratch_shapes=[
                pltpu.VMEM((pix + EXTRA, c_in), BF16),
                pltpu.VMEM((len(plan.loads), c_in, widest), BF16),
                pltpu.VMEM((c_in, pix), BF16),
                pltpu.VMEM((pix, len(plan.direct) * c_out), BF16),
                pltpu.VMEM((3 * n_sh, rows, cols, c_out), F32),
                pltpu.VMEM((rows, cols + 2 * EDGE, widest), F32),
                pltpu.SemaphoreType.DMA,
                pltpu.SemaphoreType.DMA((len(plan.loads), 4)),
                pltpu.SemaphoreType.DMA((3,)),
                pltpu.SemaphoreType.DMA((3 * n_sh,)),
            ],
        ),
        out_shape=shapes,
        input_output_aliases=aliases,
        compiler_params=pltpu.CompilerParams(
            dimension_semantics=("arbitrary",), vmem_limit_bytes=BLOCK_VMEM
        ),
        cost_estimate=pl.CostEstimate(
            flops=len(slots) * 2 * pix * c_in * c_out * (10 + 6 * n_sh),
            bytes_accessed=20_000_000 + len(slots) * 20_000_000,
            transcendentals=0,
        ),
        name="block_forward",
    )(meta, *operands)


def field_kernel(plan, last, tab, *refs):
    n, rows, cols, pix = plan.n, plan.rows, plan.cols, plan.pix
    c_in, c_out, n_sh = plan.c_in, plan.c_out, plan.n_sh
    n_rows_in = 2 * n_sh * rows
    unit_rows, depth, flags = plan.unit_rows, plan.depth, plan.flags
    cat_ref = refs[0]
    mid_refs = refs[1:1 + n_sh]
    s_refs = refs[1 + n_sh:1 + n_sh + n_rows_in]
    refs = refs[1 + n_sh + n_rows_in:]
    aux_ref, all_ref, w28_ref, wproj_ref, wcls_ref, cw_ref, xt_ref = refs[:7]
    refs = refs[7:]
    if last:
        prev_g, prev_p, prev_c = refs[:3]
        refs = refs[3:]
    g_out, p_out, c_ref_out = refs[:3]
    dbuf, pad, mean, gpt, gp, gc, sdy, spool, pact, cat5, acc, stage, sems = refs[3:]
    step = pl.program_id(0)
    edge_rows = rows - 1

    def finish(value, prev):
        grad = value.astype(BF16)
        if not last:
            return grad
        return (prev.astype(F32) + grad.astype(F32)) * 0.5

    @pl.when(step == 0)
    def _():
        zero = jnp.zeros((edge_rows, cols, dbuf.shape[2]), BF16)
        dbuf[:edge_rows] = zero
        dbuf[edge_rows + plan.height:] = zero
        pad[:, :EDGE, :] = jnp.zeros((rows, EDGE, c_out), F32)
        pad[:, EDGE + cols:, :] = jnp.zeros((rows, EDGE, c_out), F32)
        gpt[...] = jnp.zeros_like(gpt)
        gc[...] = jnp.zeros_like(gc)
        sdy[...] = jnp.zeros_like(sdy)
        total = jnp.zeros((1, c_in), F32)
        for j in range(n):
            extra = all_ref[j].astype(F32)
            total = total + ((extra[2:3] + extra[1:2]) + extra[0:1])
        mean_in = (total / plan.total).astype(BF16)
        mean[...] = jnp.broadcast_to(mean_in.astype(F32), (16, c_in))
        pact[...] = nn(mean[...].astype(BF16), w28_ref[0])

    @pl.when(step < n)
    def _():
        block = step
        for k in range(4):
            part = slice(k * c_out, (k + 1) * c_out)
            if k in plan.shifted:
                at = plan.shifted.index(k)
                r = RATE * k
                pre = mid_refs[at]
                for i in range(rows):
                    h = block * rows + i
                    line = pre[i]
                    for side, src in ((0, h - r), (1, h + r)):
                        ok = jnp.logical_and(src >= 0, src < plan.height)
                        ref = s_refs[(2 * at + side) * rows + i]
                        line = line + jnp.where(ok, ref[...], 0.0)
                    cat5[i * cols:(i + 1) * cols, part] = jnp.maximum(line, 0.0).astype(BF16)
            else:
                at = plan.direct.index(k)
                cat5[:, part] = cat_ref[:, at * c_out:(at + 1) * c_out]
        pool_act = jnp.maximum(pact[0:1, :], 0.0).astype(BF16)
        cat5[:, 4 * c_out:] = jnp.broadcast_to(pool_act, (pix, c_out))
        y_pre = nn(cat5[...], wproj_ref[...])
        y_act = jnp.maximum(y_pre, 0.0).astype(BF16)
        logits = nn(y_act, wcls_ref[...])
        lane = lax.broadcasted_iota(jnp.int32, (pix, 128), 1)
        live = lane < plan.classes
        expo = jnp.where(live, jnp.exp(logits), 0.0)
        prob = expo / jnp.sum(expo, axis=1, keepdims=True)
        names = aux_ref[3:4, :512].astype(F32)
        label = jnp.broadcast_to(names, (128, 512)).T[:pix]
        onehot = jnp.where(label == lane.astype(F32), 1.0, 0.0)
        weight = jnp.zeros((pix, 128), F32)
        for c in range(plan.classes):
            weight = jnp.where(label == float(c), cw_ref[c], weight)
        d_logits = jnp.where(
            live, (prob - onehot) * weight * (LOSS_SCALE / plan.total), 0.0
        ).astype(BF16)
        d_y = jnp.where(y_pre > 0, nt(d_logits, wcls_ref[...]), 0.0).astype(BF16)
        sdy[0:1, :] += jnp.sum(d_y.astype(F32), axis=0, keepdims=True)
        window = pl.ds(pl.multiple_of(tab[flags + n + 13], 128), plan.window)
        gpt[...] += nn(nt(identity(c_out), d_y).astype(BF16), cat5[:, window])
        gc[...] += nn(nt(identity(128), d_logits).astype(BF16), y_act)
        for k in range(4):
            want = [tab[flags + n + 3 * k + b] for b in range(3)]
            part = slice(k * c_out, (k + 1) * c_out)

            @pl.when((want[0] >= 0) | (want[1] >= 0) | (want[2] >= 0))
            def _(k=k, want=want, part=part):
                d_cat = nt(d_y, wproj_ref[part, :])
                d_k = jnp.where(cat5[:, part] > 0, d_cat, 0.0).astype(BF16)
                d_k = d_k.reshape(rows, cols, c_out)
                if k > 0:
                    pad[:, EDGE:EDGE + cols, :] = d_k.astype(F32)
                at = pl.ds(block * rows + edge_rows, rows)
                for b in range(3):
                    if k == 0 and b != 1:
                        continue

                    @pl.when(want[b] >= 0)
                    def _(b=b):
                        lanes = pl.ds(pl.multiple_of(jnp.maximum(want[b], 0) * c_out, c_out), c_out)
                        if b == 1:
                            dbuf[at, :, lanes] = d_k
                        else:
                            first = EDGE + (1 - b) * RATE * k
                            dbuf[at, :, lanes] = pad[:, first:first + cols, :].astype(BF16)

    @pl.when(step == n - 1)
    def _():
        pool = wproj_ref[4 * c_out:, :]
        rest = sdy[...]
        total = jnp.zeros(sdy.shape, F32)
        for _i in range(3):
            head = rest.astype(BF16)
            total = total + nt(head, pool)
            rest = rest - head.astype(F32)
        spool[...] = jnp.where(pact[...] > 0, jnp.broadcast_to(total[0:1, :], total.shape), 0.0)
        gp[:plan.window, :] = gpt[...].T
        index = tab[flags + n + 12]
        first = pl.multiple_of(index * plan.proj_rows - tab[flags + n + 13], 32)
        p_out[...] = finish(gp[pl.ds(first, plan.proj_rows), :], prev_p[...] if last else None)
        gp[:c_out, :128] = gc[...].T
        first = pl.multiple_of(index * plan.cls_rows, plan.cls_rows)
        c_ref_out[...] = finish(
            gp[pl.ds(first, plan.cls_rows), :128], prev_c[...] if last else None
        )

    def out_copy(part, slot, t):
        row = tab[(part * depth + t) * 6 + 5] * unit_rows
        return pltpu.make_async_copy(
            stage.at[slot, t],
            g_out.at[pl.ds(pl.multiple_of(row, unit_rows), unit_rows)],
            sems.at[slot, t],
        )

    @pl.when(step >= n)
    def _():
        part = step - n
        parity = lax.rem(part, 2)

        def one(t, _):
            base = (part * depth + t) * 6
            slot, move, low, high = tab[base], tab[base + 1], tab[base + 2], tab[base + 3]
            kind = tab[base + 4]

            def product(taps):
                width = taps * c_out
                lanes = pl.ds(pl.multiple_of(slot * c_out, c_out), width)

                def term(j):
                    first = j * rows - move + edge_rows
                    return nn(xt_ref[j], dbuf[pl.ds(first, rows), :, lanes].reshape(pix, width))

                whole = jnp.logical_and(low == 0, high == n)

                @pl.when(whole)
                def _():
                    total = term(0)
                    for j in range(1, n):
                        total = total + term(j)
                    acc[:, :width] = total

                @pl.when(jnp.logical_not(whole))
                def _():
                    acc[:, :width] = jnp.zeros((unit_rows, width), F32)

                    def add(j, _):
                        acc[:, :width] += term(j)
                        return 0

                    lax.fori_loop(low, high, add, 0)

            @pl.when(kind == 3)
            def _():
                product(3)

            @pl.when(kind == 0)
            def _():
                product(1)

            @pl.when(kind == 2)
            def _():
                acc[:, :c_out] = jnp.zeros((unit_rows, c_out), F32)

            @pl.when(kind == 1)
            def _():
                first = pl.multiple_of(part * unit_rows, unit_rows)
                row = mean[0:1, pl.ds(first, unit_rows)]
                column = jnp.broadcast_to(row, (128, unit_rows)).T
                for c in range(c_out // 128):
                    lanes = slice(c * 128, (c + 1) * 128)
                    acc[:, lanes] = column * spool[0:1, lanes]

            def emit(at, lanes):
                if last:
                    stage[parity, at] = finish(acc[:, lanes], prev_g[at])
                    out_copy(part, parity, at).start()
                else:
                    g_out[at] = finish(acc[:, lanes], None)

            @pl.when(kind != 4)
            def _():
                emit(t, slice(0, c_out))

            @pl.when(kind == 3)
            def _():
                for b in (1, 2):
                    emit(t + b, slice(b * c_out, (b + 1) * c_out))

            return 0

        lax.fori_loop(0, tab[flags + part], one, 0)

        if last:
            def drain(which, slot):
                def one(t, _):
                    out_copy(which, slot, t).wait()
                    return 0
                lax.fori_loop(0, tab[flags + which], one, 0)

            @pl.when(part > 0)
            def _():
                drain(part - 1, 1 - parity)

            @pl.when(part == n - 1)
            def _():
                drain(part, parity)


def run_field(plan, field, tab, state, w_in, w_proj, wcls, cw, prev):
    n, rows, cols, pix = plan.n, plan.rows, plan.cols, plan.pix
    c_in, c_out, n_sh = plan.c_in, plan.c_out, plan.n_sh
    unit_rows, depth = plan.unit_rows, plan.depth
    last = prev is not None
    xt, cat, s, aux = state

    def blk(i):
        return jnp.minimum(i, n - 1)

    def part(i):
        return jnp.maximum(i - n, 0)

    in_specs = [
        pl.BlockSpec(
            (None, None, pix, len(plan.direct) * c_out), lambda i, t: (field, blk(i), 0, 0)
        ),
    ]
    operands = [cat]
    for at in range(n_sh):
        in_specs.append(pl.BlockSpec(
            (None, None, rows, cols, c_out),
            lambda i, t, at=at: (3 * at + 1, field, blk(i), 0, 0),
        ))
        operands.append(s)
    for at, k in enumerate(plan.shifted):
        for side in range(2):
            move = (2 * side - 1) * RATE * k
            for row in range(rows):
                def index(i, t, at=at, side=side, move=move, row=row):
                    h = jnp.clip(blk(i) * rows + row + move, 0, plan.height - 1)
                    return (3 * at + 2 * side, field, h, 0, 0)
                in_specs.append(pl.BlockSpec((None, None, None, cols, c_out), index))
                operands.append(s)
    in_specs += [
        pl.BlockSpec((None, None, EXTRA, c_in), lambda i, t: (field, blk(i), 0, 0)),
        pl.BlockSpec((None, n, EXTRA, c_in), lambda i, t: (field, 0, 0, 0)),
        pl.BlockSpec((1, c_in, c_out), lambda i, t: (28, 0, 0)),
        pl.BlockSpec((5 * c_out, c_out), lambda i, t: (0, 0)),
        pl.BlockSpec((c_out, 128), lambda i, t: (0, 0)),
        pl.BlockSpec(memory_space=pltpu.SMEM),
        pl.BlockSpec((None, n, unit_rows, pix), lambda i, t: (field, 0, part(i), 0)),
    ]
    operands += [aux, aux, w_in, w_proj, wcls, cw, xt]
    kind = F32 if last else BF16
    inner = pl.BlockSpec((None, depth, unit_rows, c_out), lambda i, t: (part(i), 0, 0, 0))
    small = [
        pl.BlockSpec((plan.proj_rows, c_out), lambda i, t: (0, 0)),
        pl.BlockSpec((plan.cls_rows, 128), lambda i, t: (0, 0)),
    ]
    if last:
        in_specs += [inner] + small
        operands += list(prev)
        main_spec = pl.BlockSpec(memory_space=pl.ANY)
        main_shape = jax.ShapeDtypeStruct((plan.units * unit_rows, c_out), F32)
    else:
        main_spec = inner
        main_shape = jax.ShapeDtypeStruct((n, depth, unit_rows, c_out), BF16)
    return pl.pallas_call(
        functools.partial(field_kernel, plan, last),
        grid_spec=pltpu.PrefetchScalarGridSpec(
            num_scalar_prefetch=1,
            grid=(2 * n,),
            in_specs=in_specs,
            out_specs=[main_spec] + small,
            scratch_shapes=[
                pltpu.VMEM((plan.height + 2 * (rows - 1), cols, plan.n_slots * c_out), BF16),
                pltpu.VMEM((rows, cols + 2 * EDGE, c_out), F32),
                pltpu.VMEM((16, c_in), F32),
                pltpu.VMEM((c_out, plan.window), F32),
                pltpu.VMEM((max(plan.window, c_out), c_out), F32),
                pltpu.VMEM((128, c_out), F32),
                pltpu.VMEM((16, c_out), F32),
                pltpu.VMEM((16, c_out), F32),
                pltpu.VMEM((16, c_out), F32),
                pltpu.VMEM((pix, 5 * c_out), BF16),
                pltpu.VMEM((unit_rows, 3 * c_out), F32),
                pltpu.VMEM((2, depth if last else 1, unit_rows, c_out), F32),
                pltpu.SemaphoreType.DMA((2, depth)),
            ],
        ),
        out_shape=[
            main_shape,
            jax.ShapeDtypeStruct((plan.proj_rows, c_out), kind),
            jax.ShapeDtypeStruct((plan.cls_rows, 128), kind),
        ],
        compiler_params=pltpu.CompilerParams(
            dimension_semantics=("arbitrary",), vmem_limit_bytes=FIELD_VMEM
        ),
        cost_estimate=pl.CostEstimate(
            flops=10_000_000_000, bytes_accessed=90_000_000, transcendentals=0
        ),
        name="field_grads",
    )(tab, *operands)


def after(value, *others):
    return lax.optimization_barrier((value, *others))[0]


def per_device(plan, features, labels, w_in, w_proj, w_cls, class_weight, matching):
    n, reps, rows, pix, c_in = plan.n, plan.reps, plan.rows, plan.pix, plan.c_in
    names = jnp.pad(labels[0].reshape(1, pix).astype(F32), ((0, 0), (0, c_in - pix)))
    x = pl.pallas_call(
        functools.partial(pack_kernel, pix),
        out_shape=jax.ShapeDtypeStruct((pix + EXTRA, c_in), BF16),
        name="pack",
    )(features[0].reshape(pix, c_in), names)
    here = lax.axis_index("space")
    n_bits = reps.bit_length() - 1
    bits = [jnp.bitwise_and(jnp.right_shift(matching[0], b), 1) == 1 for b in range(n_bits)]
    top = jnp.int32(0)
    for at, b in enumerate(list(range(1, n_bits)) + [0]):
        top = jnp.where(bits[b], n_bits - 1 - at, top)
    tab = jnp.asarray(plan.tables)[here]
    wcls = jnp.pad(w_cls, ((0, 0), (0, 128 - plan.classes)))

    def along(value, way, step):
        pairs = [
            (i, i + way) for i in range(n)
            if 0 <= i + way < n and 0 <= i - way * (step - 1) < n
        ]
        return lax.ppermute(value, "space", pairs)

    def hop(value, b):
        return lax.ppermute(value, "rep", [(r, r ^ (1 << b)) for r in range(reps)])

    order = np.array(
        [sorted(range(n), key=lambda j: (abs(j - s), j)) for s in range(n)], np.int32
    )
    blocks = jnp.asarray(order)[here]

    def arrival(q, ups, downs):
        value = None
        for s in range(n):
            j = int(order[s, q])
            arrived = ups[s - j] if j < s else downs[j - s]
            value = arrived if value is None else jnp.where(here == s, arrived, value)
        return value

    common = (w_in, w_proj, wcls, class_weight)
    hops = list(range(1, n_bits)) + [0]
    rounds = n + n_bits - 1
    up = down = x
    ups, downs = [x], [x]
    values, moves = {0: x}, {q: [] for q in range(n)}
    state, grads = None, None
    for t in range(1, rounds + 1):
        q = t - 1
        if 0 < q < n:
            values[q] = arrival(q, ups, downs)
        for i in range(1, n_bits):
            if 0 <= q - i < n:
                values[q - i] = jnp.where(bits[hops[i - 1]], moves[q - i][0], values[q - i])
        if t < n:
            ups.append(along(ups[-1], 1, t))
            downs.append(along(downs[-1], -1, t))
        for i in range(n_bits):
            if 0 <= q - i < n:
                moves[q - i].insert(0, hop(values[q - i], hops[i]))
        slots = []
        if q < n:
            slots.append(([values[q]], (0, blocks[q], 0)))
        if t >= n_bits:
            at = t - n_bits
            slots.append((moves[at], (top, blocks[at], 1)))
        state = run_blocks(plan, slots, w_in, state)
        if q == min(n, rounds - 1):
            grads = tuple(run_field(plan, 0, tab, state, *common, None))
        if t < rounds:
            live = (ups, downs, values, moves, state, grads)
            ups, downs, values, moves, state, grads = lax.optimization_barrier(live)
    avg_in, avg_proj, avg_cls = run_field(plan, 1, tab, state, *common, grads)
    return avg_in[None], avg_proj[None], avg_cls[None, :, :plan.classes]


def solution(mesh):
    n, reps = mesh.shape["space"], mesh.shape["rep"]

    def build(features, labels, w_in, w_proj, w_cls, class_weight, matching):
        _, rows, cols, c_in = features.shape
        plan = Plan(n, reps, rows // n, cols, c_in, w_proj.shape[1], w_cls.shape[1])
        return jax.shard_map(
            functools.partial(per_device, plan),
            mesh=mesh,
            in_specs=(P("rep", "space", None, None), P("rep", "space", None), P(), P(), P(), P(), P()),
            out_specs=(P("rep", "space", None), P("rep", "space", None), P("rep", "space", None)),
            check_vma=False,
        )(features, labels, w_in, w_proj, w_cls, class_weight, matching)

    return build
```

```python
import functools

import jax
import jax.numpy as jnp
import numpy as np
from jax import lax
from jax.experimental import pallas as pl
from jax.experimental.pallas import tpu as pltpu
from jax.sharding import PartitionSpec as P

LOSS_SCALE = 1024.0
RATE = 12
EDGE = 40
EXTRA = 16
BF16 = jnp.bfloat16
F32 = jnp.float32
BLOCK_VMEM = 60 * 1024 * 1024
FIELD_VMEM = 60 * 1024 * 1024


def nn(a, b):
    return lax.dot_general(a, b, (((1,), (0,)), ((), ())), preferred_element_type=F32)


def nt(a, b):
    return lax.dot_general(a, b, (((1,), (1,)), ((), ())), preferred_element_type=F32)


def identity(size):
    rows = lax.broadcasted_iota(jnp.int32, (size, size), 0)
    cols = lax.broadcasted_iota(jnp.int32, (size, size), 1)
    return (rows == cols).astype(F32).astype(BF16)


class Plan:
    def __init__(self, n, reps, rows, cols, c_in, c_out, classes):
        self.n, self.reps, self.rows, self.cols = n, reps, rows, cols
        self.c_in, self.c_out, self.classes = c_in, c_out, classes
        self.height = rows * n
        self.pix = rows * cols
        self.total = self.pix * n
        self.shifted = [k for k in (1, 2, 3) if RATE * k < self.height]
        self.direct = [k for k in range(4) if k not in self.shifted]
        self.n_sh = len(self.shifted)
        self.loads = [0]
        for k in self.direct[1:]:
            self.loads += [1 + 9 * (k - 1) + 3 + b for b in range(3)]
        for k in self.shifted:
            self.loads += [1 + 9 * (k - 1) + i for i in range(9)]
        self.units = 29
        self.unit_rows = c_in // n
        self.proj_rows = 5 * c_out // n
        self.cls_rows = c_out // n
        starts = [self.proj_rows * s // 128 * 128 for s in range(n)]
        ends = [-(-self.proj_rows * (s + 1) // 128) * 128 for s in range(n)]
        self.window = max(e - b for b, e in zip(starts, ends))
        self.starts = [min(b, 5 * c_out - self.window) for b in starts]
        tables = [self.table(s) for s in range(n)]
        self.n_slots = max(t[1] for t in tables)
        self.depth = max(t[2] for t in tables)
        self.tables = np.array([
            sum((c + [[0] * 6] * (self.depth - len(c)) for c in t[0]), []) for t in tables
        ], np.int32).reshape(n, -1)
        self.flags = self.tables.shape[1]
        self.tables = np.concatenate([
            self.tables,
            np.array([
                [len(c) for c in t[0]] + t[3] + [s, self.starts[s]] for s, t in enumerate(tables)
            ], np.int32),
        ], axis=1)

    def tap(self, t):
        if t == 0:
            return (0, 1, 1)
        if t == 28:
            return None
        k, rest = (t - 1) // 9 + 1, (t - 1) % 9
        a, b = rest // 3, rest % 3
        if a != 1 and k not in self.shifted:
            return "zero"
        return (k, a, b)

    def table(self, s):
        parts = [[] for _ in range(self.n)]
        here = range(s * self.units, (s + 1) * self.units)
        slots = {}
        for k in range(4):
            for b in ((1,) if k == 0 else range(3)):
                if any(
                    isinstance(self.tap(u // self.n), tuple)
                    and (self.tap(u // self.n)[0], self.tap(u // self.n)[2]) == (k, b)
                    for u in here
                ):
                    slots[(k, b)] = len(slots)
        for unit in here:
            c, tap = unit % self.n, self.tap(unit // self.n)
            local = unit - s * self.units
            if tap is None or tap == "zero":
                parts[c].append([0, 0, 0, 0, 1 if tap is None else 2, local])
                continue
            k, a, b = tap
            move = (a - 1) * RATE * k
            valid = [
                j for j in range(self.n)
                if any(0 <= self.rows * j + i - move < self.height for i in range(self.rows))
            ]
            entry = [slots[(k, b)], move, valid[0], valid[-1] + 1, 0, local]
            if b == 2 and len(parts[c]) > 1 and all(
                e[4] == 0 and e[:4] == [entry[0] - back] + entry[1:4]
                for back, e in ((1, parts[c][-1]), (2, parts[c][-2]))
            ):
                parts[c][-2][4] = 3
                parts[c][-1][4] = 4
                entry[4] = 4
            parts[c].append(entry)
        want = [slots.get((k, b), -1) for k in range(4) for b in range(3)]
        return parts, len(slots), max(len(c) for c in parts), want


def pack_kernel(pix, x_ref, lab_ref, out_ref):
    x = x_ref[...]
    out_ref[:pix, :] = x
    total = jnp.sum(x.astype(F32), axis=0, keepdims=True)
    head = total.astype(BF16).astype(F32)
    mid = (total - head).astype(BF16).astype(F32)
    row = lax.broadcasted_iota(jnp.int32, (EXTRA, x.shape[1]), 0)
    extra = jnp.zeros((EXTRA, x.shape[1]), F32)
    for at, value in enumerate((head, mid, total - head - mid, lab_ref[...])):
        extra = jnp.where(row == at, value, extra)
    out_ref[pix:, :] = extra.astype(BF16)


def block_kernel(plan, n_cand, n_slots, aliased, meta, *refs):
    rows, cols, c_in, c_out = plan.rows, plan.cols, plan.c_in, plan.c_out
    pix = plan.pix
    cands = refs[:n_cand]
    w_hbm = refs[n_cand]
    refs = refs[n_cand + 1 + (4 if aliased else 0):]
    xt_out, cat_out, s_out, aux_out = refs[:4]
    xin, wbuf, xtb, catb, sb, left, right, sem_x, sem_w, sem_o, sem_s = refs[4:]
    step = pl.program_id(0)
    block, field = meta[step, 1], meta[step, 2]
    here = lax.rem(step, 2)
    xbuf = xin.at[here]

    def fetch(at, slot):
        for c in range(n_cand):
            @pl.when(meta[at, 0] == c)
            def _(c=c):
                pltpu.make_async_copy(cands[c], xin.at[slot], sem_x.at[slot]).start()

    def weights(at):
        return pltpu.make_async_copy(w_hbm.at[plan.loads[at]], wbuf.at[at], sem_w.at[at])

    def loaded(at, count):
        @pl.when(step == 0)
        def _():
            for i in range(count):
                weights(at + i).wait()

    @pl.when(step == 0)
    def _():
        fetch(0, 0)
        for at in range(len(plan.loads)):
            weights(at).start()
        zero = jnp.zeros((2, EDGE, c_out), F32)
        left[:, :EDGE, :] = zero
        right[:, EDGE + cols:, :] = zero

    if n_slots > 1:
        @pl.when(step + 1 < n_slots)
        def _():
            fetch(step + 1, 1 - here)

    pltpu.make_async_copy(cands[0], xbuf, sem_x.at[here]).wait()
    aux_copy = pltpu.make_async_copy(
        xbuf.at[pl.ds(pix, EXTRA)], aux_out.at[field, block], sem_o.at[2]
    )
    aux_copy.start()
    eye = identity(256)
    for c in range(c_in // 256):
        part = slice(c * 256, (c + 1) * 256)
        xtb[part, :] = nt(eye, xbuf[:pix, part]).astype(BF16)
    xt_copy = pltpu.make_async_copy(xtb, xt_out.at[field, block], sem_o.at[0])
    xt_copy.start()

    def in_field(move):
        first = block * rows + move
        return jnp.logical_and(first + rows - 1 >= 0, first < plan.height)

    def line(k, m, at):
        r = RATE * k
        width = -(-(cols - r) // 16) * 16
        low = r // 16 * 16
        first = m * cols
        mid = nn(xbuf[first:first + cols, :], wbuf[at + 1])
        left[m % 2, EDGE:EDGE + width, :] = nn(xbuf[first:first + width, :], wbuf[at])
        right[m % 2, EDGE + low:EDGE + cols, :] = nn(
            xbuf[first + low:first + cols, :], wbuf[at + 2]
        )
        return (
            mid + left[m % 2, EDGE - r:EDGE - r + cols, :]
            + right[m % 2, EDGE + r:EDGE + r + cols, :]
        )

    def shifted_copy(at):
        return pltpu.make_async_copy(
            sb.at[at], s_out.at[at, field, pl.ds(block * rows, rows)], sem_s.at[at]
        )

    loaded(0, 1)
    for m in range(rows):
        part = slice(m * cols, (m + 1) * cols)
        catb[part, :c_out] = jnp.maximum(nn(xbuf[part, :], wbuf[0]), 0.0).astype(BF16)
    at = 1
    for i, k in enumerate(plan.direct[1:]):
        loaded(at, 3)
        for m in range(rows):
            catb[m * cols:(m + 1) * cols, (1 + i) * c_out:(2 + i) * c_out] = jnp.maximum(
                line(k, m, at), 0.0
            ).astype(BF16)
        at += 3
    cat_copy = pltpu.make_async_copy(catb, cat_out.at[field, block], sem_o.at[1])
    cat_copy.start()
    for i, k in enumerate(plan.shifted):
        loaded(at, 9)

        def one(a, _, k=k, i=i, at=at):
            @pl.when(in_field((1 - a) * RATE * k))
            def _():
                for m in range(rows):
                    sb[3 * i + a, m] = line(k, m, at + 3 * a)
                shifted_copy(3 * i + a).start()
            return 0

        lax.fori_loop(0, 3, one, 0)
        at += 9
    aux_copy.wait()
    xt_copy.wait()
    cat_copy.wait()
    for i, k in enumerate(plan.shifted):
        for a in range(3):
            @pl.when(in_field((1 - a) * RATE * k))
            def _(i=i, a=a):
                shifted_copy(3 * i + a).wait()


def run_blocks(plan, slots, meta, w_in, state):
    arrays = [value for cands in slots for value in cands]
    n, rows, cols, pix = plan.n, plan.rows, plan.cols, plan.pix
    c_in, c_out, n_sh = plan.c_in, plan.c_out, plan.n_sh
    shapes = [
        jax.ShapeDtypeStruct((2, n, c_in, pix), BF16),
        jax.ShapeDtypeStruct((2, n, pix, len(plan.direct) * c_out), BF16),
        jax.ShapeDtypeStruct((3 * n_sh, 2, n * rows, cols, c_out), F32),
        jax.ShapeDtypeStruct((2, n, EXTRA, c_in), BF16),
    ]
    aliased = state is not None
    operands = [*arrays, w_in] + (list(state) if aliased else [])
    aliases = {1 + len(arrays) + 1 + i: i for i in range(4)} if aliased else {}
    return pl.pallas_call(
        functools.partial(block_kernel, plan, len(arrays), len(slots), aliased),
        grid_spec=pltpu.PrefetchScalarGridSpec(
            num_scalar_prefetch=1,
            grid=(len(slots),),
            in_specs=[pl.BlockSpec(memory_space=pl.ANY)] * len(operands),
            out_specs=[pl.BlockSpec(memory_space=pl.ANY)] * 4,
            scratch_shapes=[
                pltpu.VMEM((2, pix + EXTRA, c_in), BF16),
                pltpu.VMEM((len(plan.loads), c_in, c_out), BF16),
                pltpu.VMEM((c_in, pix), BF16),
                pltpu.VMEM((pix, len(plan.direct) * c_out), BF16),
                pltpu.VMEM((3 * n_sh, rows, cols, c_out), F32),
                pltpu.VMEM((2, cols + 2 * EDGE, c_out), F32),
                pltpu.VMEM((2, cols + 2 * EDGE, c_out), F32),
                pltpu.SemaphoreType.DMA((2,)),
                pltpu.SemaphoreType.DMA((len(plan.loads),)),
                pltpu.SemaphoreType.DMA((3,)),
                pltpu.SemaphoreType.DMA((3 * n_sh,)),
            ],
        ),
        out_shape=shapes,
        input_output_aliases=aliases,
        compiler_params=pltpu.CompilerParams(
            dimension_semantics=("arbitrary",), vmem_limit_bytes=BLOCK_VMEM
        ),
        cost_estimate=pl.CostEstimate(
            flops=len(slots) * 2 * pix * c_in * c_out * (10 + 6 * n_sh),
            bytes_accessed=20_000_000 + len(slots) * 20_000_000,
            transcendentals=0,
        ),
        name="block_forward",
    )(meta, *operands)


def field_kernel(plan, last, tab, *refs):
    n, rows, cols, pix = plan.n, plan.rows, plan.cols, plan.pix
    c_in, c_out, n_sh = plan.c_in, plan.c_out, plan.n_sh
    n_rows_in = 2 * n_sh * rows
    unit_rows, depth, flags = plan.unit_rows, plan.depth, plan.flags
    cat_ref = refs[0]
    mid_refs = refs[1:1 + n_sh]
    s_refs = refs[1 + n_sh:1 + n_sh + n_rows_in]
    refs = refs[1 + n_sh + n_rows_in:]
    aux_ref, all_ref, w28_ref, wproj_ref, wcls_ref, cw_ref, xt_ref = refs[:7]
    refs = refs[7:]
    if last:
        prev_g, prev_p, prev_c = refs[:3]
        refs = refs[3:]
    g_out, p_out, c_ref_out = refs[:3]
    dbuf, pad, mean, gpt, gp, gc, sdy, spool, pact, cat5, acc, stage, sems = refs[3:]
    step = pl.program_id(0)
    edge_rows = rows - 1

    def finish(value, prev):
        grad = value.astype(BF16)
        if not last:
            return grad
        return (prev.astype(F32) + grad.astype(F32)) * 0.5

    @pl.when(step == 0)
    def _():
        zero = jnp.zeros((edge_rows, cols, dbuf.shape[2]), BF16)
        dbuf[:edge_rows] = zero
        dbuf[edge_rows + plan.height:] = zero
        pad[:, :EDGE, :] = jnp.zeros((rows, EDGE, c_out), F32)
        pad[:, EDGE + cols:, :] = jnp.zeros((rows, EDGE, c_out), F32)
        gpt[...] = jnp.zeros_like(gpt)
        gc[...] = jnp.zeros_like(gc)
        sdy[...] = jnp.zeros_like(sdy)
        total = jnp.zeros((1, c_in), F32)
        for j in range(n):
            extra = all_ref[j].astype(F32)
            total = total + ((extra[2:3] + extra[1:2]) + extra[0:1])
        mean_in = (total / plan.total).astype(BF16)
        mean[...] = jnp.broadcast_to(mean_in.astype(F32), (16, c_in))
        pact[...] = nn(mean[...].astype(BF16), w28_ref[0])

    @pl.when(step < n)
    def _():
        block = step
        for k in range(4):
            part = slice(k * c_out, (k + 1) * c_out)
            if k in plan.shifted:
                at = plan.shifted.index(k)
                r = RATE * k
                pre = mid_refs[at]
                for i in range(rows):
                    h = block * rows + i
                    line = pre[i]
                    for side, src in ((0, h - r), (1, h + r)):
                        ok = jnp.logical_and(src >= 0, src < plan.height)
                        ref = s_refs[(2 * at + side) * rows + i]
                        line = line + jnp.where(ok, ref[...], 0.0)
                    cat5[i * cols:(i + 1) * cols, part] = jnp.maximum(line, 0.0).astype(BF16)
            else:
                at = plan.direct.index(k)
                cat5[:, part] = cat_ref[:, at * c_out:(at + 1) * c_out]
        pool_act = jnp.maximum(pact[0:1, :], 0.0).astype(BF16)
        cat5[:, 4 * c_out:] = jnp.broadcast_to(pool_act, (pix, c_out))
        y_pre = nn(cat5[...], wproj_ref[...])
        y_act = jnp.maximum(y_pre, 0.0).astype(BF16)
        logits = nn(y_act, wcls_ref[...])
        lane = lax.broadcasted_iota(jnp.int32, (pix, 128), 1)
        live = lane < plan.classes
        expo = jnp.where(live, jnp.exp(logits), 0.0)
        prob = expo / jnp.sum(expo, axis=1, keepdims=True)
        names = aux_ref[3:4, :512].astype(F32)
        label = jnp.broadcast_to(names, (128, 512)).T[:pix]
        onehot = jnp.where(label == lane.astype(F32), 1.0, 0.0)
        weight = jnp.zeros((pix, 128), F32)
        for c in range(plan.classes):
            weight = jnp.where(label == float(c), cw_ref[c], weight)
        d_logits = jnp.where(
            live, (prob - onehot) * weight * (LOSS_SCALE / plan.total), 0.0
        ).astype(BF16)
        d_y = jnp.where(y_pre > 0, nt(d_logits, wcls_ref[...]), 0.0).astype(BF16)
        sdy[0:1, :] += jnp.sum(d_y.astype(F32), axis=0, keepdims=True)
        window = pl.ds(pl.multiple_of(tab[flags + n + 13], 128), plan.window)
        gpt[...] += nn(nt(identity(c_out), d_y).astype(BF16), cat5[:, window])
        gc[...] += nn(nt(identity(128), d_logits).astype(BF16), y_act)
        for k in range(4):
            want = [tab[flags + n + 3 * k + b] for b in range(3)]
            part = slice(k * c_out, (k + 1) * c_out)

            @pl.when((want[0] >= 0) | (want[1] >= 0) | (want[2] >= 0))
            def _(k=k, want=want, part=part):
                d_cat = nt(d_y, wproj_ref[part, :])
                d_k = jnp.where(cat5[:, part] > 0, d_cat, 0.0).astype(BF16)
                d_k = d_k.reshape(rows, cols, c_out)
                if k > 0:
                    pad[:, EDGE:EDGE + cols, :] = d_k.astype(F32)
                at = pl.ds(block * rows + edge_rows, rows)
                for b in range(3):
                    if k == 0 and b != 1:
                        continue

                    @pl.when(want[b] >= 0)
                    def _(b=b):
                        lanes = pl.ds(pl.multiple_of(jnp.maximum(want[b], 0) * c_out, c_out), c_out)
                        if b == 1:
                            dbuf[at, :, lanes] = d_k
                        else:
                            first = EDGE + (1 - b) * RATE * k
                            dbuf[at, :, lanes] = pad[:, first:first + cols, :].astype(BF16)

    @pl.when(step == n - 1)
    def _():
        pool = wproj_ref[4 * c_out:, :]
        rest = sdy[...]
        total = jnp.zeros(sdy.shape, F32)
        for _i in range(3):
            head = rest.astype(BF16)
            total = total + nt(head, pool)
            rest = rest - head.astype(F32)
        spool[...] = jnp.where(pact[...] > 0, jnp.broadcast_to(total[0:1, :], total.shape), 0.0)
        gp[:plan.window, :] = gpt[...].T
        index = tab[flags + n + 12]
        first = pl.multiple_of(index * plan.proj_rows - tab[flags + n + 13], 32)
        p_out[...] = finish(gp[pl.ds(first, plan.proj_rows), :], prev_p[...] if last else None)
        gp[:c_out, :128] = gc[...].T
        first = pl.multiple_of(index * plan.cls_rows, plan.cls_rows)
        c_ref_out[...] = finish(
            gp[pl.ds(first, plan.cls_rows), :128], prev_c[...] if last else None
        )

    def out_copy(part, slot, t):
        row = tab[(part * depth + t) * 6 + 5] * unit_rows
        return pltpu.make_async_copy(
            stage.at[slot, t],
            g_out.at[pl.ds(pl.multiple_of(row, unit_rows), unit_rows)],
            sems.at[slot, t],
        )

    @pl.when(step >= n)
    def _():
        part = step - n
        parity = lax.rem(part, 2)

        def one(t, _):
            base = (part * depth + t) * 6
            slot, move, low, high = tab[base], tab[base + 1], tab[base + 2], tab[base + 3]
            kind = tab[base + 4]

            def product(taps):
                width = taps * c_out
                lanes = pl.ds(pl.multiple_of(slot * c_out, c_out), width)

                def term(j):
                    first = j * rows - move + edge_rows
                    return nn(xt_ref[j], dbuf[pl.ds(first, rows), :, lanes].reshape(pix, width))

                whole = jnp.logical_and(low == 0, high == n)

                @pl.when(whole)
                def _():
                    total = term(0)
                    for j in range(1, n):
                        total = total + term(j)
                    acc[:, :width] = total

                @pl.when(jnp.logical_not(whole))
                def _():
                    acc[:, :width] = jnp.zeros((unit_rows, width), F32)

                    def add(j, _):
                        acc[:, :width] += term(j)
                        return 0

                    lax.fori_loop(low, high, add, 0)

            @pl.when(kind == 3)
            def _():
                product(3)

            @pl.when(kind == 0)
            def _():
                product(1)

            @pl.when(kind == 2)
            def _():
                acc[:, :c_out] = jnp.zeros((unit_rows, c_out), F32)

            @pl.when(kind == 1)
            def _():
                first = pl.multiple_of(part * unit_rows, unit_rows)
                row = mean[0:1, pl.ds(first, unit_rows)]
                column = jnp.broadcast_to(row, (128, unit_rows)).T
                for c in range(c_out // 128):
                    lanes = slice(c * 128, (c + 1) * 128)
                    acc[:, lanes] = column * spool[0:1, lanes]

            def emit(at, lanes):
                if last:
                    stage[parity, at] = finish(acc[:, lanes], prev_g[at])
                    out_copy(part, parity, at).start()
                else:
                    g_out[at] = finish(acc[:, lanes], None)

            @pl.when(kind != 4)
            def _():
                emit(t, slice(0, c_out))

            @pl.when(kind == 3)
            def _():
                for b in (1, 2):
                    emit(t + b, slice(b * c_out, (b + 1) * c_out))

            return 0

        lax.fori_loop(0, tab[flags + part], one, 0)

        if last:
            def drain(which, slot):
                def one(t, _):
                    out_copy(which, slot, t).wait()
                    return 0
                lax.fori_loop(0, tab[flags + which], one, 0)

            @pl.when(part > 0)
            def _():
                drain(part - 1, 1 - parity)

            @pl.when(part == n - 1)
            def _():
                drain(part, parity)


def run_field(plan, field, tab, state, w_in, w_proj, wcls, cw, prev):
    n, rows, cols, pix = plan.n, plan.rows, plan.cols, plan.pix
    c_in, c_out, n_sh = plan.c_in, plan.c_out, plan.n_sh
    unit_rows, depth = plan.unit_rows, plan.depth
    last = prev is not None
    xt, cat, s, aux = state

    def blk(i):
        return jnp.minimum(i, n - 1)

    def part(i):
        return jnp.maximum(i - n, 0)

    in_specs = [
        pl.BlockSpec(
            (None, None, pix, len(plan.direct) * c_out), lambda i, t: (field, blk(i), 0, 0)
        ),
    ]
    operands = [cat]
    for at in range(n_sh):
        in_specs.append(pl.BlockSpec(
            (None, None, rows, cols, c_out),
            lambda i, t, at=at: (3 * at + 1, field, blk(i), 0, 0),
        ))
        operands.append(s)
    for at, k in enumerate(plan.shifted):
        for side in range(2):
            move = (2 * side - 1) * RATE * k
            for row in range(rows):
                def index(i, t, at=at, side=side, move=move, row=row):
                    h = jnp.clip(blk(i) * rows + row + move, 0, plan.height - 1)
                    return (3 * at + 2 * side, field, h, 0, 0)
                in_specs.append(pl.BlockSpec((None, None, None, cols, c_out), index))
                operands.append(s)
    in_specs += [
        pl.BlockSpec((None, None, EXTRA, c_in), lambda i, t: (field, blk(i), 0, 0)),
        pl.BlockSpec((None, n, EXTRA, c_in), lambda i, t: (field, 0, 0, 0)),
        pl.BlockSpec((1, c_in, c_out), lambda i, t: (28, 0, 0)),
        pl.BlockSpec((5 * c_out, c_out), lambda i, t: (0, 0)),
        pl.BlockSpec((c_out, 128), lambda i, t: (0, 0)),
        pl.BlockSpec(memory_space=pltpu.SMEM),
        pl.BlockSpec((None, n, unit_rows, pix), lambda i, t: (field, 0, part(i), 0)),
    ]
    operands += [aux, aux, w_in, w_proj, wcls, cw, xt]
    kind = F32 if last else BF16
    inner = pl.BlockSpec((None, depth, unit_rows, c_out), lambda i, t: (part(i), 0, 0, 0))
    small = [
        pl.BlockSpec((plan.proj_rows, c_out), lambda i, t: (0, 0)),
        pl.BlockSpec((plan.cls_rows, 128), lambda i, t: (0, 0)),
    ]
    if last:
        in_specs += [inner] + small
        operands += list(prev)
        main_spec = pl.BlockSpec(memory_space=pl.ANY)
        main_shape = jax.ShapeDtypeStruct((plan.units * unit_rows, c_out), F32)
    else:
        main_spec = inner
        main_shape = jax.ShapeDtypeStruct((n, depth, unit_rows, c_out), BF16)
    return pl.pallas_call(
        functools.partial(field_kernel, plan, last),
        grid_spec=pltpu.PrefetchScalarGridSpec(
            num_scalar_prefetch=1,
            grid=(2 * n,),
            in_specs=in_specs,
            out_specs=[main_spec] + small,
            scratch_shapes=[
                pltpu.VMEM((plan.height + 2 * (rows - 1), cols, plan.n_slots * c_out), BF16),
                pltpu.VMEM((rows, cols + 2 * EDGE, c_out), F32),
                pltpu.VMEM((16, c_in), F32),
                pltpu.VMEM((c_out, plan.window), F32),
                pltpu.VMEM((max(plan.window, c_out), c_out), F32),
                pltpu.VMEM((128, c_out), F32),
                pltpu.VMEM((16, c_out), F32),
                pltpu.VMEM((16, c_out), F32),
                pltpu.VMEM((16, c_out), F32),
                pltpu.VMEM((pix, 5 * c_out), BF16),
                pltpu.VMEM((unit_rows, 3 * c_out), F32),
                pltpu.VMEM((2, depth if last else 1, unit_rows, c_out), F32),
                pltpu.SemaphoreType.DMA((2, depth)),
            ],
        ),
        out_shape=[
            main_shape,
            jax.ShapeDtypeStruct((plan.proj_rows, c_out), kind),
            jax.ShapeDtypeStruct((plan.cls_rows, 128), kind),
        ],
        compiler_params=pltpu.CompilerParams(
            dimension_semantics=("arbitrary",), vmem_limit_bytes=FIELD_VMEM
        ),
        cost_estimate=pl.CostEstimate(
            flops=10_000_000_000, bytes_accessed=90_000_000, transcendentals=0
        ),
        name="field_grads",
    )(tab, *operands)


def after(value, *others):
    return lax.optimization_barrier((value, *others))[0]


def per_device(plan, features, labels, w_in, w_proj, w_cls, class_weight, matching):
    n, reps, rows, pix, c_in = plan.n, plan.reps, plan.rows, plan.pix, plan.c_in
    names = jnp.pad(labels[0].reshape(1, pix).astype(F32), ((0, 0), (0, c_in - pix)))
    x = pl.pallas_call(
        functools.partial(pack_kernel, pix),
        out_shape=jax.ShapeDtypeStruct((pix + EXTRA, c_in), BF16),
        name="pack",
    )(features[0].reshape(pix, c_in), names)
    here = lax.axis_index("space")
    n_bits = reps.bit_length() - 1
    bits = [jnp.bitwise_and(jnp.right_shift(matching[0], b), 1) == 1 for b in range(n_bits)]
    top = jnp.int32(0)
    for at, b in enumerate(list(range(1, n_bits)) + [0]):
        top = jnp.where(bits[b], n_bits - 1 - at, top)
    tab = jnp.asarray(plan.tables)[here]
    wcls = jnp.pad(w_cls, ((0, 0), (0, 128 - plan.classes)))

    def along(value, way, step):
        pairs = [
            (i, i + way) for i in range(n)
            if 0 <= i + way < n and 0 <= i - way * (step - 1) < n
        ]
        return lax.ppermute(value, "space", pairs)

    def hop(value, b):
        return lax.ppermute(value, "rep", [(r, r ^ (1 << b)) for r in range(reps)])

    order = np.array(
        [sorted(range(n), key=lambda j: (abs(j - s), j)) for s in range(n)], np.int32
    )
    blocks = jnp.asarray(order)[here]

    def arrival(q, ups, downs):
        value = None
        for s in range(n):
            j = int(order[s, q])
            arrived = ups[s - j] if j < s else downs[j - s]
            value = arrived if value is None else jnp.where(here == s, arrived, value)
        return value

    common = (w_in, w_proj, wcls, class_weight)
    hops = list(range(1, n_bits)) + [0]
    rounds = n + n_bits - 1
    ups, downs = [x], [x]
    metas = []
    for t in range(1, rounds + 1):
        meta = []
        if t - 1 < n:
            meta.append((jnp.int32(0), blocks[t - 1], jnp.int32(0)))
        if t >= n_bits:
            meta.append((top + len(meta), blocks[t - n_bits], jnp.int32(1)))
        metas.append(jnp.stack([jnp.stack(row) for row in meta]))
    values, moves = {0: x}, {q: [] for q in range(n)}
    state, grads = None, None
    for t in range(1, rounds + 1):
        q = t - 1
        if 0 < q < n:
            values[q] = arrival(q, ups, downs)
        for i in range(1, n_bits):
            if 0 <= q - i < n:
                values[q - i] = jnp.where(bits[hops[i - 1]], moves[q - i][0], values[q - i])
        if t < n:
            ups.append(along(ups[-1], 1, t))
            downs.append(along(downs[-1], -1, t))
        for i in range(n_bits):
            if 0 <= q - i < n:
                moves[q - i].insert(0, hop(values[q - i], hops[i]))
        slots = []
        if q < n:
            slots.append([values[q]])
        if t >= n_bits:
            slots.append(moves[t - n_bits])
        state = run_blocks(plan, slots, metas[q], w_in, state)
        if q == min(n, rounds - 1):
            grads = tuple(run_field(plan, 0, tab, state, *common, None))
        if t < rounds:
            live = (ups, downs, values, moves, state, grads, metas, tab, wcls)
            live = lax.optimization_barrier(live)
            ups, downs, values, moves, state, grads, metas, tab, wcls = live
    avg_in, avg_proj, avg_cls = run_field(plan, 1, tab, state, *common, grads)
    return avg_in[None], avg_proj[None], avg_cls[None, :, :plan.classes]


def solution(mesh):
    n, reps = mesh.shape["space"], mesh.shape["rep"]

    def build(features, labels, w_in, w_proj, w_cls, class_weight, matching):
        _, rows, cols, c_in = features.shape
        plan = Plan(n, reps, rows // n, cols, c_in, w_proj.shape[1], w_cls.shape[1])
        return jax.shard_map(
            functools.partial(per_device, plan),
            mesh=mesh,
            in_specs=(P("rep", "space", None, None), P("rep", "space", None), P(), P(), P(), P(), P()),
            out_specs=(P("rep", "space", None), P("rep", "space", None), P("rep", "space", None)),
            check_vma=False,
        )(features, labels, w_in, w_proj, w_cls, class_weight, matching)

    return build
```

```python
import functools

import jax
import jax.numpy as jnp
import numpy as np
from jax import lax
from jax.experimental import pallas as pl
from jax.experimental.pallas import tpu as pltpu
from jax.sharding import PartitionSpec as P

LOSS_SCALE = 1024.0
RATE = 12
EDGE = 40
EXTRA = 16
BF16 = jnp.bfloat16
F32 = jnp.float32
BLOCK_VMEM = 60 * 1024 * 1024
FIELD_VMEM = 60 * 1024 * 1024


def nn(a, b):
    return lax.dot_general(a, b, (((1,), (0,)), ((), ())), preferred_element_type=F32)


def nt(a, b):
    return lax.dot_general(a, b, (((1,), (1,)), ((), ())), preferred_element_type=F32)


def identity(size):
    rows = lax.broadcasted_iota(jnp.int32, (size, size), 0)
    cols = lax.broadcasted_iota(jnp.int32, (size, size), 1)
    return (rows == cols).astype(F32).astype(BF16)


class Plan:
    def __init__(self, n, reps, rows, cols, c_in, c_out, classes):
        self.n, self.reps, self.rows, self.cols = n, reps, rows, cols
        self.c_in, self.c_out, self.classes = c_in, c_out, classes
        self.height = rows * n
        self.pix = rows * cols
        self.total = self.pix * n
        self.shifted = [k for k in (1, 2, 3) if RATE * k < self.height]
        self.direct = [k for k in range(4) if k not in self.shifted]
        self.n_sh = len(self.shifted)
        row = lambda k, a: [1 + 9 * (k - 1) + 3 * a + b for b in range(3)]
        still = [row(k, 1) for k in self.direct[1:]]
        self.loads = [[0] + (still[0] if still else [])] + still[1:]
        for k in self.shifted:
            self.loads += [row(k, a) for a in range(3)]
        self.units = 29
        self.unit_rows = c_in // n
        self.proj_rows = 5 * c_out // n
        self.cls_rows = c_out // n
        starts = [self.proj_rows * s // 128 * 128 for s in range(n)]
        ends = [-(-self.proj_rows * (s + 1) // 128) * 128 for s in range(n)]
        self.window = max(e - b for b, e in zip(starts, ends))
        self.starts = [min(b, 5 * c_out - self.window) for b in starts]
        tables = [self.table(s) for s in range(n)]
        self.n_slots = max(t[1] for t in tables)
        self.depth = max(t[2] for t in tables)
        self.tables = np.array([
            sum((c + [[0] * 6] * (self.depth - len(c)) for c in t[0]), []) for t in tables
        ], np.int32).reshape(n, -1)
        self.flags = self.tables.shape[1]
        self.tables = np.concatenate([
            self.tables,
            np.array([
                [len(c) for c in t[0]] + t[3] + [s, self.starts[s]] for s, t in enumerate(tables)
            ], np.int32),
        ], axis=1)

    def tap(self, t):
        if t == 0:
            return (0, 1, 1)
        if t == 28:
            return None
        k, rest = (t - 1) // 9 + 1, (t - 1) % 9
        a, b = rest // 3, rest % 3
        if a != 1 and k not in self.shifted:
            return "zero"
        return (k, a, b)

    def table(self, s):
        parts = [[] for _ in range(self.n)]
        here = range(s * self.units, (s + 1) * self.units)
        slots = {}
        for k in range(4):
            for b in ((1,) if k == 0 else range(3)):
                if any(
                    isinstance(self.tap(u // self.n), tuple)
                    and (self.tap(u // self.n)[0], self.tap(u // self.n)[2]) == (k, b)
                    for u in here
                ):
                    slots[(k, b)] = len(slots)
        for unit in here:
            c, tap = unit % self.n, self.tap(unit // self.n)
            local = unit - s * self.units
            if tap is None or tap == "zero":
                parts[c].append([0, 0, 0, 0, 1 if tap is None else 2, local])
                continue
            k, a, b = tap
            move = (a - 1) * RATE * k
            valid = [
                j for j in range(self.n)
                if any(0 <= self.rows * j + i - move < self.height for i in range(self.rows))
            ]
            entry = [slots[(k, b)], move, valid[0], valid[-1] + 1, 0, local]
            if b == 2 and len(parts[c]) > 1 and all(
                e[4] == 0 and e[:4] == [entry[0] - back] + entry[1:4]
                for back, e in ((1, parts[c][-1]), (2, parts[c][-2]))
            ):
                parts[c][-2][4] = 3
                parts[c][-1][4] = 4
                entry[4] = 4
            parts[c].append(entry)
        want = [slots.get((k, b), -1) for k in range(4) for b in range(3)]
        return parts, len(slots), max(len(c) for c in parts), want


def pack_kernel(pix, x_ref, lab_ref, out_ref):
    x = x_ref[...]
    out_ref[:pix, :] = x
    total = jnp.sum(x.astype(F32), axis=0, keepdims=True)
    head = total.astype(BF16).astype(F32)
    mid = (total - head).astype(BF16).astype(F32)
    row = lax.broadcasted_iota(jnp.int32, (EXTRA, x.shape[1]), 0)
    extra = jnp.zeros((EXTRA, x.shape[1]), F32)
    for at, value in enumerate((head, mid, total - head - mid, lab_ref[...])):
        extra = jnp.where(row == at, value, extra)
    out_ref[pix:, :] = extra.astype(BF16)


def block_kernel(plan, n_cand, n_slots, aliased, meta, *refs):
    rows, cols, c_in, c_out = plan.rows, plan.cols, plan.c_in, plan.c_out
    pix = plan.pix
    cands = refs[:n_cand]
    w_hbm = refs[n_cand]
    refs = refs[n_cand + 1 + (4 if aliased else 0):]
    xt_out, cat_out, s_out, aux_out = refs[:4]
    xin, wbuf, xtb, catb, sb, res, sem_x, sem_w, sem_o, sem_s = refs[4:]
    step = pl.program_id(0)
    block, field = meta[step, 1], meta[step, 2]
    now = lax.rem(step, 2)
    xbuf = xin.at[now, pl.ds(0, pix)]

    def fetch(at, slot):
        for c in range(n_cand):
            @pl.when(meta[at, 0] == c)
            def _(c=c):
                pltpu.make_async_copy(cands[c], xin.at[slot], sem_x.at[slot]).start()

    def weights(group, taps):
        return [
            pltpu.make_async_copy(
                w_hbm.at[tap], wbuf.at[group, :, pl.ds(i * c_out, c_out)], sem_w.at[group, i]
            )
            for i, tap in enumerate(taps)
        ]

    @pl.when(step == 0)
    def _():
        fetch(0, 0)
        for group, taps in enumerate(plan.loads):
            for copy in weights(group, taps):
                copy.start()
        res[:, :EDGE, :] = jnp.zeros((rows, EDGE, res.shape[2]), F32)
        res[:, EDGE + cols:, :] = jnp.zeros((rows, EDGE, res.shape[2]), F32)

    if n_slots > 1:
        @pl.when(step + 1 < n_slots)
        def _():
            fetch(step + 1, 1 - now)

    pltpu.make_async_copy(cands[0], xin.at[now], sem_x.at[now]).wait()
    aux_copy = pltpu.make_async_copy(
        xin.at[now, pl.ds(pix, EXTRA)], aux_out.at[field, block], sem_o.at[2]
    )
    aux_copy.start()
    eye = identity(256)
    for c in range(c_in // 256):
        part = slice(c * 256, (c + 1) * 256)
        xtb[part, :] = nt(eye, xbuf[:, part]).astype(BF16)
    xt_copy = pltpu.make_async_copy(xtb, xt_out.at[field, block], sem_o.at[0])
    xt_copy.start()

    def in_field(move):
        first = block * rows + move
        return jnp.logical_and(first + rows - 1 >= 0, first < plan.height)

    def loaded(group, taps):
        @pl.when(step == 0)
        def _():
            for copy in weights(group, taps):
                copy.wait()

    def columns(k, first):
        r = RATE * k
        part = [slice(first + i * c_out, first + (i + 1) * c_out) for i in range(3)]
        return (
            res[:, EDGE - r:EDGE - r + cols, part[0]]
            + res[:, EDGE:EDGE + cols, part[1]]
            + res[:, EDGE + r:EDGE + r + cols, part[2]]
        )

    def relu_to(k, value):
        at = plan.direct.index(k)
        catb[:, at * c_out:(at + 1) * c_out] = (
            jnp.maximum(value, 0.0).astype(BF16).reshape(pix, c_out)
        )

    def shifted_copy(at):
        return pltpu.make_async_copy(
            sb.at[at], s_out.at[at, field, pl.ds(block * rows, rows)], sem_s.at[at]
        )

    group = 0
    first = c_out
    loaded(0, plan.loads[0])
    width = len(plan.loads[0]) * c_out
    res[:, EDGE:EDGE + cols, :width] = nn(xbuf[...], wbuf[0, :, :width]).reshape(
        rows, cols, width
    )
    relu_to(0, res[:, EDGE:EDGE + cols, :c_out])
    group = 1
    for k in plan.direct[1:]:
        if first + 3 * c_out > width:
            loaded(group, plan.loads[group])
            width, first = 3 * c_out, 0
            res[:, EDGE:EDGE + cols, :width] = nn(xbuf[...], wbuf[group, :, :width]).reshape(
                rows, cols, width
            )
            group += 1
        relu_to(k, columns(k, first))
        first += 3 * c_out
    cat_copy = pltpu.make_async_copy(catb, cat_out.at[field, block], sem_o.at[1])
    cat_copy.start()
    width = 3 * c_out
    for at, k in enumerate(plan.shifted):
        for a in range(3):
            loaded(group + 3 * at + a, plan.loads[group + 3 * at + a])

        def one(a, _, k=k, at=at, base=group + 3 * at):
            @pl.when(in_field((1 - a) * RATE * k))
            def _():
                res[:, EDGE:EDGE + cols, :width] = nn(
                    xbuf[...], wbuf[base + a, :, :width]
                ).reshape(rows, cols, width)
                sb[3 * at + a] = columns(k, 0)
                shifted_copy(3 * at + a).start()
            return 0

        lax.fori_loop(0, 3, one, 0)
    aux_copy.wait()
    xt_copy.wait()
    cat_copy.wait()
    for at, k in enumerate(plan.shifted):
        for a in range(3):
            @pl.when(in_field((1 - a) * RATE * k))
            def _(at=at, a=a):
                shifted_copy(3 * at + a).wait()


def run_blocks(plan, slots, meta, w_in, state):
    arrays = [value for cands in slots for value in cands]
    n, rows, cols, pix = plan.n, plan.rows, plan.cols, plan.pix
    c_in, c_out, n_sh = plan.c_in, plan.c_out, plan.n_sh
    shapes = [
        jax.ShapeDtypeStruct((2, n, c_in, pix), BF16),
        jax.ShapeDtypeStruct((2, n, pix, len(plan.direct) * c_out), BF16),
        jax.ShapeDtypeStruct((3 * n_sh, 2, n * rows, cols, c_out), F32),
        jax.ShapeDtypeStruct((2, n, EXTRA, c_in), BF16),
    ]
    widest = max(len(g) for g in plan.loads) * c_out
    aliased = state is not None
    operands = [*arrays, w_in] + (list(state) if aliased else [])
    aliases = {1 + len(arrays) + 1 + i: i for i in range(4)} if aliased else {}
    return pl.pallas_call(
        functools.partial(block_kernel, plan, len(arrays), len(slots), aliased),
        grid_spec=pltpu.PrefetchScalarGridSpec(
            num_scalar_prefetch=1,
            grid=(len(slots),),
            in_specs=[pl.BlockSpec(memory_space=pl.ANY)] * len(operands),
            out_specs=[pl.BlockSpec(memory_space=pl.ANY)] * 4,
            scratch_shapes=[
                pltpu.VMEM((2, pix + EXTRA, c_in), BF16),
                pltpu.VMEM((len(plan.loads), c_in, widest), BF16),
                pltpu.VMEM((c_in, pix), BF16),
                pltpu.VMEM((pix, len(plan.direct) * c_out), BF16),
                pltpu.VMEM((3 * n_sh, rows, cols, c_out), F32),
                pltpu.VMEM((rows, cols + 2 * EDGE, widest), F32),
                pltpu.SemaphoreType.DMA((2,)),
                pltpu.SemaphoreType.DMA((len(plan.loads), 4)),
                pltpu.SemaphoreType.DMA((3,)),
                pltpu.SemaphoreType.DMA((3 * n_sh,)),
            ],
        ),
        out_shape=shapes,
        input_output_aliases=aliases,
        compiler_params=pltpu.CompilerParams(
            dimension_semantics=("arbitrary",), vmem_limit_bytes=BLOCK_VMEM
        ),
        cost_estimate=pl.CostEstimate(
            flops=len(slots) * 2 * pix * c_in * c_out * (10 + 6 * n_sh),
            bytes_accessed=20_000_000 + len(slots) * 20_000_000,
            transcendentals=0,
        ),
        name="block_forward",
    )(meta, *operands)


def field_kernel(plan, last, tab, *refs):
    n, rows, cols, pix = plan.n, plan.rows, plan.cols, plan.pix
    c_in, c_out, n_sh = plan.c_in, plan.c_out, plan.n_sh
    n_rows_in = 2 * n_sh * rows
    unit_rows, depth, flags = plan.unit_rows, plan.depth, plan.flags
    cat_ref = refs[0]
    mid_refs = refs[1:1 + n_sh]
    s_refs = refs[1 + n_sh:1 + n_sh + n_rows_in]
    refs = refs[1 + n_sh + n_rows_in:]
    aux_ref, all_ref, w28_ref, wproj_ref, wcls_ref, cw_ref, xt_ref = refs[:7]
    refs = refs[7:]
    if last:
        prev_g, prev_p, prev_c = refs[:3]
        refs = refs[3:]
    g_out, p_out, c_ref_out = refs[:3]
    (dbuf, pad, mean, ybuf, lbuf, dybuf, gp, spool, pact, catall, acc, stage, sems) = refs[3:]
    step = pl.program_id(0)
    edge_rows = rows - 1

    def finish(value, prev):
        grad = value.astype(BF16)
        if not last:
            return grad
        return (prev.astype(F32) + grad.astype(F32)) * 0.5

    @pl.when(step == 0)
    def _():
        zero = jnp.zeros((edge_rows, cols, dbuf.shape[2]), BF16)
        dbuf[:edge_rows] = zero
        dbuf[edge_rows + plan.height:] = zero
        pad[:, :EDGE, :] = jnp.zeros((rows, EDGE, c_out), F32)
        pad[:, EDGE + cols:, :] = jnp.zeros((rows, EDGE, c_out), F32)
        total = jnp.zeros((1, c_in), F32)
        for j in range(n):
            extra = all_ref[j].astype(F32)
            total = total + ((extra[2:3] + extra[1:2]) + extra[0:1])
        mean_in = (total / plan.total).astype(BF16)
        mean[...] = jnp.broadcast_to(mean_in.astype(F32), (16, c_in))
        pact[...] = nn(mean[...].astype(BF16), w28_ref[0])

    @pl.when(step < n)
    def _():
        block = step
        cat5 = catall.at[block]
        for k in range(4):
            part = slice(k * c_out, (k + 1) * c_out)
            if k in plan.shifted:
                at = plan.shifted.index(k)
                r = RATE * k
                pre = mid_refs[at]
                for i in range(rows):
                    h = block * rows + i
                    line = pre[i]
                    for side, src in ((0, h - r), (1, h + r)):
                        ok = jnp.logical_and(src >= 0, src < plan.height)
                        ref = s_refs[(2 * at + side) * rows + i]
                        line = line + jnp.where(ok, ref[...], 0.0)
                    cat5[i * cols:(i + 1) * cols, part] = jnp.maximum(line, 0.0).astype(BF16)
            else:
                at = plan.direct.index(k)
                cat5[:, part] = cat_ref[:, at * c_out:(at + 1) * c_out]
        pool_act = jnp.maximum(pact[0:1, :], 0.0).astype(BF16)
        cat5[:, 4 * c_out:] = jnp.broadcast_to(pool_act, (pix, c_out))
        y_pre = nn(cat5[...], wproj_ref[...])
        y_act = jnp.maximum(y_pre, 0.0).astype(BF16)
        logits = nn(y_act, wcls_ref[...])
        lane = lax.broadcasted_iota(jnp.int32, (pix, 128), 1)
        live = lane < plan.classes
        expo = jnp.where(live, jnp.exp(logits), 0.0)
        prob = expo / jnp.sum(expo, axis=1, keepdims=True)
        names = aux_ref[3:4, :512].astype(F32)
        label = jnp.broadcast_to(names, (128, 512)).T[:pix]
        onehot = jnp.where(label == lane.astype(F32), 1.0, 0.0)
        weight = jnp.zeros((pix, 128), F32)
        for c in range(plan.classes):
            weight = jnp.where(label == float(c), cw_ref[c], weight)
        d_logits = jnp.where(
            live, (prob - onehot) * weight * (LOSS_SCALE / plan.total), 0.0
        ).astype(BF16)
        d_y = jnp.where(y_pre > 0, nt(d_logits, wcls_ref[...]), 0.0).astype(BF16)
        ybuf[block] = y_act
        lbuf[block] = d_logits
        dybuf[block] = d_y
        for k in range(4):
            want = [tab[flags + n + 3 * k + b] for b in range(3)]
            part = slice(k * c_out, (k + 1) * c_out)

            @pl.when((want[0] >= 0) | (want[1] >= 0) | (want[2] >= 0))
            def _(k=k, want=want, part=part):
                d_cat = nt(d_y, wproj_ref[part, :])
                d_k = jnp.where(cat5[:, part] > 0, d_cat, 0.0).astype(BF16)
                d_k = d_k.reshape(rows, cols, c_out)
                if k > 0:
                    pad[:, EDGE:EDGE + cols, :] = d_k.astype(F32)
                at = pl.ds(block * rows + edge_rows, rows)
                for b in range(3):
                    if k == 0 and b != 1:
                        continue

                    @pl.when(want[b] >= 0)
                    def _(b=b):
                        lanes = pl.ds(pl.multiple_of(jnp.maximum(want[b], 0) * c_out, c_out), c_out)
                        if b == 1:
                            dbuf[at, :, lanes] = d_k
                        else:
                            first = EDGE + (1 - b) * RATE * k
                            dbuf[at, :, lanes] = pad[:, first:first + cols, :].astype(BF16)

    @pl.when(step == n - 1)
    def _():
        all_dy = dybuf[...].reshape(n * pix, c_out)
        pool = wproj_ref[4 * c_out:, :]
        rest = nn(jnp.ones((16, n * pix), BF16), all_dy)
        total = jnp.zeros(rest.shape, F32)
        for _i in range(3):
            head = rest.astype(BF16)
            total = total + nt(head, pool)
            rest = rest - head.astype(F32)
        spool[...] = jnp.where(pact[...] > 0, jnp.broadcast_to(total[0:1, :], total.shape), 0.0)
        window = pl.ds(pl.multiple_of(tab[flags + n + 13], 128), plan.window)
        g_proj = jnp.zeros((c_out, plan.window), F32)
        g_cls = jnp.zeros((128, c_out), F32)
        for j in range(n):
            g_proj = g_proj + nn(
                nt(identity(c_out), dybuf[j]).astype(BF16), catall[j, :, window]
            )
            g_cls = g_cls + nn(nt(identity(128), lbuf[j]).astype(BF16), ybuf[j])
        gp[:plan.window, :] = g_proj.T
        index = tab[flags + n + 12]
        first = pl.multiple_of(index * plan.proj_rows - tab[flags + n + 13], 32)
        p_out[...] = finish(gp[pl.ds(first, plan.proj_rows), :], prev_p[...] if last else None)
        gp[:c_out, :128] = g_cls.T
        first = pl.multiple_of(index * plan.cls_rows, plan.cls_rows)
        c_ref_out[...] = finish(
            gp[pl.ds(first, plan.cls_rows), :128], prev_c[...] if last else None
        )

    def out_copy(part, slot, t):
        row = tab[(part * depth + t) * 6 + 5] * unit_rows
        return pltpu.make_async_copy(
            stage.at[slot, t],
            g_out.at[pl.ds(pl.multiple_of(row, unit_rows), unit_rows)],
            sems.at[slot, t],
        )

    @pl.when(step >= n)
    def _():
        part = step - n
        parity = lax.rem(part, 2)

        def one(t, _):
            base = (part * depth + t) * 6
            slot, move, low, high = tab[base], tab[base + 1], tab[base + 2], tab[base + 3]
            kind = tab[base + 4]

            def product(taps):
                width = taps * c_out
                lanes = pl.ds(pl.multiple_of(slot * c_out, c_out), width)

                def term(j):
                    first = j * rows - move + edge_rows
                    return nn(xt_ref[j], dbuf[pl.ds(first, rows), :, lanes].reshape(pix, width))

                whole = jnp.logical_and(low == 0, high == n)

                @pl.when(whole)
                def _():
                    total = term(0)
                    for j in range(1, n):
                        total = total + term(j)
                    acc[:, :width] = total

                @pl.when(jnp.logical_not(whole))
                def _():
                    acc[:, :width] = jnp.zeros((unit_rows, width), F32)

                    def add(j, _):
                        acc[:, :width] += term(j)
                        return 0

                    lax.fori_loop(low, high, add, 0)

            @pl.when(kind == 3)
            def _():
                product(3)

            @pl.when(kind == 0)
            def _():
                product(1)

            @pl.when(kind == 2)
            def _():
                acc[:, :c_out] = jnp.zeros((unit_rows, c_out), F32)

            @pl.when(kind == 1)
            def _():
                first = pl.multiple_of(part * unit_rows, unit_rows)
                row = mean[0:1, pl.ds(first, unit_rows)]
                column = jnp.broadcast_to(row, (128, unit_rows)).T
                for c in range(c_out // 128):
                    lanes = slice(c * 128, (c + 1) * 128)
                    acc[:, lanes] = column * spool[0:1, lanes]

            def emit(at, lanes):
                if last:
                    stage[parity, at] = finish(acc[:, lanes], prev_g[at])
                    out_copy(part, parity, at).start()
                else:
                    g_out[at] = finish(acc[:, lanes], None)

            @pl.when(kind != 4)
            def _():
                emit(t, slice(0, c_out))

            @pl.when(kind == 3)
            def _():
                for b in (1, 2):
                    emit(t + b, slice(b * c_out, (b + 1) * c_out))

            return 0

        lax.fori_loop(0, tab[flags + part], one, 0)

        if last:
            def drain(which, slot):
                def one(t, _):
                    out_copy(which, slot, t).wait()
                    return 0
                lax.fori_loop(0, tab[flags + which], one, 0)

            @pl.when(part > 0)
            def _():
                drain(part - 1, 1 - parity)

            @pl.when(part == n - 1)
            def _():
                drain(part, parity)


def run_field(plan, field, tab, state, w_in, w_proj, wcls, cw, prev):
    n, rows, cols, pix = plan.n, plan.rows, plan.cols, plan.pix
    c_in, c_out, n_sh = plan.c_in, plan.c_out, plan.n_sh
    unit_rows, depth = plan.unit_rows, plan.depth
    last = prev is not None
    xt, cat, s, aux = state

    def blk(i):
        return jnp.minimum(i, n - 1)

    def part(i):
        return jnp.maximum(i - n, 0)

    in_specs = [
        pl.BlockSpec(
            (None, None, pix, len(plan.direct) * c_out), lambda i, t: (field, blk(i), 0, 0)
        ),
    ]
    operands = [cat]
    for at in range(n_sh):
        in_specs.append(pl.BlockSpec(
            (None, None, rows, cols, c_out),
            lambda i, t, at=at: (3 * at + 1, field, blk(i), 0, 0),
        ))
        operands.append(s)
    for at, k in enumerate(plan.shifted):
        for side in range(2):
            move = (2 * side - 1) * RATE * k
            for row in range(rows):
                def index(i, t, at=at, side=side, move=move, row=row):
                    h = jnp.clip(blk(i) * rows + row + move, 0, plan.height - 1)
                    return (3 * at + 2 * side, field, h, 0, 0)
                in_specs.append(pl.BlockSpec((None, None, None, cols, c_out), index))
                operands.append(s)
    in_specs += [
        pl.BlockSpec((None, None, EXTRA, c_in), lambda i, t: (field, blk(i), 0, 0)),
        pl.BlockSpec((None, n, EXTRA, c_in), lambda i, t: (field, 0, 0, 0)),
        pl.BlockSpec((1, c_in, c_out), lambda i, t: (28, 0, 0)),
        pl.BlockSpec((5 * c_out, c_out), lambda i, t: (0, 0)),
        pl.BlockSpec((c_out, 128), lambda i, t: (0, 0)),
        pl.BlockSpec(memory_space=pltpu.SMEM),
        pl.BlockSpec((None, n, unit_rows, pix), lambda i, t: (field, 0, part(i), 0)),
    ]
    operands += [aux, aux, w_in, w_proj, wcls, cw, xt]
    kind = F32 if last else BF16
    inner = pl.BlockSpec((None, depth, unit_rows, c_out), lambda i, t: (part(i), 0, 0, 0))
    small = [
        pl.BlockSpec((plan.proj_rows, c_out), lambda i, t: (0, 0)),
        pl.BlockSpec((plan.cls_rows, 128), lambda i, t: (0, 0)),
    ]
    if last:
        in_specs += [inner] + small
        operands += list(prev)
        main_spec = pl.BlockSpec(memory_space=pl.ANY)
        main_shape = jax.ShapeDtypeStruct((plan.units * unit_rows, c_out), F32)
    else:
        main_spec = inner
        main_shape = jax.ShapeDtypeStruct((n, depth, unit_rows, c_out), BF16)
    return pl.pallas_call(
        functools.partial(field_kernel, plan, last),
        grid_spec=pltpu.PrefetchScalarGridSpec(
            num_scalar_prefetch=1,
            grid=(2 * n,),
            in_specs=in_specs,
            out_specs=[main_spec] + small,
            scratch_shapes=[
                pltpu.VMEM((plan.height + 2 * (rows - 1), cols, plan.n_slots * c_out), BF16),
                pltpu.VMEM((rows, cols + 2 * EDGE, c_out), F32),
                pltpu.VMEM((16, c_in), F32),
                pltpu.VMEM((n, pix, c_out), BF16),
                pltpu.VMEM((n, pix, 128), BF16),
                pltpu.VMEM((n, pix, c_out), BF16),
                pltpu.VMEM((max(plan.window, c_out), c_out), F32),
                pltpu.VMEM((16, c_out), F32),
                pltpu.VMEM((16, c_out), F32),
                pltpu.VMEM((n, pix, 5 * c_out), BF16),
                pltpu.VMEM((unit_rows, 3 * c_out), F32),
                pltpu.VMEM((2, depth if last else 1, unit_rows, c_out), F32),
                pltpu.SemaphoreType.DMA((2, depth)),
            ],
        ),
        out_shape=[
            main_shape,
            jax.ShapeDtypeStruct((plan.proj_rows, c_out), kind),
            jax.ShapeDtypeStruct((plan.cls_rows, 128), kind),
        ],
        compiler_params=pltpu.CompilerParams(
            dimension_semantics=("arbitrary",), vmem_limit_bytes=FIELD_VMEM
        ),
        cost_estimate=pl.CostEstimate(
            flops=10_000_000_000, bytes_accessed=90_000_000, transcendentals=0
        ),
        name="field_grads",
    )(tab, *operands)


def after(value, *others):
    return lax.optimization_barrier((value, *others))[0]


def per_device(plan, features, labels, w_in, w_proj, w_cls, class_weight, matching):
    n, reps, rows, pix, c_in = plan.n, plan.reps, plan.rows, plan.pix, plan.c_in
    names = jnp.pad(labels[0].reshape(1, pix).astype(F32), ((0, 0), (0, c_in - pix)))
    x = pl.pallas_call(
        functools.partial(pack_kernel, pix),
        out_shape=jax.ShapeDtypeStruct((pix + EXTRA, c_in), BF16),
        name="pack",
    )(features[0].reshape(pix, c_in), names)
    here = lax.axis_index("space")
    n_bits = reps.bit_length() - 1
    bits = [jnp.bitwise_and(jnp.right_shift(matching[0], b), 1) == 1 for b in range(n_bits)]
    top = jnp.int32(0)
    for at, b in enumerate(list(range(1, n_bits)) + [0]):
        top = jnp.where(bits[b], n_bits - 1 - at, top)
    tab = jnp.asarray(plan.tables)[here]
    wcls = jnp.pad(w_cls, ((0, 0), (0, 128 - plan.classes)))

    def along(value, way, step):
        pairs = [
            (i, i + way) for i in range(n)
            if 0 <= i + way < n and 0 <= i - way * (step - 1) < n
        ]
        return lax.ppermute(value, "space", pairs)

    def hop(value, b):
        return lax.ppermute(value, "rep", [(r, r ^ (1 << b)) for r in range(reps)])

    order = np.array(
        [sorted(range(n), key=lambda j: (abs(j - s), j)) for s in range(n)], np.int32
    )
    blocks = jnp.asarray(order)[here]

    def arrival(q, ups, downs):
        value = None
        for s in range(n):
            j = int(order[s, q])
            arrived = ups[s - j] if j < s else downs[j - s]
            value = arrived if value is None else jnp.where(here == s, arrived, value)
        return value

    common = (w_in, w_proj, wcls, class_weight)
    hops = list(range(1, n_bits)) + [0]
    rounds = n + n_bits - 1
    ups, downs = [x], [x]
    turns = []
    for t in range(1, rounds + 1):
        turn = [(t - 1, 0)] if t - 1 < n else []
        if t == rounds:
            turn += [(q, 1) for q in range(max(0, n + 1 - n_bits), n)]
        elif t >= n_bits and t <= n:
            turn.append((t - n_bits, 1))
        turns.append(turn)
    metas = [
        jnp.stack([
            jnp.stack([(top if f else 0) + jnp.int32(n_bits * at if f and turn[0][1] else at),
                       blocks[q], jnp.int32(f)])
            for at, (q, f) in enumerate(turn)
        ]) if turn else None
        for turn in turns
    ]
    values, moves = {0: x}, {q: [] for q in range(n)}
    state, grads = None, None
    for t in range(1, rounds + 1):
        q = t - 1
        if 0 < q < n:
            values[q] = arrival(q, ups, downs)
        for i in range(1, n_bits):
            if 0 <= q - i < n:
                values[q - i] = jnp.where(bits[hops[i - 1]], moves[q - i][0], values[q - i])
        for i in reversed(range(n_bits)):
            if 0 <= q - i < n:
                moves[q - i].insert(0, hop(values[q - i], hops[i]))
        if t < n:
            ups.append(along(ups[-1], 1, t))
            downs.append(along(downs[-1], -1, t))
        slots = [moves[at] if f else [values[at]] for at, f in turns[q]]
        if slots:
            state = run_blocks(plan, slots, metas[q], w_in, state)
        if q == min(n, rounds - 1):
            grads = tuple(run_field(plan, 0, tab, state, *common, None))
        if t < rounds:
            live = (ups, downs, values, moves, state, grads, metas, tab, wcls)
            live = lax.optimization_barrier(live)
            ups, downs, values, moves, state, grads, metas, tab, wcls = live
    avg_in, avg_proj, avg_cls = run_field(plan, 1, tab, state, *common, grads)
    return avg_in[None], avg_proj[None], avg_cls[None, :, :plan.classes]


def solution(mesh):
    n, reps = mesh.shape["space"], mesh.shape["rep"]

    def build(features, labels, w_in, w_proj, w_cls, class_weight, matching):
        _, rows, cols, c_in = features.shape
        plan = Plan(n, reps, rows // n, cols, c_in, w_proj.shape[1], w_cls.shape[1])
        return jax.shard_map(
            functools.partial(per_device, plan),
            mesh=mesh,
            in_specs=(P("rep", "space", None, None), P("rep", "space", None), P(), P(), P(), P(), P()),
            out_specs=(P("rep", "space", None), P("rep", "space", None), P("rep", "space", None)),
            check_vma=False,
        )(features, labels, w_in, w_proj, w_cls, class_weight, matching)

    return build
```

```python
import functools

import jax
import jax.numpy as jnp
import numpy as np
from jax import lax
from jax.experimental import pallas as pl
from jax.experimental.pallas import tpu as pltpu
from jax.sharding import PartitionSpec as P

LOSS_SCALE = 1024.0
RATE = 12
EDGE = 40
EXTRA = 16
BF16 = jnp.bfloat16
F32 = jnp.float32
BLOCK_VMEM = 50 * 1024 * 1024
FIELD_VMEM = 50 * 1024 * 1024


def nn(a, b):
    return lax.dot_general(a, b, (((1,), (0,)), ((), ())), preferred_element_type=F32)


def nt(a, b):
    return lax.dot_general(a, b, (((1,), (1,)), ((), ())), preferred_element_type=F32)


def tn(a, b):
    return lax.dot_general(a, b, (((0,), (0,)), ((), ())), preferred_element_type=F32)


def identity(size):
    rows = lax.broadcasted_iota(jnp.int32, (size, size), 0)
    cols = lax.broadcasted_iota(jnp.int32, (size, size), 1)
    return (rows == cols).astype(F32).astype(BF16)


class Plan:
    def __init__(self, n, reps, rows, cols, c_in, c_out, classes):
        self.n, self.reps, self.rows, self.cols = n, reps, rows, cols
        self.c_in, self.c_out, self.classes = c_in, c_out, classes
        self.height = rows * n
        self.pix = rows * cols
        self.total = self.pix * n
        self.shifted = [k for k in (1, 2, 3) if RATE * k < self.height]
        self.direct = [k for k in range(4) if k not in self.shifted]
        self.n_sh = len(self.shifted)
        row = lambda k, a: [1 + 9 * (k - 1) + 3 * a + b for b in range(3)]
        still = [row(k, 1) for k in self.direct[1:]]
        self.loads = [[0] + (still[0] if still else [])] + still[1:]
        for k in self.shifted:
            self.loads += [row(k, a) for a in range(3)]
        self.units = 29
        self.unit_rows = c_in // n
        self.proj_rows = 5 * c_out // n
        self.cls_rows = c_out // n
        starts = [self.proj_rows * s // 128 * 128 for s in range(n)]
        ends = [-(-self.proj_rows * (s + 1) // 128) * 128 for s in range(n)]
        self.window = max(e - b for b, e in zip(starts, ends))
        self.starts = [min(b, 5 * c_out - self.window) for b in starts]
        tables = [self.table(s) for s in range(n)]
        self.n_slots = max(t[1] for t in tables)
        self.depth = max(t[2] for t in tables)
        self.tables = np.array([
            sum((c + [[0] * 6] * (self.depth - len(c)) for c in t[0]), []) for t in tables
        ], np.int32).reshape(n, -1)
        self.flags = self.tables.shape[1]
        self.tables = np.concatenate([
            self.tables,
            np.array([
                [len(c) for c in t[0]] + t[3] + [s, self.starts[s]] for s, t in enumerate(tables)
            ], np.int32),
        ], axis=1)

    def tap(self, t):
        if t == 0:
            return (0, 1, 1)
        if t == 28:
            return None
        k, rest = (t - 1) // 9 + 1, (t - 1) % 9
        a, b = rest // 3, rest % 3
        if a != 1 and k not in self.shifted:
            return "zero"
        return (k, a, b)

    def table(self, s):
        parts = [[] for _ in range(self.n)]
        here = range(s * self.units, (s + 1) * self.units)
        slots = {}
        for k in range(4):
            for b in ((1,) if k == 0 else range(3)):
                if any(
                    isinstance(self.tap(u // self.n), tuple)
                    and (self.tap(u // self.n)[0], self.tap(u // self.n)[2]) == (k, b)
                    for u in here
                ):
                    slots[(k, b)] = len(slots)
        for unit in here:
            c, tap = unit % self.n, self.tap(unit // self.n)
            local = unit - s * self.units
            if tap is None or tap == "zero":
                parts[c].append([0, 0, 0, 0, 1 if tap is None else 2, local])
                continue
            k, a, b = tap
            move = (a - 1) * RATE * k
            valid = [
                j for j in range(self.n)
                if any(0 <= self.rows * j + i - move < self.height for i in range(self.rows))
            ]
            entry = [slots[(k, b)], move, valid[0], valid[-1] + 1, 0, local]
            if b == 2 and len(parts[c]) > 1 and all(
                e[4] == 0 and e[:4] == [entry[0] - back] + entry[1:4]
                for back, e in ((1, parts[c][-1]), (2, parts[c][-2]))
            ):
                parts[c][-2][4] = 3
                parts[c][-1][4] = 4
                entry[4] = 4
            parts[c].append(entry)
        want = [slots.get((k, b), -1) for k in range(4) for b in range(3)]
        return parts, len(slots), max(len(c) for c in parts), want


def pack_kernel(pix, x_ref, lab_ref, out_ref):
    x = x_ref[...]
    out_ref[:pix, :] = x
    total = jnp.sum(x.astype(F32), axis=0, keepdims=True)
    head = total.astype(BF16).astype(F32)
    mid = (total - head).astype(BF16).astype(F32)
    row = lax.broadcasted_iota(jnp.int32, (EXTRA, x.shape[1]), 0)
    extra = jnp.zeros((EXTRA, x.shape[1]), F32)
    for at, value in enumerate((head, mid, total - head - mid, lab_ref[...])):
        extra = jnp.where(row == at, value, extra)
    out_ref[pix:, :] = extra.astype(BF16)


def block_kernel(plan, n_cand, n_slots, aliased, meta, *refs):
    rows, cols, c_in, c_out = plan.rows, plan.cols, plan.c_in, plan.c_out
    pix = plan.pix
    cands = refs[:n_cand]
    w_hbm = refs[n_cand]
    refs = refs[n_cand + 1 + (4 if aliased else 0):]
    xt_out, cat_out, s_out, aux_out = refs[:4]
    xin, wbuf, xtb, catb, sb, res, sem_x, sem_w, sem_o, sem_s = refs[4:]
    step = pl.program_id(0)
    block, field = meta[step, 1], meta[step, 2]
    now = lax.rem(step, 2)
    xbuf = xin.at[now, pl.ds(0, pix)]

    def fetch(at, slot):
        for c in range(n_cand):
            @pl.when(meta[at, 0] == c)
            def _(c=c):
                pltpu.make_async_copy(cands[c], xin.at[slot], sem_x.at[slot]).start()

    def weights(group, taps):
        return [
            pltpu.make_async_copy(
                w_hbm.at[tap], wbuf.at[group, :, pl.ds(i * c_out, c_out)], sem_w.at[group, i]
            )
            for i, tap in enumerate(taps)
        ]

    @pl.when(step == 0)
    def _():
        fetch(0, 0)
        for group, taps in enumerate(plan.loads):
            for copy in weights(group, taps):
                copy.start()
        res[:, :EDGE, :] = jnp.zeros((rows, EDGE, res.shape[2]), F32)
        res[:, EDGE + cols:, :] = jnp.zeros((rows, EDGE, res.shape[2]), F32)

    if n_slots > 1:
        @pl.when(step + 1 < n_slots)
        def _():
            fetch(step + 1, 1 - now)

    pltpu.make_async_copy(cands[0], xin.at[now], sem_x.at[now]).wait()
    aux_copy = pltpu.make_async_copy(
        xin.at[now, pl.ds(pix, EXTRA)], aux_out.at[field, block], sem_o.at[2]
    )
    aux_copy.start()
    eye = identity(256)
    for c in range(c_in // 256):
        part = slice(c * 256, (c + 1) * 256)
        xtb[part, :] = nt(eye, xbuf[:, part]).astype(BF16)
    xt_copy = pltpu.make_async_copy(xtb, xt_out.at[field, block], sem_o.at[0])
    xt_copy.start()

    def in_field(move):
        first = block * rows + move
        return jnp.logical_and(first + rows - 1 >= 0, first < plan.height)

    def loaded(group, taps):
        @pl.when(step == 0)
        def _():
            for copy in weights(group, taps):
                copy.wait()

    def columns(k, first):
        r = RATE * k
        part = [slice(first + i * c_out, first + (i + 1) * c_out) for i in range(3)]
        return (
            res[:, EDGE - r:EDGE - r + cols, part[0]]
            + res[:, EDGE:EDGE + cols, part[1]]
            + res[:, EDGE + r:EDGE + r + cols, part[2]]
        )

    def relu_to(k, value):
        at = plan.direct.index(k)
        catb[:, at * c_out:(at + 1) * c_out] = (
            jnp.maximum(value, 0.0).astype(BF16).reshape(pix, c_out)
        )

    def shifted_copy(at):
        return pltpu.make_async_copy(
            sb.at[at], s_out.at[at, field, pl.ds(block * rows, rows)], sem_s.at[at]
        )

    group = 0
    first = c_out
    loaded(0, plan.loads[0])
    width = len(plan.loads[0]) * c_out
    res[:, EDGE:EDGE + cols, :width] = nn(xbuf[...], wbuf[0, :, :width]).reshape(
        rows, cols, width
    )
    relu_to(0, res[:, EDGE:EDGE + cols, :c_out])
    group = 1
    for k in plan.direct[1:]:
        if first + 3 * c_out > width:
            loaded(group, plan.loads[group])
            width, first = 3 * c_out, 0
            res[:, EDGE:EDGE + cols, :width] = nn(xbuf[...], wbuf[group, :, :width]).reshape(
                rows, cols, width
            )
            group += 1
        relu_to(k, columns(k, first))
        first += 3 * c_out
    cat_copy = pltpu.make_async_copy(catb, cat_out.at[field, block], sem_o.at[1])
    cat_copy.start()
    width = 3 * c_out
    for at, k in enumerate(plan.shifted):
        for a in range(3):
            loaded(group + 3 * at + a, plan.loads[group + 3 * at + a])

        def one(a, _, k=k, at=at, base=group + 3 * at):
            @pl.when(in_field((1 - a) * RATE * k))
            def _():
                res[:, EDGE:EDGE + cols, :width] = nn(
                    xbuf[...], wbuf[base + a, :, :width]
                ).reshape(rows, cols, width)
                sb[3 * at + a] = columns(k, 0)
                shifted_copy(3 * at + a).start()
            return 0

        lax.fori_loop(0, 3, one, 0)
    aux_copy.wait()
    xt_copy.wait()
    cat_copy.wait()
    for at, k in enumerate(plan.shifted):
        for a in range(3):
            @pl.when(in_field((1 - a) * RATE * k))
            def _(at=at, a=a):
                shifted_copy(3 * at + a).wait()


def run_blocks(plan, slots, meta, w_in, state):
    arrays = [value for cands in slots for value in cands]
    n, rows, cols, pix = plan.n, plan.rows, plan.cols, plan.pix
    c_in, c_out, n_sh = plan.c_in, plan.c_out, plan.n_sh
    shapes = [
        jax.ShapeDtypeStruct((2, n, c_in, pix), BF16),
        jax.ShapeDtypeStruct((2, n, pix, len(plan.direct) * c_out), BF16),
        jax.ShapeDtypeStruct((3 * n_sh, 2, n * rows, cols, c_out), F32),
        jax.ShapeDtypeStruct((2, n, EXTRA, c_in), BF16),
    ]
    widest = max(len(g) for g in plan.loads) * c_out
    aliased = state is not None
    operands = [*arrays, w_in] + (list(state) if aliased else [])
    aliases = {1 + len(arrays) + 1 + i: i for i in range(4)} if aliased else {}
    return pl.pallas_call(
        functools.partial(block_kernel, plan, len(arrays), len(slots), aliased),
        grid_spec=pltpu.PrefetchScalarGridSpec(
            num_scalar_prefetch=1,
            grid=(len(slots),),
            in_specs=[pl.BlockSpec(memory_space=pl.ANY)] * len(operands),
            out_specs=[pl.BlockSpec(memory_space=pl.ANY)] * 4,
            scratch_shapes=[
                pltpu.VMEM((2, pix + EXTRA, c_in), BF16),
                pltpu.VMEM((len(plan.loads), c_in, widest), BF16),
                pltpu.VMEM((c_in, pix), BF16),
                pltpu.VMEM((pix, len(plan.direct) * c_out), BF16),
                pltpu.VMEM((3 * n_sh, rows, cols, c_out), F32),
                pltpu.VMEM((rows, cols + 2 * EDGE, widest), F32),
                pltpu.SemaphoreType.DMA((2,)),
                pltpu.SemaphoreType.DMA((len(plan.loads), 4)),
                pltpu.SemaphoreType.DMA((3,)),
                pltpu.SemaphoreType.DMA((3 * n_sh,)),
            ],
        ),
        out_shape=shapes,
        input_output_aliases=aliases,
        compiler_params=pltpu.CompilerParams(
            dimension_semantics=("arbitrary",), vmem_limit_bytes=BLOCK_VMEM
        ),
        cost_estimate=pl.CostEstimate(
            flops=len(slots) * 2 * pix * c_in * c_out * (10 + 6 * n_sh),
            bytes_accessed=20_000_000 + len(slots) * 20_000_000,
            transcendentals=0,
        ),
        name="block_forward",
    )(meta, *operands)


def field_kernel(plan, field, last, tab, *refs):
    n, rows, cols, pix = plan.n, plan.rows, plan.cols, plan.pix
    c_in, c_out, n_sh = plan.c_in, plan.c_out, plan.n_sh
    n_rows_in = 2 * n_sh * rows
    unit_rows, depth, flags = plan.unit_rows, plan.depth, plan.flags
    cat_ref = refs[0]
    mid_refs = refs[1:1 + n_sh]
    s_refs = refs[1 + n_sh:1 + n_sh + n_rows_in]
    refs = refs[1 + n_sh + n_rows_in:]
    aux_ref, all_ref, w28_ref, wproj_ref, wcls_ref, cw_ref, xt_hbm = refs[:7]
    refs = refs[7:]
    if last:
        prev_g, prev_p, prev_c = refs[:3]
        refs = refs[3:]
    g_out, p_out, c_ref_out = refs[:3]
    (dbuf, pad, mean, ybuf, lbuf, dybuf, gp, spool, pact, catall, acc, stage, xt_ref, sem_xt,
     sems) = refs[3:]
    xt_copy = pltpu.make_async_copy(xt_hbm.at[field], xt_ref, sem_xt)
    step = pl.program_id(0)
    edge_rows = rows - 1

    def finish(value, prev):
        grad = value.astype(BF16)
        if not last:
            return grad
        return (prev.astype(F32) + grad.astype(F32)) * 0.5

    @pl.when(step == 0)
    def _():
        xt_copy.start()
        zero = jnp.zeros((edge_rows, cols, dbuf.shape[2]), BF16)
        dbuf[:edge_rows] = zero
        dbuf[edge_rows + plan.height:] = zero
        pad[:, :EDGE, :] = jnp.zeros((rows, EDGE, c_out), F32)
        pad[:, EDGE + cols:, :] = jnp.zeros((rows, EDGE, c_out), F32)
        total = jnp.zeros((1, c_in), F32)
        for j in range(n):
            extra = all_ref[j].astype(F32)
            total = total + ((extra[2:3] + extra[1:2]) + extra[0:1])
        mean_in = (total / plan.total).astype(BF16)
        mean[...] = jnp.broadcast_to(mean_in.astype(F32), (16, c_in))
        pact[...] = nn(mean[...].astype(BF16), w28_ref[0])

    @pl.when(step < n)
    def _():
        block = step
        cat5 = catall.at[block]
        for k in range(4):
            part = slice(k * c_out, (k + 1) * c_out)
            if k in plan.shifted:
                at = plan.shifted.index(k)
                r = RATE * k
                pre = mid_refs[at]
                for i in range(rows):
                    h = block * rows + i
                    line = pre[i]
                    for side, src in ((0, h - r), (1, h + r)):
                        ok = jnp.logical_and(src >= 0, src < plan.height)
                        ref = s_refs[(2 * at + side) * rows + i]
                        line = line + jnp.where(ok, ref[...], 0.0)
                    cat5[i * cols:(i + 1) * cols, part] = jnp.maximum(line, 0.0).astype(BF16)
            else:
                at = plan.direct.index(k)
                cat5[:, part] = cat_ref[:, at * c_out:(at + 1) * c_out]
        pool_act = jnp.maximum(pact[0:1, :], 0.0).astype(BF16)
        cat5[:, 4 * c_out:] = jnp.broadcast_to(pool_act, (pix, c_out))
        y_pre = nn(cat5[...], wproj_ref[...])
        y_act = jnp.maximum(y_pre, 0.0).astype(BF16)
        logits = nt(wcls_ref[...], y_act)
        row = lax.broadcasted_iota(jnp.int32, (16, pix), 0)
        live = row < plan.classes
        expo = jnp.where(live, jnp.exp(logits), 0.0)
        prob = expo / jnp.sum(expo, axis=0, keepdims=True)
        label = jnp.broadcast_to(aux_ref[3:4, :pix].astype(F32), (16, pix))
        onehot = jnp.where(label == row.astype(F32), 1.0, 0.0)
        weight = jnp.zeros((16, pix), F32)
        for c in range(plan.classes):
            weight = jnp.where(label == float(c), cw_ref[c], weight)
        d_logits = jnp.where(
            live, (prob - onehot) * weight * (LOSS_SCALE / plan.total), 0.0
        ).astype(BF16)
        d_y = jnp.where(y_pre > 0, tn(d_logits, wcls_ref[...]), 0.0).astype(BF16)
        ybuf[block] = y_act
        lbuf[block] = d_logits
        dybuf[block] = d_y
        for k in range(4):
            want = [tab[flags + n + 3 * k + b] for b in range(3)]
            part = slice(k * c_out, (k + 1) * c_out)

            @pl.when((want[0] >= 0) | (want[1] >= 0) | (want[2] >= 0))
            def _(k=k, want=want, part=part):
                d_cat = nt(d_y, wproj_ref[part, :])
                d_k = jnp.where(cat5[:, part] > 0, d_cat, 0.0).astype(BF16)
                d_k = d_k.reshape(rows, cols, c_out)
                if k > 0:
                    pad[:, EDGE:EDGE + cols, :] = d_k.astype(F32)
                at = pl.ds(block * rows + edge_rows, rows)
                for b in range(3):
                    if k == 0 and b != 1:
                        continue

                    @pl.when(want[b] >= 0)
                    def _(b=b):
                        lanes = pl.ds(pl.multiple_of(jnp.maximum(want[b], 0) * c_out, c_out), c_out)
                        if b == 1:
                            dbuf[at, :, lanes] = d_k
                        else:
                            first = EDGE + (1 - b) * RATE * k
                            dbuf[at, :, lanes] = pad[:, first:first + cols, :].astype(BF16)

    @pl.when(step == n - 1)
    def _():
        all_dy = dybuf[...].reshape(n * pix, c_out)
        pool = wproj_ref[4 * c_out:, :]
        rest = nn(jnp.ones((16, n * pix), BF16), all_dy)
        total = jnp.zeros(rest.shape, F32)
        for _i in range(3):
            head = rest.astype(BF16)
            total = total + nt(head, pool)
            rest = rest - head.astype(F32)
        spool[...] = jnp.where(pact[...] > 0, jnp.broadcast_to(total[0:1, :], total.shape), 0.0)
        window = pl.ds(pl.multiple_of(tab[flags + n + 13], 128), plan.window)
        g_proj = jnp.zeros((c_out, plan.window), F32)
        g_cls = jnp.zeros((16, c_out), F32)
        for j in range(n):
            g_proj = g_proj + nn(
                nt(identity(c_out), dybuf[j]).astype(BF16), catall[j, :, window]
            )
            g_cls = g_cls + nn(lbuf[j], ybuf[j])
        gp[:plan.window, :] = g_proj.T
        index = tab[flags + n + 12]
        first = pl.multiple_of(index * plan.proj_rows - tab[flags + n + 13], 32)
        p_out[...] = finish(gp[pl.ds(first, plan.proj_rows), :], prev_p[...] if last else None)
        gp[:c_out, :128] = jnp.concatenate([g_cls, jnp.zeros((112, c_out), F32)], axis=0).T
        first = pl.multiple_of(index * plan.cls_rows, plan.cls_rows)
        c_ref_out[...] = finish(
            gp[pl.ds(first, plan.cls_rows), :128], prev_c[...] if last else None
        )

    def out_copy(part, slot, t):
        row = tab[(part * depth + t) * 6 + 5] * unit_rows
        return pltpu.make_async_copy(
            stage.at[slot, t],
            g_out.at[pl.ds(pl.multiple_of(row, unit_rows), unit_rows)],
            sems.at[slot, t],
        )

    @pl.when(step == n)
    def _():
        xt_copy.wait()

    @pl.when(step >= n)
    def _():
        part = step - n
        parity = lax.rem(part, 2)
        mine = pl.ds(pl.multiple_of(part * unit_rows, unit_rows), unit_rows)

        def one(t, _):
            base = (part * depth + t) * 6
            slot, move, low, high = tab[base], tab[base + 1], tab[base + 2], tab[base + 3]
            kind = tab[base + 4]

            def product(taps):
                width = taps * c_out
                lanes = pl.ds(pl.multiple_of(slot * c_out, c_out), width)

                def term(j):
                    first = j * rows - move + edge_rows
                    return nn(xt_ref[j, mine, :], dbuf[pl.ds(first, rows), :, lanes].reshape(pix, width))

                whole = jnp.logical_and(low == 0, high == n)

                @pl.when(whole)
                def _():
                    total = term(0)
                    for j in range(1, n):
                        total = total + term(j)
                    acc[:, :width] = total

                @pl.when(jnp.logical_not(whole))
                def _():
                    acc[:, :width] = jnp.zeros((unit_rows, width), F32)

                    def add(j, _):
                        acc[:, :width] += term(j)
                        return 0

                    lax.fori_loop(low, high, add, 0)

            @pl.when(kind == 3)
            def _():
                product(3)

            @pl.when(kind == 0)
            def _():
                product(1)

            @pl.when(kind == 2)
            def _():
                acc[:, :c_out] = jnp.zeros((unit_rows, c_out), F32)

            @pl.when(kind == 1)
            def _():
                first = pl.multiple_of(part * unit_rows, unit_rows)
                row = mean[0:1, pl.ds(first, unit_rows)]
                column = jnp.broadcast_to(row, (128, unit_rows)).T
                for c in range(c_out // 128):
                    lanes = slice(c * 128, (c + 1) * 128)
                    acc[:, lanes] = column * spool[0:1, lanes]

            def emit(at, lanes):
                if last:
                    stage[parity, at] = finish(acc[:, lanes], prev_g[at])
                    out_copy(part, parity, at).start()
                else:
                    g_out[at] = finish(acc[:, lanes], None)

            @pl.when(kind != 4)
            def _():
                emit(t, slice(0, c_out))

            @pl.when(kind == 3)
            def _():
                for b in (1, 2):
                    emit(t + b, slice(b * c_out, (b + 1) * c_out))

            return 0

        lax.fori_loop(0, tab[flags + part], one, 0)

        if last:
            def drain(which, slot):
                def one(t, _):
                    out_copy(which, slot, t).wait()
                    return 0
                lax.fori_loop(0, tab[flags + which], one, 0)

            @pl.when(part > 0)
            def _():
                drain(part - 1, 1 - parity)

            @pl.when(part == n - 1)
            def _():
                drain(part, parity)


def run_field(plan, field, tab, state, w_in, w_proj, wcls, cw, prev):
    n, rows, cols, pix = plan.n, plan.rows, plan.cols, plan.pix
    c_in, c_out, n_sh = plan.c_in, plan.c_out, plan.n_sh
    unit_rows, depth = plan.unit_rows, plan.depth
    last = prev is not None
    xt, cat, s, aux = state

    def blk(i):
        return jnp.minimum(i, n - 1)

    def part(i):
        return jnp.maximum(i - n, 0)

    in_specs = [
        pl.BlockSpec(
            (None, None, pix, len(plan.direct) * c_out), lambda i, t: (field, blk(i), 0, 0)
        ),
    ]
    operands = [cat]
    for at in range(n_sh):
        in_specs.append(pl.BlockSpec(
            (None, None, rows, cols, c_out),
            lambda i, t, at=at: (3 * at + 1, field, blk(i), 0, 0),
        ))
        operands.append(s)
    for at, k in enumerate(plan.shifted):
        for side in range(2):
            move = (2 * side - 1) * RATE * k
            for row in range(rows):
                def index(i, t, at=at, side=side, move=move, row=row):
                    h = jnp.clip(blk(i) * rows + row + move, 0, plan.height - 1)
                    return (3 * at + 2 * side, field, h, 0, 0)
                in_specs.append(pl.BlockSpec((None, None, None, cols, c_out), index))
                operands.append(s)
    in_specs += [
        pl.BlockSpec((None, None, EXTRA, c_in), lambda i, t: (field, blk(i), 0, 0)),
        pl.BlockSpec((None, n, EXTRA, c_in), lambda i, t: (field, 0, 0, 0)),
        pl.BlockSpec((1, c_in, c_out), lambda i, t: (28, 0, 0)),
        pl.BlockSpec((5 * c_out, c_out), lambda i, t: (0, 0)),
        pl.BlockSpec((16, c_out), lambda i, t: (0, 0)),
        pl.BlockSpec(memory_space=pltpu.SMEM),
        pl.BlockSpec(memory_space=pl.ANY),
    ]
    operands += [aux, aux, w_in, w_proj, wcls, cw, xt]
    kind = F32 if last else BF16
    inner = pl.BlockSpec((None, depth, unit_rows, c_out), lambda i, t: (part(i), 0, 0, 0))
    small = [
        pl.BlockSpec((plan.proj_rows, c_out), lambda i, t: (0, 0)),
        pl.BlockSpec((plan.cls_rows, 128), lambda i, t: (0, 0)),
    ]
    if last:
        in_specs += [inner] + small
        operands += list(prev)
        main_spec = pl.BlockSpec(memory_space=pl.ANY)
        main_shape = jax.ShapeDtypeStruct((plan.units * unit_rows, c_out), F32)
    else:
        main_spec = inner
        main_shape = jax.ShapeDtypeStruct((n, depth, unit_rows, c_out), BF16)
    return pl.pallas_call(
        functools.partial(field_kernel, plan, field, last),
        grid_spec=pltpu.PrefetchScalarGridSpec(
            num_scalar_prefetch=1,
            grid=(2 * n,),
            in_specs=in_specs,
            out_specs=[main_spec] + small,
            scratch_shapes=[
                pltpu.VMEM((plan.height + 2 * (rows - 1), cols, plan.n_slots * c_out), BF16),
                pltpu.VMEM((rows, cols + 2 * EDGE, c_out), F32),
                pltpu.VMEM((16, c_in), F32),
                pltpu.VMEM((n, pix, c_out), BF16),
                pltpu.VMEM((n, 16, pix), BF16),
                pltpu.VMEM((n, pix, c_out), BF16),
                pltpu.VMEM((max(plan.window, c_out), c_out), F32),
                pltpu.VMEM((16, c_out), F32),
                pltpu.VMEM((16, c_out), F32),
                pltpu.VMEM((n, pix, 5 * c_out), BF16),
                pltpu.VMEM((unit_rows, 3 * c_out), F32),
                pltpu.VMEM((2, depth if last else 1, unit_rows, c_out), F32),
                pltpu.VMEM((n, c_in, pix), BF16),
                pltpu.SemaphoreType.DMA,
                pltpu.SemaphoreType.DMA((2, depth)),
            ],
        ),
        out_shape=[
            main_shape,
            jax.ShapeDtypeStruct((plan.proj_rows, c_out), kind),
            jax.ShapeDtypeStruct((plan.cls_rows, 128), kind),
        ],
        compiler_params=pltpu.CompilerParams(
            dimension_semantics=("arbitrary",), vmem_limit_bytes=FIELD_VMEM
        ),
        cost_estimate=pl.CostEstimate(
            flops=10_000_000_000, bytes_accessed=90_000_000, transcendentals=0
        ),
        name="field_grads",
    )(tab, *operands)


def after(value, *others):
    return lax.optimization_barrier((value, *others))[0]


def per_device(plan, features, labels, w_in, w_proj, w_cls, class_weight, matching):
    n, reps, rows, pix, c_in = plan.n, plan.reps, plan.rows, plan.pix, plan.c_in
    names = jnp.pad(labels[0].reshape(1, pix).astype(F32), ((0, 0), (0, c_in - pix)))
    x = pl.pallas_call(
        functools.partial(pack_kernel, pix),
        out_shape=jax.ShapeDtypeStruct((pix + EXTRA, c_in), BF16),
        name="pack",
    )(features[0].reshape(pix, c_in), names)
    here = lax.axis_index("space")
    n_bits = reps.bit_length() - 1
    bits = [jnp.bitwise_and(jnp.right_shift(matching[0], b), 1) == 1 for b in range(n_bits)]
    top = jnp.int32(0)
    for at, b in enumerate(list(range(1, n_bits)) + [0]):
        top = jnp.where(bits[b], n_bits - 1 - at, top)
    tab = jnp.asarray(plan.tables)[here]
    wcls = jnp.pad(w_cls.T, ((0, 16 - plan.classes), (0, 0)))

    def along(value, way, step):
        pairs = [
            (i, i + way) for i in range(n)
            if 0 <= i + way < n and 0 <= i - way * (step - 1) < n
        ]
        return lax.ppermute(value, "space", pairs)

    def hop(value, b):
        return lax.ppermute(value, "rep", [(r, r ^ (1 << b)) for r in range(reps)])

    order = np.array(
        [sorted(range(n), key=lambda j: (abs(j - s), j)) for s in range(n)], np.int32
    )
    blocks = jnp.asarray(order)[here]

    def arrival(q, ups, downs):
        value = None
        for s in range(n):
            j = int(order[s, q])
            arrived = ups[s - j] if j < s else downs[j - s]
            value = arrived if value is None else jnp.where(here == s, arrived, value)
        return value

    common = (w_in, w_proj, wcls, class_weight)
    hops = list(range(1, n_bits)) + [0]
    rounds = n + n_bits - 1
    ups, downs, raw = [x], [x], (x, x)
    turns = []
    for t in range(1, rounds + 1):
        turn = [(t - 1, 0)] if t - 1 < n else []
        if t == rounds:
            turn += [(q, 1) for q in range(max(0, n + 1 - n_bits), n)]
        elif t >= n_bits and t <= n:
            turn.append((t - n_bits, 1))
        turns.append(turn)
    metas = [
        jnp.stack([
            jnp.stack([(top if f else 0) + jnp.int32(n_bits * at if f and turn[0][1] else at),
                       blocks[q], jnp.int32(f)])
            for at, (q, f) in enumerate(turn)
        ]) if turn else None
        for turn in turns
    ]
    values, moves = {0: x}, {q: [] for q in range(n)}
    state, grads = None, None
    for t in range(1, rounds + 1):
        q = t - 1
        if 0 < q < n:
            values[q] = arrival(q, ups, downs)
        for i in range(1, n_bits):
            if 0 <= q - i < n:
                values[q - i] = jnp.where(bits[hops[i - 1]], moves[q - i][0], values[q - i])
        for i in reversed(range(n_bits)):
            if 0 <= q - i < n:
                moves[q - i].insert(0, hop(values[q - i], hops[i]))
        if t < n:
            raw = along(raw[0], 1, t), along(raw[1], -1, t)
            ups.append(raw[0])
            downs.append(raw[1])
        slots = [moves[at] if f else [values[at]] for at, f in turns[q]]
        if slots:
            state = run_blocks(plan, slots, metas[q], w_in, state)
        if q == min(n, rounds - 1):
            grads = tuple(run_field(plan, 0, tab, state, *common, None))
        if t < rounds:
            live = (ups, downs, values, moves, state, grads, metas, tab, wcls)
            live = lax.optimization_barrier(live)
            ups, downs, values, moves, state, grads, metas, tab, wcls = live
    avg_in, avg_proj, avg_cls = run_field(plan, 1, tab, state, *common, grads)
    return avg_in[None], avg_proj[None], avg_cls[None, :, :plan.classes]


def solution(mesh):
    n, reps = mesh.shape["space"], mesh.shape["rep"]

    def build(features, labels, w_in, w_proj, w_cls, class_weight, matching):
        _, rows, cols, c_in = features.shape
        plan = Plan(n, reps, rows // n, cols, c_in, w_proj.shape[1], w_cls.shape[1])
        return jax.shard_map(
            functools.partial(per_device, plan),
            mesh=mesh,
            in_specs=(P("rep", "space", None, None), P("rep", "space", None), P(), P(), P(), P(), P()),
            out_specs=(P("rep", "space", None), P("rep", "space", None), P("rep", "space", None)),
            check_vma=False,
        )(features, labels, w_in, w_proj, w_cls, class_weight, matching)

    return build
```

```python
import functools

import jax
import jax.numpy as jnp
import numpy as np
from jax import lax
from jax.experimental import pallas as pl
from jax.experimental.pallas import tpu as pltpu
from jax.sharding import PartitionSpec as P

LOSS_SCALE = 1024.0
RATE = 12
EDGE = 40
EXTRA = 16
BF16 = jnp.bfloat16
F32 = jnp.float32
BLOCK_VMEM = 50 * 1024 * 1024
FIELD_VMEM = 50 * 1024 * 1024


def nn(a, b):
    return lax.dot_general(a, b, (((1,), (0,)), ((), ())), preferred_element_type=F32)


def nt(a, b):
    return lax.dot_general(a, b, (((1,), (1,)), ((), ())), preferred_element_type=F32)


def tn(a, b):
    return lax.dot_general(a, b, (((0,), (0,)), ((), ())), preferred_element_type=F32)


def identity(size):
    rows = lax.broadcasted_iota(jnp.int32, (size, size), 0)
    cols = lax.broadcasted_iota(jnp.int32, (size, size), 1)
    return (rows == cols).astype(F32).astype(BF16)


class Plan:
    def __init__(self, n, reps, rows, cols, c_in, c_out, classes):
        self.n, self.reps, self.rows, self.cols = n, reps, rows, cols
        self.c_in, self.c_out, self.classes = c_in, c_out, classes
        self.height = rows * n
        self.pix = rows * cols
        self.total = self.pix * n
        self.shifted = [k for k in (1, 2, 3) if RATE * k < self.height]
        self.direct = [k for k in range(4) if k not in self.shifted]
        self.n_sh = len(self.shifted)
        row = lambda k, a: [1 + 9 * (k - 1) + 3 * a + b for b in range(3)]
        still = [row(k, 1) for k in self.direct[1:]]
        self.loads = [[0] + (still[0] if still else [])] + still[1:]
        for k in self.shifted:
            self.loads += [row(k, a) for a in range(3)]
        self.units = 29
        self.unit_rows = c_in // n
        self.proj_rows = 5 * c_out // n
        self.cls_rows = c_out // n
        starts = [self.proj_rows * s // 128 * 128 for s in range(n)]
        ends = [-(-self.proj_rows * (s + 1) // 128) * 128 for s in range(n)]
        self.window = max(e - b for b, e in zip(starts, ends))
        self.starts = [min(b, 5 * c_out - self.window) for b in starts]
        tables = [self.table(s) for s in range(n)]
        self.n_slots = max(t[1] for t in tables)
        self.depth = max(t[2] for t in tables)
        self.tables = np.array([
            sum((c + [[0] * 6] * (self.depth - len(c)) for c in t[0]), []) for t in tables
        ], np.int32).reshape(n, -1)
        self.flags = self.tables.shape[1]
        self.tables = np.concatenate([
            self.tables,
            np.array([
                [len(c) for c in t[0]] + t[3] + [s, self.starts[s]] for s, t in enumerate(tables)
            ], np.int32),
        ], axis=1)

    def tap(self, t):
        if t == 0:
            return (0, 1, 1)
        if t == 28:
            return None
        k, rest = (t - 1) // 9 + 1, (t - 1) % 9
        a, b = rest // 3, rest % 3
        if a != 1 and k not in self.shifted:
            return "zero"
        return (k, a, b)

    def table(self, s):
        parts = [[] for _ in range(self.n)]
        here = range(s * self.units, (s + 1) * self.units)
        slots = {}
        for k in range(4):
            for b in ((1,) if k == 0 else range(3)):
                if any(
                    isinstance(self.tap(u // self.n), tuple)
                    and (self.tap(u // self.n)[0], self.tap(u // self.n)[2]) == (k, b)
                    for u in here
                ):
                    slots[(k, b)] = len(slots)
        for unit in here:
            c, tap = unit % self.n, self.tap(unit // self.n)
            local = unit - s * self.units
            if tap is None or tap == "zero":
                parts[c].append([0, 0, 0, 0, 1 if tap is None else 2, local])
                continue
            k, a, b = tap
            move = (a - 1) * RATE * k
            valid = [
                j for j in range(self.n)
                if any(0 <= self.rows * j + i - move < self.height for i in range(self.rows))
            ]
            entry = [slots[(k, b)], move, valid[0], valid[-1] + 1, 0, local]
            if b == 2 and len(parts[c]) > 1 and all(
                e[4] == 0 and e[:4] == [entry[0] - back] + entry[1:4]
                for back, e in ((1, parts[c][-1]), (2, parts[c][-2]))
            ):
                parts[c][-2][4] = 3
                parts[c][-1][4] = 4
                entry[4] = 4
            parts[c].append(entry)
        want = [slots.get((k, b), -1) for k in range(4) for b in range(3)]
        return parts, len(slots), max(len(c) for c in parts), want


def pack_kernel(pix, x_ref, lab_ref, out_ref):
    x = x_ref[...]
    out_ref[:pix, :] = x
    total = jnp.sum(x.astype(F32), axis=0, keepdims=True)
    head = total.astype(BF16).astype(F32)
    mid = (total - head).astype(BF16).astype(F32)
    row = lax.broadcasted_iota(jnp.int32, (EXTRA, x.shape[1]), 0)
    extra = jnp.zeros((EXTRA, x.shape[1]), F32)
    for at, value in enumerate((head, mid, total - head - mid, lab_ref[...])):
        extra = jnp.where(row == at, value, extra)
    out_ref[pix:, :] = extra.astype(BF16)


def block_kernel(plan, n_cand, n_slots, aliased, meta, *refs):
    rows, cols, c_in, c_out = plan.rows, plan.cols, plan.c_in, plan.c_out
    pix = plan.pix
    cands = refs[:n_cand]
    w_hbm = refs[n_cand]
    refs = refs[n_cand + 1 + (4 if aliased else 0):]
    xt_out, cat_out, s_out, aux_out = refs[:4]
    xin, wbuf, xtb, catb, sb, res, sem_x, sem_w, sem_o, sem_s = refs[4:]
    step = pl.program_id(0)
    block, field = meta[step, 1], meta[step, 2]
    now = lax.rem(step, 2)
    xbuf = xin.at[now, pl.ds(0, pix)]

    def fetch(at, slot):
        for c in range(n_cand):
            @pl.when(meta[at, 0] == c)
            def _(c=c):
                pltpu.make_async_copy(cands[c], xin.at[slot], sem_x.at[slot]).start()

    def weights(group, taps):
        return [
            pltpu.make_async_copy(
                w_hbm.at[tap], wbuf.at[group, :, pl.ds(i * c_out, c_out)], sem_w.at[group, i]
            )
            for i, tap in enumerate(taps)
        ]

    @pl.when(step == 0)
    def _():
        fetch(0, 0)
        for group, taps in enumerate(plan.loads):
            for copy in weights(group, taps):
                copy.start()
        res[:, :EDGE, :] = jnp.zeros((rows, EDGE, res.shape[2]), F32)
        res[:, EDGE + cols:, :] = jnp.zeros((rows, EDGE, res.shape[2]), F32)

    if n_slots > 1:
        @pl.when(step + 1 < n_slots)
        def _():
            fetch(step + 1, 1 - now)

    pltpu.make_async_copy(cands[0], xin.at[now], sem_x.at[now]).wait()
    aux_copy = pltpu.make_async_copy(
        xin.at[now, pl.ds(pix, EXTRA)], aux_out.at[field, block], sem_o.at[2]
    )
    aux_copy.start()
    eye = identity(256)
    for c in range(c_in // 256):
        part = slice(c * 256, (c + 1) * 256)
        xtb[part, :] = nt(eye, xbuf[:, part]).astype(BF16)
    xt_copy = pltpu.make_async_copy(xtb, xt_out.at[field, block], sem_o.at[0])
    xt_copy.start()

    def in_field(move):
        first = block * rows + move
        return jnp.logical_and(first + rows - 1 >= 0, first < plan.height)

    def loaded(group, taps):
        @pl.when(step == 0)
        def _():
            for copy in weights(group, taps):
                copy.wait()

    def columns(k, first):
        r = RATE * k
        part = [slice(first + i * c_out, first + (i + 1) * c_out) for i in range(3)]
        return (
            res[:, EDGE - r:EDGE - r + cols, part[0]]
            + res[:, EDGE:EDGE + cols, part[1]]
            + res[:, EDGE + r:EDGE + r + cols, part[2]]
        )

    def relu_to(k, value):
        at = plan.direct.index(k)
        catb[:, at * c_out:(at + 1) * c_out] = (
            jnp.maximum(value, 0.0).astype(BF16).reshape(pix, c_out)
        )

    def shifted_copy(at):
        return pltpu.make_async_copy(
            sb.at[at], s_out.at[at, field, pl.ds(block * rows, rows)], sem_s.at[at]
        )

    group = 0
    first = c_out
    loaded(0, plan.loads[0])
    width = len(plan.loads[0]) * c_out
    res[:, EDGE:EDGE + cols, :width] = nn(xbuf[...], wbuf[0, :, :width]).reshape(
        rows, cols, width
    )
    relu_to(0, res[:, EDGE:EDGE + cols, :c_out])
    group = 1
    for k in plan.direct[1:]:
        if first + 3 * c_out > width:
            loaded(group, plan.loads[group])
            width, first = 3 * c_out, 0
            res[:, EDGE:EDGE + cols, :width] = nn(xbuf[...], wbuf[group, :, :width]).reshape(
                rows, cols, width
            )
            group += 1
        relu_to(k, columns(k, first))
        first += 3 * c_out
    cat_copy = pltpu.make_async_copy(catb, cat_out.at[field, block], sem_o.at[1])
    cat_copy.start()
    width = 3 * c_out
    for at, k in enumerate(plan.shifted):
        for a in range(3):
            loaded(group + 3 * at + a, plan.loads[group + 3 * at + a])

        def one(a, _, k=k, at=at, base=group + 3 * at):
            @pl.when(in_field((1 - a) * RATE * k))
            def _():
                res[:, EDGE:EDGE + cols, :width] = nn(
                    xbuf[...], wbuf[base + a, :, :width]
                ).reshape(rows, cols, width)
                sb[3 * at + a] = columns(k, 0)
                shifted_copy(3 * at + a).start()
            return 0

        lax.fori_loop(0, 3, one, 0)
    aux_copy.wait()
    xt_copy.wait()
    cat_copy.wait()
    for at, k in enumerate(plan.shifted):
        for a in range(3):
            @pl.when(in_field((1 - a) * RATE * k))
            def _(at=at, a=a):
                shifted_copy(3 * at + a).wait()


def run_blocks(plan, slots, meta, w_in, state):
    arrays = [value for cands in slots for value in cands]
    n, rows, cols, pix = plan.n, plan.rows, plan.cols, plan.pix
    c_in, c_out, n_sh = plan.c_in, plan.c_out, plan.n_sh
    shapes = [
        jax.ShapeDtypeStruct((2, n, c_in, pix), BF16),
        jax.ShapeDtypeStruct((2, n, pix, len(plan.direct) * c_out), BF16),
        jax.ShapeDtypeStruct((3 * n_sh, 2, n * rows, cols, c_out), F32),
        jax.ShapeDtypeStruct((2, n, EXTRA, c_in), BF16),
    ]
    widest = max(len(g) for g in plan.loads) * c_out
    aliased = state is not None
    operands = [*arrays, w_in] + (list(state) if aliased else [])
    aliases = {1 + len(arrays) + 1 + i: i for i in range(4)} if aliased else {}
    return pl.pallas_call(
        functools.partial(block_kernel, plan, len(arrays), len(slots), aliased),
        grid_spec=pltpu.PrefetchScalarGridSpec(
            num_scalar_prefetch=1,
            grid=(len(slots),),
            in_specs=[pl.BlockSpec(memory_space=pl.ANY)] * len(operands),
            out_specs=[pl.BlockSpec(memory_space=pl.ANY)] * 4,
            scratch_shapes=[
                pltpu.VMEM((2, pix + EXTRA, c_in), BF16),
                pltpu.VMEM((len(plan.loads), c_in, widest), BF16),
                pltpu.VMEM((c_in, pix), BF16),
                pltpu.VMEM((pix, len(plan.direct) * c_out), BF16),
                pltpu.VMEM((3 * n_sh, rows, cols, c_out), F32),
                pltpu.VMEM((rows, cols + 2 * EDGE, widest), F32),
                pltpu.SemaphoreType.DMA((2,)),
                pltpu.SemaphoreType.DMA((len(plan.loads), 4)),
                pltpu.SemaphoreType.DMA((3,)),
                pltpu.SemaphoreType.DMA((3 * n_sh,)),
            ],
        ),
        out_shape=shapes,
        input_output_aliases=aliases,
        compiler_params=pltpu.CompilerParams(
            dimension_semantics=("arbitrary",), vmem_limit_bytes=BLOCK_VMEM
        ),
        cost_estimate=pl.CostEstimate(
            flops=len(slots) * 2 * pix * c_in * c_out * (10 + 6 * n_sh),
            bytes_accessed=20_000_000 + len(slots) * 20_000_000,
            transcendentals=0,
        ),
        name="block_forward",
    )(meta, *operands)


def field_kernel(plan, field, last, tab, *refs):
    n, rows, cols, pix = plan.n, plan.rows, plan.cols, plan.pix
    c_in, c_out, n_sh = plan.c_in, plan.c_out, plan.n_sh
    unit_rows, depth, flags = plan.unit_rows, plan.depth, plan.flags
    cat_ref = refs[0]
    mid_refs = refs[1:1 + n_sh]
    s_hbm = refs[1 + n_sh]
    refs = refs[2 + n_sh:]
    aux_ref, all_ref, w28_ref, wproj_ref, wcls_ref, cw_ref, xt_hbm = refs[:7]
    refs = refs[7:]
    if last:
        prev_g, prev_p, prev_c = refs[:3]
        refs = refs[3:]
    g_out, p_out, c_ref_out = refs[:3]
    side_refs = refs[3:3 + 2 * n_sh]
    (dbuf, pad, mean, ybuf, lbuf, dybuf, gp, spool, pact, catall, acc, stage, xt_ref, sem_xt,
     sems, sem_s) = refs[3 + 2 * n_sh:]
    xt_copy = pltpu.make_async_copy(xt_hbm.at[field], xt_ref, sem_xt)
    step = pl.program_id(0)
    edge_rows = rows - 1

    def finish(value, prev):
        grad = value.astype(BF16)
        if not last:
            return grad
        return (prev.astype(F32) + grad.astype(F32)) * 0.5

    def side_copies():
        copies = []
        for at, k in enumerate(plan.shifted):
            for side in range(2):
                first, count = side * RATE * k, plan.height - RATE * k
                copies.append(pltpu.make_async_copy(
                    s_hbm.at[3 * at + 2 * side, field, pl.ds(first, count)],
                    side_refs[2 * at + side], sem_s.at[2 * at + side],
                ))
        return copies

    @pl.when(step == 0)
    def _():
        for copy in side_copies():
            copy.start()
        xt_copy.start()
        zero = jnp.zeros((edge_rows, cols, dbuf.shape[2]), BF16)
        dbuf[:edge_rows] = zero
        dbuf[edge_rows + plan.height:] = zero
        pad[:, :EDGE, :] = jnp.zeros((rows, EDGE, c_out), F32)
        pad[:, EDGE + cols:, :] = jnp.zeros((rows, EDGE, c_out), F32)
        total = jnp.zeros((1, c_in), F32)
        for j in range(n):
            extra = all_ref[j].astype(F32)
            total = total + ((extra[2:3] + extra[1:2]) + extra[0:1])
        mean_in = (total / plan.total).astype(BF16)
        mean[...] = jnp.broadcast_to(mean_in.astype(F32), (16, c_in))
        pact[...] = nn(mean[...].astype(BF16), w28_ref[0])
        for copy in side_copies():
            copy.wait()

    @pl.when(step < n)
    def _():
        block = step
        cat5 = catall.at[block]
        for k in range(4):
            part = slice(k * c_out, (k + 1) * c_out)
            if k in plan.shifted:
                at = plan.shifted.index(k)
                r = RATE * k
                pre = mid_refs[at]
                for i in range(rows):
                    h = block * rows + i
                    line = pre[i]
                    for side, src in ((0, h - r), (1, h)):
                        last_row = plan.height - r - 1
                        ok = jnp.logical_and(src >= 0, src <= last_row)
                        got = side_refs[2 * at + side][jnp.clip(src, 0, last_row)]
                        line = line + jnp.where(ok, got, 0.0)
                    cat5[i * cols:(i + 1) * cols, part] = jnp.maximum(line, 0.0).astype(BF16)
            else:
                at = plan.direct.index(k)
                cat5[:, part] = cat_ref[:, at * c_out:(at + 1) * c_out]
        pool_act = jnp.maximum(pact[0:1, :], 0.0).astype(BF16)
        cat5[:, 4 * c_out:] = jnp.broadcast_to(pool_act, (pix, c_out))
        y_pre = nn(cat5[...], wproj_ref[...])
        y_act = jnp.maximum(y_pre, 0.0).astype(BF16)
        logits = nt(wcls_ref[...], y_act)
        row = lax.broadcasted_iota(jnp.int32, (16, pix), 0)
        live = row < plan.classes
        expo = jnp.where(live, jnp.exp(logits), 0.0)
        prob = expo / jnp.sum(expo, axis=0, keepdims=True)
        label = jnp.broadcast_to(aux_ref[3:4, :pix].astype(F32), (16, pix))
        onehot = jnp.where(label == row.astype(F32), 1.0, 0.0)
        weight = jnp.zeros((16, pix), F32)
        for c in range(plan.classes):
            weight = jnp.where(label == float(c), cw_ref[c], weight)
        d_logits = jnp.where(
            live, (prob - onehot) * weight * (LOSS_SCALE / plan.total), 0.0
        ).astype(BF16)
        d_y = jnp.where(y_pre > 0, tn(d_logits, wcls_ref[...]), 0.0).astype(BF16)
        ybuf[block] = y_act
        lbuf[block] = d_logits
        dybuf[block] = d_y
        for k in range(4):
            want = [tab[flags + n + 3 * k + b] for b in range(3)]
            part = slice(k * c_out, (k + 1) * c_out)

            @pl.when((want[0] >= 0) | (want[1] >= 0) | (want[2] >= 0))
            def _(k=k, want=want, part=part):
                d_cat = nt(d_y, wproj_ref[part, :])
                d_k = jnp.where(cat5[:, part] > 0, d_cat, 0.0).astype(BF16)
                d_k = d_k.reshape(rows, cols, c_out)
                if k > 0:
                    pad[:, EDGE:EDGE + cols, :] = d_k.astype(F32)
                at = pl.ds(block * rows + edge_rows, rows)
                for b in range(3):
                    if k == 0 and b != 1:
                        continue

                    @pl.when(want[b] >= 0)
                    def _(b=b):
                        lanes = pl.ds(pl.multiple_of(jnp.maximum(want[b], 0) * c_out, c_out), c_out)
                        if b == 1:
                            dbuf[at, :, lanes] = d_k
                        else:
                            first = EDGE + (1 - b) * RATE * k
                            dbuf[at, :, lanes] = pad[:, first:first + cols, :].astype(BF16)

    @pl.when(step == n - 1)
    def _():
        all_dy = dybuf[...].reshape(n * pix, c_out)
        pool = wproj_ref[4 * c_out:, :]
        rest = nn(jnp.ones((16, n * pix), BF16), all_dy)
        total = jnp.zeros(rest.shape, F32)
        for _i in range(3):
            head = rest.astype(BF16)
            total = total + nt(head, pool)
            rest = rest - head.astype(F32)
        spool[...] = jnp.where(pact[...] > 0, jnp.broadcast_to(total[0:1, :], total.shape), 0.0)
        window = pl.ds(pl.multiple_of(tab[flags + n + 13], 128), plan.window)
        g_proj = jnp.zeros((c_out, plan.window), F32)
        g_cls = jnp.zeros((16, c_out), F32)
        for j in range(n):
            g_proj = g_proj + nn(
                nt(identity(c_out), dybuf[j]).astype(BF16), catall[j, :, window]
            )
            g_cls = g_cls + nn(lbuf[j], ybuf[j])
        gp[:plan.window, :] = g_proj.T
        index = tab[flags + n + 12]
        first = pl.multiple_of(index * plan.proj_rows - tab[flags + n + 13], 32)
        p_out[...] = finish(gp[pl.ds(first, plan.proj_rows), :], prev_p[...] if last else None)
        gp[:c_out, :128] = jnp.concatenate([g_cls, jnp.zeros((112, c_out), F32)], axis=0).T
        first = pl.multiple_of(index * plan.cls_rows, plan.cls_rows)
        c_ref_out[...] = finish(
            gp[pl.ds(first, plan.cls_rows), :128], prev_c[...] if last else None
        )

    def out_copy(part, slot, t):
        row = tab[(part * depth + t) * 6 + 5] * unit_rows
        return pltpu.make_async_copy(
            stage.at[slot, t],
            g_out.at[pl.ds(pl.multiple_of(row, unit_rows), unit_rows)],
            sems.at[slot, t],
        )

    @pl.when(step == n)
    def _():
        xt_copy.wait()

    @pl.when(step >= n)
    def _():
        part = step - n
        parity = lax.rem(part, 2)
        mine = pl.ds(pl.multiple_of(part * unit_rows, unit_rows), unit_rows)

        def one(t, _):
            base = (part * depth + t) * 6
            slot, move, low, high = tab[base], tab[base + 1], tab[base + 2], tab[base + 3]
            kind = tab[base + 4]

            def product(taps):
                width = taps * c_out
                lanes = pl.ds(pl.multiple_of(slot * c_out, c_out), width)

                def term(j):
                    first = j * rows - move + edge_rows
                    return nn(xt_ref[j, mine, :], dbuf[pl.ds(first, rows), :, lanes].reshape(pix, width))

                whole = jnp.logical_and(low == 0, high == n)

                @pl.when(whole)
                def _():
                    total = term(0)
                    for j in range(1, n):
                        total = total + term(j)
                    acc[:, :width] = total

                @pl.when(jnp.logical_not(whole))
                def _():
                    acc[:, :width] = jnp.zeros((unit_rows, width), F32)

                    def add(j, _):
                        acc[:, :width] += term(j)
                        return 0

                    lax.fori_loop(low, high, add, 0)

            @pl.when(kind == 3)
            def _():
                product(3)

            @pl.when(kind == 0)
            def _():
                product(1)

            @pl.when(kind == 2)
            def _():
                acc[:, :c_out] = jnp.zeros((unit_rows, c_out), F32)

            @pl.when(kind == 1)
            def _():
                first = pl.multiple_of(part * unit_rows, unit_rows)
                row = mean[0:1, pl.ds(first, unit_rows)]
                column = jnp.broadcast_to(row, (128, unit_rows)).T
                for c in range(c_out // 128):
                    lanes = slice(c * 128, (c + 1) * 128)
                    acc[:, lanes] = column * spool[0:1, lanes]

            def emit(at, lanes):
                if last:
                    stage[parity, at] = finish(acc[:, lanes], prev_g[at])
                    out_copy(part, parity, at).start()
                else:
                    g_out[at] = finish(acc[:, lanes], None)

            @pl.when(kind != 4)
            def _():
                emit(t, slice(0, c_out))

            @pl.when(kind == 3)
            def _():
                for b in (1, 2):
                    emit(t + b, slice(b * c_out, (b + 1) * c_out))

            return 0

        lax.fori_loop(0, tab[flags + part], one, 0)

        if last:
            def drain(which, slot):
                def one(t, _):
                    out_copy(which, slot, t).wait()
                    return 0
                lax.fori_loop(0, tab[flags + which], one, 0)

            @pl.when(part > 0)
            def _():
                drain(part - 1, 1 - parity)

            @pl.when(part == n - 1)
            def _():
                drain(part, parity)


def run_field(plan, field, tab, state, w_in, w_proj, wcls, cw, prev):
    n, rows, cols, pix = plan.n, plan.rows, plan.cols, plan.pix
    c_in, c_out, n_sh = plan.c_in, plan.c_out, plan.n_sh
    unit_rows, depth = plan.unit_rows, plan.depth
    last = prev is not None
    xt, cat, s, aux = state

    def blk(i):
        return jnp.minimum(i, n - 1)

    def part(i):
        return jnp.maximum(i - n, 0)

    in_specs = [
        pl.BlockSpec(
            (None, None, pix, len(plan.direct) * c_out), lambda i, t: (field, blk(i), 0, 0)
        ),
    ]
    operands = [cat]
    for at in range(n_sh):
        in_specs.append(pl.BlockSpec(
            (None, None, rows, cols, c_out),
            lambda i, t, at=at: (3 * at + 1, field, blk(i), 0, 0),
        ))
        operands.append(s)
    in_specs.append(pl.BlockSpec(memory_space=pl.ANY))
    operands.append(s)
    in_specs += [
        pl.BlockSpec((None, None, EXTRA, c_in), lambda i, t: (field, blk(i), 0, 0)),
        pl.BlockSpec((None, n, EXTRA, c_in), lambda i, t: (field, 0, 0, 0)),
        pl.BlockSpec((1, c_in, c_out), lambda i, t: (28, 0, 0)),
        pl.BlockSpec((5 * c_out, c_out), lambda i, t: (0, 0)),
        pl.BlockSpec((16, c_out), lambda i, t: (0, 0)),
        pl.BlockSpec(memory_space=pltpu.SMEM),
        pl.BlockSpec(memory_space=pl.ANY),
    ]
    operands += [aux, aux, w_in, w_proj, wcls, cw, xt]
    kind = F32 if last else BF16
    inner = pl.BlockSpec((None, depth, unit_rows, c_out), lambda i, t: (part(i), 0, 0, 0))
    small = [
        pl.BlockSpec((plan.proj_rows, c_out), lambda i, t: (0, 0)),
        pl.BlockSpec((plan.cls_rows, 128), lambda i, t: (0, 0)),
    ]
    if last:
        in_specs += [inner] + small
        operands += list(prev)
        main_spec = pl.BlockSpec(memory_space=pl.ANY)
        main_shape = jax.ShapeDtypeStruct((plan.units * unit_rows, c_out), F32)
    else:
        main_spec = inner
        main_shape = jax.ShapeDtypeStruct((n, depth, unit_rows, c_out), BF16)
    return pl.pallas_call(
        functools.partial(field_kernel, plan, field, last),
        grid_spec=pltpu.PrefetchScalarGridSpec(
            num_scalar_prefetch=1,
            grid=(2 * n,),
            in_specs=in_specs,
            out_specs=[main_spec] + small,
            scratch_shapes=[
                pltpu.VMEM((plan.height - RATE * k, cols, c_out), F32)
                for k in plan.shifted for _ in range(2)
            ] + [
                pltpu.VMEM((plan.height + 2 * (rows - 1), cols, plan.n_slots * c_out), BF16),
                pltpu.VMEM((rows, cols + 2 * EDGE, c_out), F32),
                pltpu.VMEM((16, c_in), F32),
                pltpu.VMEM((n, pix, c_out), BF16),
                pltpu.VMEM((n, 16, pix), BF16),
                pltpu.VMEM((n, pix, c_out), BF16),
                pltpu.VMEM((max(plan.window, c_out), c_out), F32),
                pltpu.VMEM((16, c_out), F32),
                pltpu.VMEM((16, c_out), F32),
                pltpu.VMEM((n, pix, 5 * c_out), BF16),
                pltpu.VMEM((unit_rows, 3 * c_out), F32),
                pltpu.VMEM((2, depth if last else 1, unit_rows, c_out), F32),
                pltpu.VMEM((n, c_in, pix), BF16),
                pltpu.SemaphoreType.DMA,
                pltpu.SemaphoreType.DMA((2, depth)),
                pltpu.SemaphoreType.DMA((2 * n_sh,)),
            ],
        ),
        out_shape=[
            main_shape,
            jax.ShapeDtypeStruct((plan.proj_rows, c_out), kind),
            jax.ShapeDtypeStruct((plan.cls_rows, 128), kind),
        ],
        compiler_params=pltpu.CompilerParams(
            dimension_semantics=("arbitrary",), vmem_limit_bytes=FIELD_VMEM
        ),
        cost_estimate=pl.CostEstimate(
            flops=10_000_000_000, bytes_accessed=90_000_000, transcendentals=0
        ),
        name="field_grads",
    )(tab, *operands)


def after(value, *others):
    return lax.optimization_barrier((value, *others))[0]


def per_device(plan, features, labels, w_in, w_proj, w_cls, class_weight, matching):
    n, reps, rows, pix, c_in = plan.n, plan.reps, plan.rows, plan.pix, plan.c_in
    names = jnp.pad(labels[0].reshape(1, pix).astype(F32), ((0, 0), (0, c_in - pix)))
    x = pl.pallas_call(
        functools.partial(pack_kernel, pix),
        out_shape=jax.ShapeDtypeStruct((pix + EXTRA, c_in), BF16),
        name="pack",
    )(features[0].reshape(pix, c_in), names)
    here = lax.axis_index("space")
    n_bits = reps.bit_length() - 1
    bits = [jnp.bitwise_and(jnp.right_shift(matching[0], b), 1) == 1 for b in range(n_bits)]
    top = jnp.int32(0)
    for at, b in enumerate(list(range(1, n_bits)) + [0]):
        top = jnp.where(bits[b], n_bits - 1 - at, top)
    tab = jnp.asarray(plan.tables)[here]
    wcls = jnp.pad(w_cls.T, ((0, 16 - plan.classes), (0, 0)))

    def along(value, way, step):
        pairs = [
            (i, i + way) for i in range(n)
            if 0 <= i + way < n and 0 <= i - way * (step - 1) < n
        ]
        return lax.ppermute(value, "space", pairs)

    def hop(value, b):
        return lax.ppermute(value, "rep", [(r, r ^ (1 << b)) for r in range(reps)])

    order = np.array(
        [sorted(range(n), key=lambda j: (abs(j - s), j)) for s in range(n)], np.int32
    )
    blocks = jnp.asarray(order)[here]

    def arrival(q, ups, downs):
        value = None
        for s in range(n):
            j = int(order[s, q])
            arrived = ups[s - j] if j < s else downs[j - s]
            value = arrived if value is None else jnp.where(here == s, arrived, value)
        return value

    common = (w_in, w_proj, wcls, class_weight)
    hops = list(range(1, n_bits)) + [0]
    rounds = n + n_bits - 1
    ups, downs, raw = [x], [x], (x, x)
    turns = []
    for t in range(1, rounds + 1):
        turn = [(t - 1, 0)] if t - 1 < n else []
        if t == rounds:
            turn += [(q, 1) for q in range(max(0, n + 1 - n_bits), n)]
        elif t >= n_bits and t <= n:
            turn.append((t - n_bits, 1))
        turns.append(turn)
    metas = [
        jnp.stack([
            jnp.stack([(top if f else 0) + jnp.int32(n_bits * at if f and turn[0][1] else at),
                       blocks[q], jnp.int32(f)])
            for at, (q, f) in enumerate(turn)
        ]) if turn else None
        for turn in turns
    ]
    values, moves = {0: x}, {q: [] for q in range(n)}
    state, grads = None, None
    for t in range(1, rounds + 1):
        q = t - 1
        if 0 < q < n:
            values[q] = arrival(q, ups, downs)
        for i in range(1, n_bits):
            if 0 <= q - i < n:
                values[q - i] = jnp.where(bits[hops[i - 1]], moves[q - i][0], values[q - i])
        for i in reversed(range(n_bits)):
            if 0 <= q - i < n:
                moves[q - i].insert(0, hop(values[q - i], hops[i]))
        if t < n:
            raw = along(raw[0], 1, t), along(raw[1], -1, t)
            ups.append(raw[0])
            downs.append(raw[1])
        slots = [moves[at] if f else [values[at]] for at, f in turns[q]]
        if slots:
            state = run_blocks(plan, slots, metas[q], w_in, state)
        if q == min(n, rounds - 1):
            grads = tuple(run_field(plan, 0, tab, state, *common, None))
        if t < rounds:
            live = (ups, downs, values, moves, state, grads, metas, tab, wcls)
            live = lax.optimization_barrier(live)
            ups, downs, values, moves, state, grads, metas, tab, wcls = live
    avg_in, avg_proj, avg_cls = run_field(plan, 1, tab, state, *common, grads)
    return avg_in[None], avg_proj[None], avg_cls[None, :, :plan.classes]


def solution(mesh):
    n, reps = mesh.shape["space"], mesh.shape["rep"]

    def build(features, labels, w_in, w_proj, w_cls, class_weight, matching):
        _, rows, cols, c_in = features.shape
        plan = Plan(n, reps, rows // n, cols, c_in, w_proj.shape[1], w_cls.shape[1])
        return jax.shard_map(
            functools.partial(per_device, plan),
            mesh=mesh,
            in_specs=(P("rep", "space", None, None), P("rep", "space", None), P(), P(), P(), P(), P()),
            out_specs=(P("rep", "space", None), P("rep", "space", None), P("rep", "space", None)),
            check_vma=False,
        )(features, labels, w_in, w_proj, w_cls, class_weight, matching)

    return build
```

```python
import functools

import jax
import jax.numpy as jnp
import numpy as np
from jax import lax
from jax.experimental import pallas as pl
from jax.experimental.pallas import tpu as pltpu
from jax.sharding import PartitionSpec as P

LOSS_SCALE = 1024.0
RATE = 12
EDGE = 40
EXTRA = 16
BF16 = jnp.bfloat16
F32 = jnp.float32
BLOCK_VMEM = 50 * 1024 * 1024
FIELD_VMEM = 50 * 1024 * 1024


def nn(a, b):
    return lax.dot_general(a, b, (((1,), (0,)), ((), ())), preferred_element_type=F32)


def nt(a, b):
    return lax.dot_general(a, b, (((1,), (1,)), ((), ())), preferred_element_type=F32)


def tn(a, b):
    return lax.dot_general(a, b, (((0,), (0,)), ((), ())), preferred_element_type=F32)


def identity(size):
    rows = lax.broadcasted_iota(jnp.int32, (size, size), 0)
    cols = lax.broadcasted_iota(jnp.int32, (size, size), 1)
    return (rows == cols).astype(F32).astype(BF16)


class Plan:
    def __init__(self, n, reps, rows, cols, c_in, c_out, classes):
        self.n, self.reps, self.rows, self.cols = n, reps, rows, cols
        self.c_in, self.c_out, self.classes = c_in, c_out, classes
        self.height = rows * n
        self.pix = rows * cols
        self.total = self.pix * n
        self.shifted = [k for k in (1, 2, 3) if RATE * k < self.height]
        self.direct = [k for k in range(4) if k not in self.shifted]
        self.n_sh = len(self.shifted)
        self.together = 2 if n % 2 == 0 and self.n_sh == 1 else 1
        row = lambda k, a: [1 + 9 * (k - 1) + 3 * a + b for b in range(3)]
        still = [row(k, 1) for k in self.direct[1:]]
        self.loads = [[0] + (still[0] if still else [])] + still[1:]
        for k in self.shifted:
            self.loads += [row(k, a) for a in range(3)]
        self.units = 29
        self.unit_rows = c_in // n
        self.proj_rows = 5 * c_out // n
        self.cls_rows = c_out // n
        starts = [self.proj_rows * s // 128 * 128 for s in range(n)]
        ends = [-(-self.proj_rows * (s + 1) // 128) * 128 for s in range(n)]
        self.window = max(e - b for b, e in zip(starts, ends))
        self.starts = [min(b, 5 * c_out - self.window) for b in starts]
        tables = [self.table(s) for s in range(n)]
        self.n_slots = max(t[1] for t in tables)
        self.depth = max(t[2] for t in tables)
        self.tables = np.array([
            sum((c + [[0] * 6] * (self.depth - len(c)) for c in t[0]), []) for t in tables
        ], np.int32).reshape(n, -1)
        self.flags = self.tables.shape[1]
        self.tables = np.concatenate([
            self.tables,
            np.array([
                [len(c) for c in t[0]] + t[3] + [s, self.starts[s]] for s, t in enumerate(tables)
            ], np.int32),
        ], axis=1)

    def tap(self, t):
        if t == 0:
            return (0, 1, 1)
        if t == 28:
            return None
        k, rest = (t - 1) // 9 + 1, (t - 1) % 9
        a, b = rest // 3, rest % 3
        if a != 1 and k not in self.shifted:
            return "zero"
        return (k, a, b)

    def table(self, s):
        parts = [[] for _ in range(self.n)]
        here = range(s * self.units, (s + 1) * self.units)
        slots = {}
        for k in range(4):
            for b in ((1,) if k == 0 else range(3)):
                if any(
                    isinstance(self.tap(u // self.n), tuple)
                    and (self.tap(u // self.n)[0], self.tap(u // self.n)[2]) == (k, b)
                    for u in here
                ):
                    slots[(k, b)] = len(slots)
        for unit in here:
            c, tap = unit % self.n, self.tap(unit // self.n)
            local = unit - s * self.units
            if tap is None or tap == "zero":
                parts[c].append([0, 0, 0, 0, 1 if tap is None else 2, local])
                continue
            k, a, b = tap
            move = (a - 1) * RATE * k
            valid = [
                j for j in range(self.n)
                if any(0 <= self.rows * j + i - move < self.height for i in range(self.rows))
            ]
            entry = [slots[(k, b)], move, valid[0], valid[-1] + 1, 0, local]
            if b == 2 and len(parts[c]) > 1 and all(
                e[4] == 0 and e[:4] == [entry[0] - back] + entry[1:4]
                for back, e in ((1, parts[c][-1]), (2, parts[c][-2]))
            ):
                parts[c][-2][4] = 3
                parts[c][-1][4] = 4
                entry[4] = 4
            parts[c].append(entry)
        want = [slots.get((k, b), -1) for k in range(4) for b in range(3)]
        return parts, len(slots), max(len(c) for c in parts), want


def pack_kernel(pix, x_ref, lab_ref, out_ref):
    x = x_ref[...]
    out_ref[:pix, :] = x
    total = jnp.sum(x.astype(F32), axis=0, keepdims=True)
    head = total.astype(BF16).astype(F32)
    mid = (total - head).astype(BF16).astype(F32)
    row = lax.broadcasted_iota(jnp.int32, (EXTRA, x.shape[1]), 0)
    extra = jnp.zeros((EXTRA, x.shape[1]), F32)
    for at, value in enumerate((head, mid, total - head - mid, lab_ref[...])):
        extra = jnp.where(row == at, value, extra)
    out_ref[pix:, :] = extra.astype(BF16)


def block_kernel(plan, n_cand, n_slots, aliased, meta, *refs):
    rows, cols, c_in, c_out = plan.rows, plan.cols, plan.c_in, plan.c_out
    pix = plan.pix
    cands = refs[:n_cand]
    w_hbm = refs[n_cand]
    refs = refs[n_cand + 1 + (4 if aliased else 0):]
    xt_out, cat_out, s_out, aux_out = refs[:4]
    xin, wbuf, xtb, catb, sb, res, sem_x, sem_w, sem_o, sem_s = refs[4:]
    step = pl.program_id(0)
    block, field = meta[step, 1], meta[step, 2]
    now = lax.rem(step, 2)
    xbuf = xin.at[now, pl.ds(0, pix)]

    def fetch(at, slot):
        for c in range(n_cand):
            @pl.when(meta[at, 0] == c)
            def _(c=c):
                pltpu.make_async_copy(cands[c], xin.at[slot], sem_x.at[slot]).start()

    def weights(group, taps):
        return [
            pltpu.make_async_copy(
                w_hbm.at[tap], wbuf.at[group, :, pl.ds(i * c_out, c_out)], sem_w.at[group, i]
            )
            for i, tap in enumerate(taps)
        ]

    @pl.when(step == 0)
    def _():
        fetch(0, 0)
        for group, taps in enumerate(plan.loads):
            for copy in weights(group, taps):
                copy.start()
        res[:, :EDGE, :] = jnp.zeros((rows, EDGE, res.shape[2]), F32)
        res[:, EDGE + cols:, :] = jnp.zeros((rows, EDGE, res.shape[2]), F32)

    if n_slots > 1:
        @pl.when(step + 1 < n_slots)
        def _():
            fetch(step + 1, 1 - now)

    pltpu.make_async_copy(cands[0], xin.at[now], sem_x.at[now]).wait()
    aux_copy = pltpu.make_async_copy(
        xin.at[now, pl.ds(pix, EXTRA)], aux_out.at[field, block], sem_o.at[2]
    )
    aux_copy.start()
    eye = identity(256)
    for c in range(c_in // 256):
        part = slice(c * 256, (c + 1) * 256)
        xtb[part, :] = nt(eye, xbuf[:, part]).astype(BF16)
    xt_copy = pltpu.make_async_copy(xtb, xt_out.at[field, block], sem_o.at[0])
    xt_copy.start()

    def in_field(move):
        first = block * rows + move
        return jnp.logical_and(first + rows - 1 >= 0, first < plan.height)

    def loaded(group, taps):
        @pl.when(step == 0)
        def _():
            for copy in weights(group, taps):
                copy.wait()

    def columns(k, first):
        r = RATE * k
        part = [slice(first + i * c_out, first + (i + 1) * c_out) for i in range(3)]
        return (
            res[:, EDGE - r:EDGE - r + cols, part[0]]
            + res[:, EDGE:EDGE + cols, part[1]]
            + res[:, EDGE + r:EDGE + r + cols, part[2]]
        )

    def relu_to(k, value):
        at = plan.direct.index(k)
        catb[:, at * c_out:(at + 1) * c_out] = (
            jnp.maximum(value, 0.0).astype(BF16).reshape(pix, c_out)
        )

    def shifted_copy(at):
        return pltpu.make_async_copy(
            sb.at[at], s_out.at[at, field, pl.ds(block * rows, rows)], sem_s.at[at]
        )

    group = 0
    first = c_out
    loaded(0, plan.loads[0])
    width = len(plan.loads[0]) * c_out
    res[:, EDGE:EDGE + cols, :width] = nn(xbuf[...], wbuf[0, :, :width]).reshape(
        rows, cols, width
    )
    relu_to(0, res[:, EDGE:EDGE + cols, :c_out])
    group = 1
    for k in plan.direct[1:]:
        if first + 3 * c_out > width:
            loaded(group, plan.loads[group])
            width, first = 3 * c_out, 0
            res[:, EDGE:EDGE + cols, :width] = nn(xbuf[...], wbuf[group, :, :width]).reshape(
                rows, cols, width
            )
            group += 1
        relu_to(k, columns(k, first))
        first += 3 * c_out
    cat_copy = pltpu.make_async_copy(catb, cat_out.at[field, block], sem_o.at[1])
    cat_copy.start()
    width = 3 * c_out
    for at, k in enumerate(plan.shifted):
        for a in range(3):
            loaded(group + 3 * at + a, plan.loads[group + 3 * at + a])

        def one(a, _, k=k, at=at, base=group + 3 * at):
            @pl.when(in_field((1 - a) * RATE * k))
            def _():
                res[:, EDGE:EDGE + cols, :width] = nn(
                    xbuf[...], wbuf[base + a, :, :width]
                ).reshape(rows, cols, width)
                sb[3 * at + a] = columns(k, 0)
                shifted_copy(3 * at + a).start()
            return 0

        lax.fori_loop(0, 3, one, 0)
    aux_copy.wait()
    xt_copy.wait()
    cat_copy.wait()
    for at, k in enumerate(plan.shifted):
        for a in range(3):
            @pl.when(in_field((1 - a) * RATE * k))
            def _(at=at, a=a):
                shifted_copy(3 * at + a).wait()


def run_blocks(plan, slots, meta, w_in, state):
    arrays = [value for cands in slots for value in cands]
    n, rows, cols, pix = plan.n, plan.rows, plan.cols, plan.pix
    c_in, c_out, n_sh = plan.c_in, plan.c_out, plan.n_sh
    shapes = [
        jax.ShapeDtypeStruct((2, n, c_in, pix), BF16),
        jax.ShapeDtypeStruct((2, n, pix, len(plan.direct) * c_out), BF16),
        jax.ShapeDtypeStruct((3 * n_sh, 2, n * rows, cols, c_out), F32),
        jax.ShapeDtypeStruct((2, n, EXTRA, c_in), BF16),
    ]
    widest = max(len(g) for g in plan.loads) * c_out
    aliased = state is not None
    operands = [*arrays, w_in] + (list(state) if aliased else [])
    aliases = {1 + len(arrays) + 1 + i: i for i in range(4)} if aliased else {}
    return pl.pallas_call(
        functools.partial(block_kernel, plan, len(arrays), len(slots), aliased),
        grid_spec=pltpu.PrefetchScalarGridSpec(
            num_scalar_prefetch=1,
            grid=(len(slots),),
            in_specs=[pl.BlockSpec(memory_space=pl.ANY)] * len(operands),
            out_specs=[pl.BlockSpec(memory_space=pl.ANY)] * 4,
            scratch_shapes=[
                pltpu.VMEM((2, pix + EXTRA, c_in), BF16),
                pltpu.VMEM((len(plan.loads), c_in, widest), BF16),
                pltpu.VMEM((c_in, pix), BF16),
                pltpu.VMEM((pix, len(plan.direct) * c_out), BF16),
                pltpu.VMEM((3 * n_sh, rows, cols, c_out), F32),
                pltpu.VMEM((rows, cols + 2 * EDGE, widest), F32),
                pltpu.SemaphoreType.DMA((2,)),
                pltpu.SemaphoreType.DMA((len(plan.loads), 4)),
                pltpu.SemaphoreType.DMA((3,)),
                pltpu.SemaphoreType.DMA((3 * n_sh,)),
            ],
        ),
        out_shape=shapes,
        input_output_aliases=aliases,
        compiler_params=pltpu.CompilerParams(
            dimension_semantics=("arbitrary",), vmem_limit_bytes=BLOCK_VMEM
        ),
        cost_estimate=pl.CostEstimate(
            flops=len(slots) * 2 * pix * c_in * c_out * (10 + 6 * n_sh),
            bytes_accessed=20_000_000 + len(slots) * 20_000_000,
            transcendentals=0,
        ),
        name="block_forward",
    )(meta, *operands)


def field_kernel(plan, field, last, tab, *refs):
    n, rows, cols, pix = plan.n, plan.rows, plan.cols, plan.pix
    c_in, c_out, n_sh = plan.c_in, plan.c_out, plan.n_sh
    unit_rows, depth, flags = plan.unit_rows, plan.depth, plan.flags
    cat_ref = refs[0]
    mid_refs = refs[1:1 + n_sh]
    s_hbm = refs[1 + n_sh]
    refs = refs[2 + n_sh:]
    aux_ref, all_ref, w28_ref, wproj_ref, wturn_ref, wcls_ref, cw_ref, xt_hbm = refs[:8]
    refs = refs[8:]
    if last:
        prev_g, prev_p, prev_c = refs[:3]
        refs = refs[3:]
    g_out, p_out, c_ref_out = refs[:3]
    side_refs = refs[3:3 + 2 * n_sh]
    (dbuf, pad, mean, ybuf, lbuf, dybuf, gp, spool, pact, catall, acc, stage, xt_ref, sem_xt,
     sems, sem_s) = refs[3 + 2 * n_sh:]
    xt_copy = pltpu.make_async_copy(xt_hbm.at[field], xt_ref, sem_xt)
    step = pl.program_id(0)
    edge_rows = rows - 1
    nb, turns = plan.together, n // plan.together

    def finish(value, prev):
        grad = value.astype(BF16)
        if not last:
            return grad
        return (prev.astype(F32) + grad.astype(F32)) * 0.5

    def side_copies():
        copies = []
        for at, k in enumerate(plan.shifted):
            for side in range(2):
                first, count = side * RATE * k, plan.height - RATE * k
                copies.append(pltpu.make_async_copy(
                    s_hbm.at[3 * at + 2 * side, field, pl.ds(first, count)],
                    side_refs[2 * at + side], sem_s.at[2 * at + side],
                ))
        return copies

    @pl.when(step == 0)
    def _():
        for copy in side_copies():
            copy.start()
        xt_copy.start()
        zero = jnp.zeros((edge_rows, cols, dbuf.shape[2]), BF16)
        dbuf[:edge_rows] = zero
        dbuf[edge_rows + plan.height:] = zero
        pad[:, :EDGE, :] = jnp.zeros((nb * rows, EDGE, c_out), F32)
        pad[:, EDGE + cols:, :] = jnp.zeros((nb * rows, EDGE, c_out), F32)
        total = jnp.zeros((1, c_in), F32)
        for j in range(n):
            extra = all_ref[j].astype(F32)
            total = total + ((extra[2:3] + extra[1:2]) + extra[0:1])
        mean_in = (total / plan.total).astype(BF16)
        mean[...] = jnp.broadcast_to(mean_in.astype(F32), (16, c_in))
        pact[...] = nn(mean[...].astype(BF16), w28_ref[0])
        for copy in side_copies():
            copy.wait()

    @pl.when(step < turns)
    def _():
        cat5 = catall.at[step]
        for k in range(4):
            part = slice(k * c_out, (k + 1) * c_out)
            if k in plan.shifted:
                at = plan.shifted.index(k)
                r = RATE * k
                pre = mid_refs[at]
                for i in range(nb * rows):
                    h = step * nb * rows + i
                    line = pre[i]
                    for side, src in ((0, h - r), (1, h)):
                        last_row = plan.height - r - 1
                        ok = jnp.logical_and(src >= 0, src <= last_row)
                        got = side_refs[2 * at + side][jnp.clip(src, 0, last_row)]
                        line = line + jnp.where(ok, got, 0.0)
                    cat5[i * cols:(i + 1) * cols, part] = jnp.maximum(line, 0.0).astype(BF16)
            else:
                at = plan.direct.index(k)
                cat5[:, part] = cat_ref[:, :, at * c_out:(at + 1) * c_out].reshape(nb * pix, c_out)
        pool_act = jnp.maximum(pact[0:1, :], 0.0).astype(BF16)
        cat5[:, 4 * c_out:] = jnp.broadcast_to(pool_act, (nb * pix, c_out))
        y_pre = nn(cat5[...], wproj_ref[...])
        y_act = jnp.maximum(y_pre, 0.0).astype(BF16)
        ybuf[step] = y_act
        row = lax.broadcasted_iota(jnp.int32, (16, pix), 0)
        live = row < plan.classes
        for sub in range(nb):
            cells = slice(sub * pix, (sub + 1) * pix)
            logits = nt(wcls_ref[...], y_act[cells])
            expo = jnp.where(live, jnp.exp(logits), 0.0)
            prob = expo / jnp.sum(expo, axis=0, keepdims=True)
            label = jnp.broadcast_to(aux_ref[sub, 3:4, :pix].astype(F32), (16, pix))
            onehot = jnp.where(label == row.astype(F32), 1.0, 0.0)
            weight = jnp.zeros((16, pix), F32)
            for c in range(plan.classes):
                weight = jnp.where(label == float(c), cw_ref[c], weight)
            d_logits = jnp.where(
                live, (prob - onehot) * weight * (LOSS_SCALE / plan.total), 0.0
            ).astype(BF16)
            lbuf[step * nb + sub] = d_logits
            dybuf[step, cells] = jnp.where(
                y_pre[cells] > 0, tn(d_logits, wcls_ref[...]), 0.0
            ).astype(BF16)
        d_y = dybuf[step]
        for k in range(4):
            want = [tab[flags + n + 3 * k + b] for b in range(3)]
            part = slice(k * c_out, (k + 1) * c_out)

            @pl.when((want[0] >= 0) | (want[1] >= 0) | (want[2] >= 0))
            def _(k=k, want=want, part=part):
                d_cat = nn(d_y, wturn_ref[:, part])
                d_k = jnp.where(cat5[:, part] > 0, d_cat, 0.0).astype(BF16)
                d_k = d_k.reshape(nb * rows, cols, c_out)
                if k > 0:
                    pad[:, EDGE:EDGE + cols, :] = d_k.astype(F32)
                at = pl.ds(step * nb * rows + edge_rows, nb * rows)
                for b in range(3):
                    if k == 0 and b != 1:
                        continue

                    @pl.when(want[b] >= 0)
                    def _(b=b):
                        lanes = pl.ds(pl.multiple_of(jnp.maximum(want[b], 0) * c_out, c_out), c_out)
                        if b == 1:
                            dbuf[at, :, lanes] = d_k
                        else:
                            first = EDGE + (1 - b) * RATE * k
                            dbuf[at, :, lanes] = pad[:, first:first + cols, :].astype(BF16)

    @pl.when(step == turns - 1)
    def _():
        all_dy = dybuf[...].reshape(n * pix, c_out)
        pool = wproj_ref[4 * c_out:, :]
        rest = nn(jnp.ones((16, n * pix), BF16), all_dy)
        total = jnp.zeros(rest.shape, F32)
        for _i in range(3):
            head = rest.astype(BF16)
            total = total + nt(head, pool)
            rest = rest - head.astype(F32)
        spool[...] = jnp.where(pact[...] > 0, jnp.broadcast_to(total[0:1, :], total.shape), 0.0)
        window = pl.ds(pl.multiple_of(tab[flags + n + 13], 128), plan.window)
        g_proj = jnp.zeros((c_out, plan.window), F32)
        g_cls = jnp.zeros((16, c_out), F32)
        for j in range(turns):
            g_proj = g_proj + nn(
                nt(identity(c_out), dybuf[j]).astype(BF16), catall[j, :, window]
            )
        for j in range(n):
            cells = slice(j % nb * pix, (j % nb + 1) * pix)
            g_cls = g_cls + nn(lbuf[j], ybuf[j // nb, cells])
        gp[:plan.window, :] = g_proj.T
        index = tab[flags + n + 12]
        first = pl.multiple_of(index * plan.proj_rows - tab[flags + n + 13], 32)
        p_out[...] = finish(gp[pl.ds(first, plan.proj_rows), :], prev_p[...] if last else None)
        gp[:c_out, :128] = jnp.concatenate([g_cls, jnp.zeros((112, c_out), F32)], axis=0).T
        first = pl.multiple_of(index * plan.cls_rows, plan.cls_rows)
        c_ref_out[...] = finish(
            gp[pl.ds(first, plan.cls_rows), :128], prev_c[...] if last else None
        )

    def out_copy(part, slot, t):
        row = tab[(part * depth + t) * 6 + 5] * unit_rows
        return pltpu.make_async_copy(
            stage.at[slot, t],
            g_out.at[pl.ds(pl.multiple_of(row, unit_rows), unit_rows)],
            sems.at[slot, t],
        )

    @pl.when(step == turns)
    def _():
        xt_copy.wait()

    @pl.when(step >= turns)
    def _():
        part = step - turns
        parity = lax.rem(part, 2)
        mine = pl.ds(pl.multiple_of(part * unit_rows, unit_rows), unit_rows)

        def one(t, _):
            base = (part * depth + t) * 6
            slot, move, low, high = tab[base], tab[base + 1], tab[base + 2], tab[base + 3]
            kind = tab[base + 4]

            def product(taps):
                width = taps * c_out
                lanes = pl.ds(pl.multiple_of(slot * c_out, c_out), width)

                def term(j):
                    first = j * rows - move + edge_rows
                    return nn(xt_ref[j, mine, :], dbuf[pl.ds(first, rows), :, lanes].reshape(pix, width))

                whole = jnp.logical_and(low == 0, high == n)

                @pl.when(whole)
                def _():
                    total = term(0)
                    for j in range(1, n):
                        total = total + term(j)
                    acc[:, :width] = total

                @pl.when(jnp.logical_not(whole))
                def _():
                    acc[:, :width] = jnp.zeros((unit_rows, width), F32)

                    def add(j, _):
                        acc[:, :width] += term(j)
                        return 0

                    lax.fori_loop(low, high, add, 0)

            @pl.when(kind == 3)
            def _():
                product(3)

            @pl.when(kind == 0)
            def _():
                product(1)

            @pl.when(kind == 2)
            def _():
                acc[:, :c_out] = jnp.zeros((unit_rows, c_out), F32)

            @pl.when(kind == 1)
            def _():
                first = pl.multiple_of(part * unit_rows, unit_rows)
                row = mean[0:1, pl.ds(first, unit_rows)]
                column = jnp.broadcast_to(row, (128, unit_rows)).T
                for c in range(c_out // 128):
                    lanes = slice(c * 128, (c + 1) * 128)
                    acc[:, lanes] = column * spool[0:1, lanes]

            def emit(at, lanes):
                if last:
                    stage[parity, at] = finish(acc[:, lanes], prev_g[at])
                    out_copy(part, parity, at).start()
                else:
                    g_out[at] = finish(acc[:, lanes], None)

            @pl.when(kind != 4)
            def _():
                emit(t, slice(0, c_out))

            @pl.when(kind == 3)
            def _():
                for b in (1, 2):
                    emit(t + b, slice(b * c_out, (b + 1) * c_out))

            return 0

        lax.fori_loop(0, tab[flags + part], one, 0)

        if last:
            def drain(which, slot):
                def one(t, _):
                    out_copy(which, slot, t).wait()
                    return 0
                lax.fori_loop(0, tab[flags + which], one, 0)

            @pl.when(part > 0)
            def _():
                drain(part - 1, 1 - parity)

            @pl.when(part == n - 1)
            def _():
                drain(part, parity)


def run_field(plan, field, tab, state, w_in, w_proj, w_turn, wcls, cw, prev):
    n, rows, cols, pix = plan.n, plan.rows, plan.cols, plan.pix
    c_in, c_out, n_sh = plan.c_in, plan.c_out, plan.n_sh
    unit_rows, depth = plan.unit_rows, plan.depth
    last = prev is not None
    nb, turns = plan.together, n // plan.together
    xt, cat, s, aux = state

    def blk(i):
        return jnp.minimum(i, turns - 1)

    def part(i):
        return jnp.maximum(i - turns, 0)

    in_specs = [
        pl.BlockSpec(
            (None, nb, pix, len(plan.direct) * c_out), lambda i, t: (field, blk(i), 0, 0)
        ),
    ]
    operands = [cat]
    for at in range(n_sh):
        in_specs.append(pl.BlockSpec(
            (None, None, nb * rows, cols, c_out),
            lambda i, t, at=at: (3 * at + 1, field, blk(i), 0, 0),
        ))
        operands.append(s)
    in_specs.append(pl.BlockSpec(memory_space=pl.ANY))
    operands.append(s)
    in_specs += [
        pl.BlockSpec((None, nb, EXTRA, c_in), lambda i, t: (field, blk(i), 0, 0)),
        pl.BlockSpec((None, n, EXTRA, c_in), lambda i, t: (field, 0, 0, 0)),
        pl.BlockSpec((1, c_in, c_out), lambda i, t: (28, 0, 0)),
        pl.BlockSpec((5 * c_out, c_out), lambda i, t: (0, 0)),
        pl.BlockSpec((c_out, 4 * c_out), lambda i, t: (0, 0)),
        pl.BlockSpec((16, c_out), lambda i, t: (0, 0)),
        pl.BlockSpec(memory_space=pltpu.SMEM),
        pl.BlockSpec(memory_space=pl.ANY),
    ]
    operands += [aux, aux, w_in, w_proj, w_turn, wcls, cw, xt]
    kind = F32 if last else BF16
    inner = pl.BlockSpec((None, depth, unit_rows, c_out), lambda i, t: (part(i), 0, 0, 0))
    small = [
        pl.BlockSpec((plan.proj_rows, c_out), lambda i, t: (0, 0)),
        pl.BlockSpec((plan.cls_rows, 128), lambda i, t: (0, 0)),
    ]
    if last:
        in_specs += [inner] + small
        operands += list(prev)
        main_spec = pl.BlockSpec(memory_space=pl.ANY)
        main_shape = jax.ShapeDtypeStruct((plan.units * unit_rows, c_out), F32)
    else:
        main_spec = inner
        main_shape = jax.ShapeDtypeStruct((n, depth, unit_rows, c_out), BF16)
    return pl.pallas_call(
        functools.partial(field_kernel, plan, field, last),
        grid_spec=pltpu.PrefetchScalarGridSpec(
            num_scalar_prefetch=1,
            grid=(turns + n,),
            in_specs=in_specs,
            out_specs=[main_spec] + small,
            scratch_shapes=[
                pltpu.VMEM((plan.height - RATE * k, cols, c_out), F32)
                for k in plan.shifted for _ in range(2)
            ] + [
                pltpu.VMEM((plan.height + 2 * (rows - 1), cols, plan.n_slots * c_out), BF16),
                pltpu.VMEM((nb * rows, cols + 2 * EDGE, c_out), F32),
                pltpu.VMEM((16, c_in), F32),
                pltpu.VMEM((turns, nb * pix, c_out), BF16),
                pltpu.VMEM((n, 16, pix), BF16),
                pltpu.VMEM((turns, nb * pix, c_out), BF16),
                pltpu.VMEM((max(plan.window, c_out), c_out), F32),
                pltpu.VMEM((16, c_out), F32),
                pltpu.VMEM((16, c_out), F32),
                pltpu.VMEM((turns, nb * pix, 5 * c_out), BF16),
                pltpu.VMEM((unit_rows, 3 * c_out), F32),
                pltpu.VMEM((2, depth if last else 1, unit_rows, c_out), F32),
                pltpu.VMEM((n, c_in, pix), BF16),
                pltpu.SemaphoreType.DMA,
                pltpu.SemaphoreType.DMA((2, depth)),
                pltpu.SemaphoreType.DMA((2 * n_sh,)),
            ],
        ),
        out_shape=[
            main_shape,
            jax.ShapeDtypeStruct((plan.proj_rows, c_out), kind),
            jax.ShapeDtypeStruct((plan.cls_rows, 128), kind),
        ],
        compiler_params=pltpu.CompilerParams(
            dimension_semantics=("arbitrary",), vmem_limit_bytes=FIELD_VMEM
        ),
        cost_estimate=pl.CostEstimate(
            flops=10_000_000_000, bytes_accessed=90_000_000, transcendentals=0
        ),
        name="field_grads",
    )(tab, *operands)


def after(value, *others):
    return lax.optimization_barrier((value, *others))[0]


def per_device(plan, features, labels, w_in, w_proj, w_cls, class_weight, matching):
    n, reps, rows, pix, c_in = plan.n, plan.reps, plan.rows, plan.pix, plan.c_in
    names = jnp.pad(labels[0].reshape(1, pix).astype(F32), ((0, 0), (0, c_in - pix)))
    x = pl.pallas_call(
        functools.partial(pack_kernel, pix),
        out_shape=jax.ShapeDtypeStruct((pix + EXTRA, c_in), BF16),
        name="pack",
    )(features[0].reshape(pix, c_in), names)
    here = lax.axis_index("space")
    n_bits = reps.bit_length() - 1
    bits = [jnp.bitwise_and(jnp.right_shift(matching[0], b), 1) == 1 for b in range(n_bits)]
    top = jnp.int32(0)
    for at, b in enumerate(list(range(1, n_bits)) + [0]):
        top = jnp.where(bits[b], n_bits - 1 - at, top)
    tab = jnp.asarray(plan.tables)[here]
    wcls = jnp.pad(w_cls.T, ((0, 16 - plan.classes), (0, 0)))

    def along(value, way, step):
        pairs = [
            (i, i + way) for i in range(n)
            if 0 <= i + way < n and 0 <= i - way * (step - 1) < n
        ]
        return lax.ppermute(value, "space", pairs)

    def hop(value, b):
        return lax.ppermute(value, "rep", [(r, r ^ (1 << b)) for r in range(reps)])

    order = np.array(
        [sorted(range(n), key=lambda j: (abs(j - s), j)) for s in range(n)], np.int32
    )
    blocks = jnp.asarray(order)[here]

    def arrival(q, ups, downs):
        value = None
        for s in range(n):
            j = int(order[s, q])
            arrived = ups[s - j] if j < s else downs[j - s]
            value = arrived if value is None else jnp.where(here == s, arrived, value)
        return value

    w_turn = w_proj[:4 * plan.c_out].T
    hops = list(range(1, n_bits)) + [0]
    rounds = n + n_bits - 1
    ups, downs, raw = [x], [x], (x, x)
    turns = []
    for t in range(1, rounds + 1):
        turn = [(t - 1, 0)] if t - 1 < n else []
        if t == rounds:
            turn += [(q, 1) for q in range(max(0, n + 1 - n_bits), n)]
        elif t >= n_bits and t <= n:
            turn.append((t - n_bits, 1))
        turns.append(turn)
    metas = [
        jnp.stack([
            jnp.stack([(top if f else 0) + jnp.int32(n_bits * at if f and turn[0][1] else at),
                       blocks[q], jnp.int32(f)])
            for at, (q, f) in enumerate(turn)
        ]) if turn else None
        for turn in turns
    ]
    values, moves = {0: x}, {q: [] for q in range(n)}
    state, grads = None, None
    for t in range(1, rounds + 1):
        q = t - 1
        if 0 < q < n:
            values[q] = arrival(q, ups, downs)
        for i in range(1, n_bits):
            if 0 <= q - i < n:
                values[q - i] = jnp.where(bits[hops[i - 1]], moves[q - i][0], values[q - i])
        for i in reversed(range(n_bits)):
            if 0 <= q - i < n:
                moves[q - i].insert(0, hop(values[q - i], hops[i]))
        if t < n:
            raw = along(raw[0], 1, t), along(raw[1], -1, t)
            ups.append(raw[0])
            downs.append(raw[1])
        slots = [moves[at] if f else [values[at]] for at, f in turns[q]]
        if slots:
            state = run_blocks(plan, slots, metas[q], w_in, state)
        if q == min(n, rounds - 1):
            grads = tuple(run_field(
                plan, 0, tab, state, w_in, w_proj, w_turn, wcls, class_weight, None
            ))
        if t < rounds:
            live = (ups, downs, values, moves, state, grads, metas, tab, wcls, w_turn)
            live = lax.optimization_barrier(live)
            ups, downs, values, moves, state, grads, metas, tab, wcls, w_turn = live
    avg_in, avg_proj, avg_cls = run_field(
        plan, 1, tab, state, w_in, w_proj, w_turn, wcls, class_weight, grads
    )
    return avg_in[None], avg_proj[None], avg_cls[None, :, :plan.classes]


def solution(mesh):
    n, reps = mesh.shape["space"], mesh.shape["rep"]

    def build(features, labels, w_in, w_proj, w_cls, class_weight, matching):
        _, rows, cols, c_in = features.shape
        plan = Plan(n, reps, rows // n, cols, c_in, w_proj.shape[1], w_cls.shape[1])
        return jax.shard_map(
            functools.partial(per_device, plan),
            mesh=mesh,
            in_specs=(P("rep", "space", None, None), P("rep", "space", None), P(), P(), P(), P(), P()),
            out_specs=(P("rep", "space", None), P("rep", "space", None), P("rep", "space", None)),
            check_vma=False,
        )(features, labels, w_in, w_proj, w_cls, class_weight, matching)

    return build
```

```python
import functools

import jax
import jax.numpy as jnp
import numpy as np
from jax import lax
from jax.experimental import pallas as pl
from jax.experimental.pallas import tpu as pltpu
from jax.sharding import PartitionSpec as P

LOSS_SCALE = 1024.0
RATE = 12
EDGE = 40
EXTRA = 16
BF16 = jnp.bfloat16
F32 = jnp.float32
MIB = 1024 * 1024


def nn(a, b):
    return lax.dot_general(a, b, (((1,), (0,)), ((), ())), preferred_element_type=F32)


def nt(a, b):
    return lax.dot_general(a, b, (((1,), (1,)), ((), ())), preferred_element_type=F32)


def tn(a, b):
    return lax.dot_general(a, b, (((0,), (0,)), ((), ())), preferred_element_type=F32)


def identity(size):
    rows = lax.broadcasted_iota(jnp.int32, (size, size), 0)
    cols = lax.broadcasted_iota(jnp.int32, (size, size), 1)
    return (rows == cols).astype(F32).astype(BF16)


class Plan:
    def __init__(self, n, reps, rows, cols, c_in, c_out, classes):
        self.n, self.reps, self.rows, self.cols = n, reps, rows, cols
        self.c_in, self.c_out, self.classes = c_in, c_out, classes
        self.height = rows * n
        self.pix = rows * cols
        self.total = self.pix * n
        self.shifted = [k for k in (1, 2, 3) if RATE * k < self.height]
        self.direct = [k for k in range(4) if k not in self.shifted]
        self.n_sh = len(self.shifted)
        self.vmem = (40 if self.n_sh == 1 else 50) * MIB
        self.together = 2 if n % 2 == 0 and self.n_sh == 1 else 1
        row = lambda k, a: [1 + 9 * (k - 1) + 3 * a + b for b in range(3)]
        still = [row(k, 1) for k in self.direct[1:]]
        self.loads = [[0] + (still[0] if still else [])] + still[1:]
        for k in self.shifted:
            self.loads += [row(k, a) for a in range(3)]
        self.units = 29
        self.unit_rows = c_in // n
        self.proj_rows = 5 * c_out // n
        self.cls_rows = c_out // n
        starts = [self.proj_rows * s // 128 * 128 for s in range(n)]
        ends = [-(-self.proj_rows * (s + 1) // 128) * 128 for s in range(n)]
        self.window = max(e - b for b, e in zip(starts, ends))
        self.starts = [min(b, 5 * c_out - self.window) for b in starts]
        tables = [self.table(s) for s in range(n)]
        self.n_slots = max(t[1] for t in tables)
        self.depth = max(t[2] for t in tables)
        self.tables = np.array([
            sum((c + [[0] * 6] * (self.depth - len(c)) for c in t[0]), []) for t in tables
        ], np.int32).reshape(n, -1)
        self.flags = self.tables.shape[1]
        self.tables = np.concatenate([
            self.tables,
            np.array([
                [len(c) for c in t[0]] + t[3] + [s, self.starts[s]]
                + sum(([len(h)] + h + [0] * (self.depth - len(h)) for h in t[4]), [])
                for s, t in enumerate(tables)
            ], np.int32),
        ], axis=1)

    def tap(self, t):
        if t == 0:
            return (0, 1, 1)
        if t == 28:
            return None
        k, rest = (t - 1) // 9 + 1, (t - 1) % 9
        a, b = rest // 3, rest % 3
        if a != 1 and k not in self.shifted:
            return "zero"
        return (k, a, b)

    def table(self, s):
        parts = [[] for _ in range(self.n)]
        here = range(s * self.units, (s + 1) * self.units)
        slots = {}
        for k in range(4):
            for b in ((1,) if k == 0 else range(3)):
                if any(
                    isinstance(self.tap(u // self.n), tuple)
                    and (self.tap(u // self.n)[0], self.tap(u // self.n)[2]) == (k, b)
                    for u in here
                ):
                    slots[(k, b)] = len(slots)
        for unit in here:
            c, tap = unit % self.n, self.tap(unit // self.n)
            local = unit - s * self.units
            if tap is None or tap == "zero":
                parts[c].append([0, 0, 0, 0, 1 if tap is None else 2, local])
                continue
            k, a, b = tap
            move = (a - 1) * RATE * k
            valid = [
                j for j in range(self.n)
                if any(0 <= self.rows * j + i - move < self.height for i in range(self.rows))
            ]
            entry = [slots[(k, b)], move, valid[0], valid[-1] + 1, 0, local]
            if b == 2 and len(parts[c]) > 1 and all(
                e[4] == 0 and e[:4] == [entry[0] - back] + entry[1:4]
                for back, e in ((1, parts[c][-1]), (2, parts[c][-2]))
            ):
                parts[c][-2][4] = 3
                parts[c][-1][4] = 4
                entry[4] = 4
            parts[c].append(entry)
        want = [slots.get((k, b), -1) for k in range(4) for b in range(3)]
        heads = [[i for i, e in enumerate(c) if e[4] != 4] for c in parts]
        return parts, len(slots), max(len(c) for c in parts), want, heads


def pack_kernel(pix, x_ref, lab_ref, out_ref):
    x = x_ref[...]
    out_ref[:pix, :] = x
    total = jnp.sum(x.astype(F32), axis=0, keepdims=True)
    head = total.astype(BF16).astype(F32)
    mid = (total - head).astype(BF16).astype(F32)
    row = lax.broadcasted_iota(jnp.int32, (EXTRA, x.shape[1]), 0)
    extra = jnp.zeros((EXTRA, x.shape[1]), F32)
    for at, value in enumerate((head, mid, total - head - mid, lab_ref[...])):
        extra = jnp.where(row == at, value, extra)
    out_ref[pix:, :] = extra.astype(BF16)


def block_kernel(plan, n_cand, n_slots, aliased, meta, *refs):
    rows, cols, c_in, c_out = plan.rows, plan.cols, plan.c_in, plan.c_out
    pix = plan.pix
    cands = refs[:n_cand]
    w_hbm = refs[n_cand]
    refs = refs[n_cand + 1 + (4 if aliased else 0):]
    xt_out, cat_out, s_out, aux_out = refs[:4]
    xin, wbuf, xtb, catb, sb, res, sem_x, sem_w, sem_o, sem_s = refs[4:]
    step = pl.program_id(0)
    block, field = meta[step, 1], meta[step, 2]
    now = lax.rem(step, 2)
    xbuf = xin.at[now, pl.ds(0, pix)]

    def fetch(at, slot):
        for c in range(n_cand):
            @pl.when(meta[at, 0] == c)
            def _(c=c):
                pltpu.make_async_copy(cands[c], xin.at[slot], sem_x.at[slot]).start()

    def weights(group, taps):
        return [
            pltpu.make_async_copy(
                w_hbm.at[tap], wbuf.at[group, :, pl.ds(i * c_out, c_out)], sem_w.at[group, i]
            )
            for i, tap in enumerate(taps)
        ]

    @pl.when(step == 0)
    def _():
        fetch(0, 0)
        for group, taps in enumerate(plan.loads):
            for copy in weights(group, taps):
                copy.start()
        res[:, :EDGE, :] = jnp.zeros((rows, EDGE, res.shape[2]), F32)
        res[:, EDGE + cols:, :] = jnp.zeros((rows, EDGE, res.shape[2]), F32)

    if n_slots > 1:
        @pl.when(step + 1 < n_slots)
        def _():
            fetch(step + 1, 1 - now)

    pltpu.make_async_copy(cands[0], xin.at[now], sem_x.at[now]).wait()
    aux_copy = pltpu.make_async_copy(
        xin.at[now, pl.ds(pix, EXTRA)], aux_out.at[field, block], sem_o.at[2]
    )
    aux_copy.start()
    eye = identity(256)
    for c in range(c_in // 256):
        part = slice(c * 256, (c + 1) * 256)
        xtb[part, :] = nt(eye, xbuf[:, part]).astype(BF16)
    xt_copy = pltpu.make_async_copy(xtb, xt_out.at[field, block], sem_o.at[0])
    xt_copy.start()

    def in_field(move):
        first = block * rows + move
        return jnp.logical_and(first + rows - 1 >= 0, first < plan.height)

    def loaded(group, taps):
        @pl.when(step == 0)
        def _():
            for copy in weights(group, taps):
                copy.wait()

    def columns(k, first):
        r = RATE * k
        part = [slice(first + i * c_out, first + (i + 1) * c_out) for i in range(3)]
        return (
            res[:, EDGE - r:EDGE - r + cols, part[0]]
            + res[:, EDGE:EDGE + cols, part[1]]
            + res[:, EDGE + r:EDGE + r + cols, part[2]]
        )

    def relu_to(k, value):
        at = plan.direct.index(k)
        catb[:, at * c_out:(at + 1) * c_out] = (
            jnp.maximum(value, 0.0).astype(BF16).reshape(pix, c_out)
        )

    def shifted_copy(at):
        return pltpu.make_async_copy(
            sb.at[at], s_out.at[at, field, pl.ds(block * rows, rows)], sem_s.at[at]
        )

    group = 0
    first = c_out
    loaded(0, plan.loads[0])
    width = len(plan.loads[0]) * c_out
    res[:, EDGE:EDGE + cols, :width] = nn(xbuf[...], wbuf[0, :, :width]).reshape(
        rows, cols, width
    )
    relu_to(0, res[:, EDGE:EDGE + cols, :c_out])
    group = 1
    for k in plan.direct[1:]:
        if first + 3 * c_out > width:
            loaded(group, plan.loads[group])
            width, first = 3 * c_out, 0
            res[:, EDGE:EDGE + cols, :width] = nn(xbuf[...], wbuf[group, :, :width]).reshape(
                rows, cols, width
            )
            group += 1
        relu_to(k, columns(k, first))
        first += 3 * c_out
    cat_copy = pltpu.make_async_copy(catb, cat_out.at[field, block], sem_o.at[1])
    cat_copy.start()
    width = 3 * c_out
    for at, k in enumerate(plan.shifted):
        for a in range(3):
            loaded(group + 3 * at + a, plan.loads[group + 3 * at + a])

        def one(a, _, k=k, at=at, base=group + 3 * at):
            @pl.when(in_field((1 - a) * RATE * k))
            def _():
                res[:, EDGE:EDGE + cols, :width] = nn(
                    xbuf[...], wbuf[base + a, :, :width]
                ).reshape(rows, cols, width)
                sb[3 * at + a] = columns(k, 0)
                shifted_copy(3 * at + a).start()
            return 0

        lax.fori_loop(0, 3, one, 0)
    aux_copy.wait()
    xt_copy.wait()
    cat_copy.wait()
    for at, k in enumerate(plan.shifted):
        for a in range(3):
            @pl.when(in_field((1 - a) * RATE * k))
            def _(at=at, a=a):
                shifted_copy(3 * at + a).wait()


def run_blocks(plan, slots, meta, w_in, state):
    arrays = [value for cands in slots for value in cands]
    n, rows, cols, pix = plan.n, plan.rows, plan.cols, plan.pix
    c_in, c_out, n_sh = plan.c_in, plan.c_out, plan.n_sh
    shapes = [
        jax.ShapeDtypeStruct((2, n, c_in, pix), BF16),
        jax.ShapeDtypeStruct((2, n, pix, len(plan.direct) * c_out), BF16),
        jax.ShapeDtypeStruct((3 * n_sh, 2, n * rows, cols, c_out), F32),
        jax.ShapeDtypeStruct((2, n, EXTRA, c_in), BF16),
    ]
    widest = max(len(g) for g in plan.loads) * c_out
    aliased = state is not None
    operands = [*arrays, w_in] + (list(state) if aliased else [])
    aliases = {1 + len(arrays) + 1 + i: i for i in range(4)} if aliased else {}
    return pl.pallas_call(
        functools.partial(block_kernel, plan, len(arrays), len(slots), aliased),
        grid_spec=pltpu.PrefetchScalarGridSpec(
            num_scalar_prefetch=1,
            grid=(len(slots),),
            in_specs=[pl.BlockSpec(memory_space=pl.ANY)] * len(operands),
            out_specs=[pl.BlockSpec(memory_space=pl.ANY)] * 4,
            scratch_shapes=[
                pltpu.VMEM((2, pix + EXTRA, c_in), BF16),
                pltpu.VMEM((len(plan.loads), c_in, widest), BF16),
                pltpu.VMEM((c_in, pix), BF16),
                pltpu.VMEM((pix, len(plan.direct) * c_out), BF16),
                pltpu.VMEM((3 * n_sh, rows, cols, c_out), F32),
                pltpu.VMEM((rows, cols + 2 * EDGE, widest), F32),
                pltpu.SemaphoreType.DMA((2,)),
                pltpu.SemaphoreType.DMA((len(plan.loads), 4)),
                pltpu.SemaphoreType.DMA((3,)),
                pltpu.SemaphoreType.DMA((3 * n_sh,)),
            ],
        ),
        out_shape=shapes,
        input_output_aliases=aliases,
        compiler_params=pltpu.CompilerParams(
            dimension_semantics=("arbitrary",), vmem_limit_bytes=plan.vmem
        ),
        cost_estimate=pl.CostEstimate(
            flops=len(slots) * 2 * pix * c_in * c_out * (10 + 6 * n_sh),
            bytes_accessed=20_000_000 + len(slots) * 20_000_000,
            transcendentals=0,
        ),
        name="block_forward",
    )(meta, *operands)


def field_kernel(plan, field, last, tab, *refs):
    n, rows, cols, pix = plan.n, plan.rows, plan.cols, plan.pix
    c_in, c_out, n_sh = plan.c_in, plan.c_out, plan.n_sh
    unit_rows, depth, flags = plan.unit_rows, plan.depth, plan.flags
    cat_ref = refs[0]
    mid_refs = refs[1:1 + n_sh]
    s_hbm = refs[1 + n_sh]
    refs = refs[2 + n_sh:]
    aux_ref, all_ref, w28_ref, wproj_ref, wturn_ref, wcls_ref, cw_ref, xt_hbm = refs[:8]
    refs = refs[8:]
    if last:
        prev_g, prev_p, prev_c = refs[:3]
        refs = refs[3:]
    g_out, p_out, c_ref_out = refs[:3]
    side_refs = refs[3:3 + 2 * n_sh]
    (dbuf, pad, mean, ybuf, lbuf, dybuf, gp, spool, pact, catall, acc, stage, xt_ref, sem_xt,
     sems, sem_s) = refs[3 + 2 * n_sh:]
    xt_copy = pltpu.make_async_copy(xt_hbm.at[field], xt_ref, sem_xt)
    step = pl.program_id(0)
    edge_rows = rows - 1
    nb, turns = plan.together, n // plan.together

    def finish(value, prev):
        grad = value.astype(BF16)
        if not last:
            return grad
        return (prev.astype(F32) + grad.astype(F32)) * 0.5

    def side_copies():
        copies = []
        for at, k in enumerate(plan.shifted):
            for side in range(2):
                first, count = side * RATE * k, plan.height - RATE * k
                copies.append(pltpu.make_async_copy(
                    s_hbm.at[3 * at + 2 * side, field, pl.ds(first, count)],
                    side_refs[2 * at + side], sem_s.at[2 * at + side],
                ))
        return copies

    @pl.when(step == 0)
    def _():
        for copy in side_copies():
            copy.start()
        xt_copy.start()
        zero = jnp.zeros((edge_rows, cols, dbuf.shape[2]), BF16)
        dbuf[:edge_rows] = zero
        dbuf[edge_rows + plan.height:] = zero
        pad[:, :EDGE, :] = jnp.zeros((nb * rows, EDGE, c_out), F32)
        pad[:, EDGE + cols:, :] = jnp.zeros((nb * rows, EDGE, c_out), F32)
        total = jnp.zeros((1, c_in), F32)
        for j in range(n):
            extra = all_ref[j].astype(F32)
            total = total + ((extra[2:3] + extra[1:2]) + extra[0:1])
        mean_in = (total / plan.total).astype(BF16)
        mean[...] = jnp.broadcast_to(mean_in.astype(F32), (16, c_in))
        pact[...] = nn(mean[...].astype(BF16), w28_ref[0])
        for copy in side_copies():
            copy.wait()

    @pl.when(step < turns)
    def _():
        cat5 = catall.at[step]
        for k in range(4):
            part = slice(k * c_out, (k + 1) * c_out)
            if k in plan.shifted:
                at = plan.shifted.index(k)
                r = RATE * k
                pre = mid_refs[at]
                for i in range(nb * rows):
                    h = step * nb * rows + i
                    line = pre[i]
                    for side, src in ((0, h - r), (1, h)):
                        last_row = plan.height - r - 1
                        ok = jnp.logical_and(src >= 0, src <= last_row)
                        got = side_refs[2 * at + side][jnp.clip(src, 0, last_row)]
                        line = line + jnp.where(ok, got, 0.0)
                    cat5[i * cols:(i + 1) * cols, part] = jnp.maximum(line, 0.0).astype(BF16)
            else:
                at = plan.direct.index(k)
                cat5[:, part] = cat_ref[:, :, at * c_out:(at + 1) * c_out].reshape(nb * pix, c_out)
        pool_act = jnp.maximum(pact[0:1, :], 0.0).astype(BF16)
        cat5[:, 4 * c_out:] = jnp.broadcast_to(pool_act, (nb * pix, c_out))
        y_pre = nn(cat5[...], wproj_ref[...])
        y_act = jnp.maximum(y_pre, 0.0).astype(BF16)
        ybuf[step] = y_act
        row = lax.broadcasted_iota(jnp.int32, (16, pix), 0)
        live = row < plan.classes
        for sub in range(nb):
            cells = slice(sub * pix, (sub + 1) * pix)
            logits = nt(wcls_ref[...], y_act[cells])
            expo = jnp.where(live, jnp.exp(logits), 0.0)
            prob = expo / jnp.sum(expo, axis=0, keepdims=True)
            label = jnp.broadcast_to(aux_ref[sub, 3:4, :pix].astype(F32), (16, pix))
            onehot = jnp.where(label == row.astype(F32), 1.0, 0.0)
            weight = jnp.zeros((16, pix), F32)
            for c in range(plan.classes):
                weight = jnp.where(label == float(c), cw_ref[c], weight)
            d_logits = jnp.where(
                live, (prob - onehot) * weight * (LOSS_SCALE / plan.total), 0.0
            ).astype(BF16)
            lbuf[step * nb + sub] = d_logits
            dybuf[step, cells] = jnp.where(
                y_pre[cells] > 0, tn(d_logits, wcls_ref[...]), 0.0
            ).astype(BF16)
        d_y = dybuf[step]
        for k in range(4):
            want = [tab[flags + n + 3 * k + b] for b in range(3)]
            part = slice(k * c_out, (k + 1) * c_out)

            @pl.when((want[0] >= 0) | (want[1] >= 0) | (want[2] >= 0))
            def _(k=k, want=want, part=part):
                d_cat = nn(d_y, wturn_ref[:, part])
                d_k = jnp.where(cat5[:, part] > 0, d_cat, 0.0).astype(BF16)
                d_k = d_k.reshape(nb * rows, cols, c_out)
                if k > 0:
                    pad[:, EDGE:EDGE + cols, :] = d_k.astype(F32)
                at = pl.ds(step * nb * rows + edge_rows, nb * rows)
                for b in range(3):
                    if k == 0 and b != 1:
                        continue

                    @pl.when(want[b] >= 0)
                    def _(b=b):
                        lanes = pl.ds(pl.multiple_of(jnp.maximum(want[b], 0) * c_out, c_out), c_out)
                        if b == 1:
                            dbuf[at, :, lanes] = d_k
                        else:
                            first = EDGE + (1 - b) * RATE * k
                            dbuf[at, :, lanes] = pad[:, first:first + cols, :].astype(BF16)

    @pl.when(step == turns - 1)
    def _():
        all_dy = dybuf[...].reshape(n * pix, c_out)
        pool = wproj_ref[4 * c_out:, :]
        rest = nn(jnp.ones((16, n * pix), BF16), all_dy)
        total = jnp.zeros(rest.shape, F32)
        for _i in range(3):
            head = rest.astype(BF16)
            total = total + nt(head, pool)
            rest = rest - head.astype(F32)
        spool[...] = jnp.where(pact[...] > 0, jnp.broadcast_to(total[0:1, :], total.shape), 0.0)
        window = pl.ds(pl.multiple_of(tab[flags + n + 13], 128), plan.window)
        g_proj = jnp.zeros((c_out, plan.window), F32)
        g_cls = jnp.zeros((16, c_out), F32)
        for j in range(turns):
            g_proj = g_proj + nn(
                nt(identity(c_out), dybuf[j]).astype(BF16), catall[j, :, window]
            )
        for j in range(n):
            cells = slice(j % nb * pix, (j % nb + 1) * pix)
            g_cls = g_cls + nn(lbuf[j], ybuf[j // nb, cells])
        gp[:plan.window, :] = g_proj.T
        index = tab[flags + n + 12]
        first = pl.multiple_of(index * plan.proj_rows - tab[flags + n + 13], 32)
        p_out[...] = finish(gp[pl.ds(first, plan.proj_rows), :], prev_p[...] if last else None)
        gp[:c_out, :128] = jnp.concatenate([g_cls, jnp.zeros((112, c_out), F32)], axis=0).T
        first = pl.multiple_of(index * plan.cls_rows, plan.cls_rows)
        mine = finish(gp[pl.ds(first, plan.cls_rows), :128], prev_c[...] if last else None)
        c_ref_out[...] = mine[:, :c_ref_out.shape[1]]

    def out_copy(part, slot, t):
        row = tab[(part * depth + t) * 6 + 5] * unit_rows
        return pltpu.make_async_copy(
            stage.at[slot, t],
            g_out.at[pl.ds(pl.multiple_of(row, unit_rows), unit_rows)],
            sems.at[slot, t],
        )

    @pl.when(step == turns)
    def _():
        xt_copy.wait()

    @pl.when(step >= turns)
    def _():
        part = step - turns
        parity = lax.rem(part, 2)
        mine = pl.ds(pl.multiple_of(part * unit_rows, unit_rows), unit_rows)

        heads = flags + n + 14 + part * (depth + 1)

        def one(i, _):
            t = tab[heads + 1 + i]
            base = (part * depth + t) * 6
            slot, move, low, high = tab[base], tab[base + 1], tab[base + 2], tab[base + 3]
            kind = tab[base + 4]

            def product(taps):
                width = taps * c_out
                lanes = pl.ds(pl.multiple_of(slot * c_out, c_out), width)

                def term(j):
                    first = j * rows - move + edge_rows
                    return nn(xt_ref[j, mine, :], dbuf[pl.ds(first, rows), :, lanes].reshape(pix, width))

                whole = jnp.logical_and(low == 0, high == n)

                @pl.when(whole)
                def _():
                    total = term(0)
                    for j in range(1, n):
                        total = total + term(j)
                    acc[:, :width] = total

                @pl.when(jnp.logical_not(whole))
                def _():
                    acc[:, :width] = jnp.zeros((unit_rows, width), F32)

                    def add(j, _):
                        acc[:, :width] += term(j)
                        return 0

                    lax.fori_loop(low, high, add, 0)

            @pl.when(kind == 3)
            def _():
                product(3)

            @pl.when(kind == 0)
            def _():
                product(1)

            @pl.when(kind == 2)
            def _():
                acc[:, :c_out] = jnp.zeros((unit_rows, c_out), F32)

            @pl.when(kind == 1)
            def _():
                first = pl.multiple_of(part * unit_rows, unit_rows)
                row = mean[0:1, pl.ds(first, unit_rows)]
                column = jnp.broadcast_to(row, (128, unit_rows)).T
                for c in range(c_out // 128):
                    lanes = slice(c * 128, (c + 1) * 128)
                    acc[:, lanes] = column * spool[0:1, lanes]

            def emit(at, lanes):
                if last:
                    stage[parity, at] = finish(acc[:, lanes], prev_g[at])
                    out_copy(part, parity, at).start()
                else:
                    g_out[at] = finish(acc[:, lanes], None)

            emit(t, slice(0, c_out))

            @pl.when(kind == 3)
            def _():
                for b in (1, 2):
                    emit(t + b, slice(b * c_out, (b + 1) * c_out))

            return 0

        lax.fori_loop(0, tab[heads], one, 0)

        if last:
            def drain(which, slot):
                def one(t, _):
                    out_copy(which, slot, t).wait()
                    return 0
                lax.fori_loop(0, tab[flags + which], one, 0)

            @pl.when(part > 0)
            def _():
                drain(part - 1, 1 - parity)

            @pl.when(part == n - 1)
            def _():
                drain(part, parity)


def run_field(plan, field, tab, state, w_in, w_proj, w_turn, wcls, cw, prev):
    n, rows, cols, pix = plan.n, plan.rows, plan.cols, plan.pix
    c_in, c_out, n_sh = plan.c_in, plan.c_out, plan.n_sh
    unit_rows, depth = plan.unit_rows, plan.depth
    last = prev is not None
    nb, turns = plan.together, n // plan.together
    xt, cat, s, aux = state

    def blk(i):
        return jnp.minimum(i, turns - 1)

    def part(i):
        return jnp.maximum(i - turns, 0)

    in_specs = [
        pl.BlockSpec(
            (None, nb, pix, len(plan.direct) * c_out), lambda i, t: (field, blk(i), 0, 0)
        ),
    ]
    operands = [cat]
    for at in range(n_sh):
        in_specs.append(pl.BlockSpec(
            (None, None, nb * rows, cols, c_out),
            lambda i, t, at=at: (3 * at + 1, field, blk(i), 0, 0),
        ))
        operands.append(s)
    in_specs.append(pl.BlockSpec(memory_space=pl.ANY))
    operands.append(s)
    in_specs += [
        pl.BlockSpec((None, nb, EXTRA, c_in), lambda i, t: (field, blk(i), 0, 0)),
        pl.BlockSpec((None, n, EXTRA, c_in), lambda i, t: (field, 0, 0, 0)),
        pl.BlockSpec((1, c_in, c_out), lambda i, t: (28, 0, 0)),
        pl.BlockSpec((5 * c_out, c_out), lambda i, t: (0, 0)),
        pl.BlockSpec((c_out, 4 * c_out), lambda i, t: (0, 0)),
        pl.BlockSpec((16, c_out), lambda i, t: (0, 0)),
        pl.BlockSpec(memory_space=pltpu.SMEM),
        pl.BlockSpec(memory_space=pl.ANY),
    ]
    operands += [aux, aux, w_in, w_proj, w_turn, wcls, cw, xt]
    kind = F32 if last else BF16
    out_lanes = plan.classes if last else 128
    inner = pl.BlockSpec((None, depth, unit_rows, c_out), lambda i, t: (part(i), 0, 0, 0))
    small = [
        pl.BlockSpec((plan.proj_rows, c_out), lambda i, t: (0, 0)),
        pl.BlockSpec((plan.cls_rows, 128), lambda i, t: (0, 0)),
    ]
    out_small = [small[0], pl.BlockSpec((plan.cls_rows, out_lanes), lambda i, t: (0, 0))]
    if last:
        in_specs += [inner] + small
        operands += list(prev)
        main_spec = pl.BlockSpec(memory_space=pl.ANY)
        main_shape = jax.ShapeDtypeStruct((plan.units * unit_rows, c_out), F32)
    else:
        main_spec = inner
        main_shape = jax.ShapeDtypeStruct((n, depth, unit_rows, c_out), BF16)
    return pl.pallas_call(
        functools.partial(field_kernel, plan, field, last),
        grid_spec=pltpu.PrefetchScalarGridSpec(
            num_scalar_prefetch=1,
            grid=(turns + n,),
            in_specs=in_specs,
            out_specs=[main_spec] + out_small,
            scratch_shapes=[
                pltpu.VMEM((plan.height - RATE * k, cols, c_out), F32)
                for k in plan.shifted for _ in range(2)
            ] + [
                pltpu.VMEM((plan.height + 2 * (rows - 1), cols, plan.n_slots * c_out), BF16),
                pltpu.VMEM((nb * rows, cols + 2 * EDGE, c_out), F32),
                pltpu.VMEM((16, c_in), F32),
                pltpu.VMEM((turns, nb * pix, c_out), BF16),
                pltpu.VMEM((n, 16, pix), BF16),
                pltpu.VMEM((turns, nb * pix, c_out), BF16),
                pltpu.VMEM((max(plan.window, c_out), c_out), F32),
                pltpu.VMEM((16, c_out), F32),
                pltpu.VMEM((16, c_out), F32),
                pltpu.VMEM((turns, nb * pix, 5 * c_out), BF16),
                pltpu.VMEM((unit_rows, 3 * c_out), F32),
                pltpu.VMEM((2, depth if last else 1, unit_rows, c_out), F32),
                pltpu.VMEM((n, c_in, pix), BF16),
                pltpu.SemaphoreType.DMA,
                pltpu.SemaphoreType.DMA((2, depth)),
                pltpu.SemaphoreType.DMA((2 * n_sh,)),
            ],
        ),
        out_shape=[
            main_shape,
            jax.ShapeDtypeStruct((plan.proj_rows, c_out), kind),
            jax.ShapeDtypeStruct((plan.cls_rows, out_lanes), kind),
        ],
        compiler_params=pltpu.CompilerParams(
            dimension_semantics=("arbitrary",), vmem_limit_bytes=plan.vmem
        ),
        cost_estimate=pl.CostEstimate(
            flops=10_000_000_000, bytes_accessed=90_000_000, transcendentals=0
        ),
        name="field_grads",
    )(tab, *operands)


def after(value, *others):
    return lax.optimization_barrier((value, *others))[0]


def per_device(plan, features, labels, w_in, w_proj, w_cls, class_weight, matching):
    n, reps, rows, pix, c_in = plan.n, plan.reps, plan.rows, plan.pix, plan.c_in
    names = jnp.pad(labels[0].reshape(1, pix).astype(F32), ((0, 0), (0, c_in - pix)))
    x = pl.pallas_call(
        functools.partial(pack_kernel, pix),
        out_shape=jax.ShapeDtypeStruct((pix + EXTRA, c_in), BF16),
        name="pack",
    )(features[0].reshape(pix, c_in), names)
    here = lax.axis_index("space")
    n_bits = reps.bit_length() - 1
    bits = [jnp.bitwise_and(jnp.right_shift(matching[0], b), 1) == 1 for b in range(n_bits)]
    top = jnp.int32(0)
    for at, b in enumerate(list(range(1, n_bits)) + [0]):
        top = jnp.where(bits[b], n_bits - 1 - at, top)
    tab = jnp.asarray(plan.tables)[here]
    wcls = jnp.pad(w_cls.T, ((0, 16 - plan.classes), (0, 0)))

    def along(value, way, step):
        pairs = [
            (i, i + way) for i in range(n)
            if 0 <= i + way < n and 0 <= i - way * (step - 1) < n
        ]
        return lax.ppermute(value, "space", pairs)

    def hop(value, b):
        return lax.ppermute(value, "rep", [(r, r ^ (1 << b)) for r in range(reps)])

    order = np.array(
        [sorted(range(n), key=lambda j: (abs(j - s), j)) for s in range(n)], np.int32
    )
    blocks = jnp.asarray(order)[here]

    def arrival(q, ups, downs):
        value = None
        for s in range(n):
            j = int(order[s, q])
            arrived = ups[s - j] if j < s else downs[j - s]
            value = arrived if value is None else jnp.where(here == s, arrived, value)
        return value

    w_turn = w_proj[:4 * plan.c_out].T
    hops = list(range(1, n_bits)) + [0]
    rounds = n + n_bits - 1
    ups, downs, raw = [x], [x], (x, x)
    turns = []
    for t in range(1, rounds + 1):
        turn = [(t - 1, 0)] if t - 1 < n else []
        if t == rounds:
            turn += [(q, 1) for q in range(max(0, n + 1 - n_bits), n)]
        elif t >= n_bits and t <= n:
            turn.append((t - n_bits, 1))
        turns.append(turn)
    metas = [
        jnp.stack([
            jnp.stack([(top if f else 0) + jnp.int32(n_bits * at if f and turn[0][1] else at),
                       blocks[q], jnp.int32(f)])
            for at, (q, f) in enumerate(turn)
        ]) if turn else None
        for turn in turns
    ]
    values, moves = {0: x}, {q: [] for q in range(n)}
    state, grads = None, None
    for t in range(1, rounds + 1):
        q = t - 1
        if 0 < q < n:
            values[q] = arrival(q, ups, downs)
        for i in range(1, n_bits):
            if 0 <= q - i < n:
                values[q - i] = jnp.where(bits[hops[i - 1]], moves[q - i][0], values[q - i])
        for i in reversed(range(n_bits)):
            if 0 <= q - i < n:
                moves[q - i].insert(0, hop(values[q - i], hops[i]))
        if t < n:
            raw = along(raw[0], 1, t), along(raw[1], -1, t)
            ups.append(raw[0])
            downs.append(raw[1])
        slots = [moves[at] if f else [values[at]] for at, f in turns[q]]
        if slots:
            state = run_blocks(plan, slots, metas[q], w_in, state)
        if q == min(n, rounds - 1):
            grads = tuple(run_field(
                plan, 0, tab, state, w_in, w_proj, w_turn, wcls, class_weight, None
            ))
        if t < rounds:
            live = (ups, downs, values, moves, state, grads, metas, tab, wcls, w_turn)
            live = lax.optimization_barrier(live)
            ups, downs, values, moves, state, grads, metas, tab, wcls, w_turn = live
    avg_in, avg_proj, avg_cls = run_field(
        plan, 1, tab, state, w_in, w_proj, w_turn, wcls, class_weight, grads
    )
    return avg_in[None], avg_proj[None], avg_cls[None]


def solution(mesh):
    n, reps = mesh.shape["space"], mesh.shape["rep"]

    def build(features, labels, w_in, w_proj, w_cls, class_weight, matching):
        _, rows, cols, c_in = features.shape
        plan = Plan(n, reps, rows // n, cols, c_in, w_proj.shape[1], w_cls.shape[1])
        return jax.shard_map(
            functools.partial(per_device, plan),
            mesh=mesh,
            in_specs=(P("rep", "space", None, None), P("rep", "space", None), P(), P(), P(), P(), P()),
            out_specs=(P("rep", "space", None), P("rep", "space", None), P("rep", "space", None)),
            check_vma=False,
        )(features, labels, w_in, w_proj, w_cls, class_weight, matching)

    return build
```

```python
import functools

import jax
import jax.numpy as jnp
import numpy as np
from jax import lax
from jax.experimental import pallas as pl
from jax.experimental.pallas import tpu as pltpu
from jax.sharding import PartitionSpec as P

LOSS_SCALE = 1024.0
RATE = 12
EDGE = 40
EXTRA = 16
BF16 = jnp.bfloat16
F32 = jnp.float32
MIB = 1024 * 1024


def nn(a, b):
    return lax.dot_general(a, b, (((1,), (0,)), ((), ())), preferred_element_type=F32)


def nt(a, b):
    return lax.dot_general(a, b, (((1,), (1,)), ((), ())), preferred_element_type=F32)


def tn(a, b):
    return lax.dot_general(a, b, (((0,), (0,)), ((), ())), preferred_element_type=F32)


def identity(size):
    rows = lax.broadcasted_iota(jnp.int32, (size, size), 0)
    cols = lax.broadcasted_iota(jnp.int32, (size, size), 1)
    return (rows == cols).astype(F32).astype(BF16)


class Plan:
    def __init__(self, n, reps, rows, cols, c_in, c_out, classes):
        self.n, self.reps, self.rows, self.cols = n, reps, rows, cols
        self.c_in, self.c_out, self.classes = c_in, c_out, classes
        self.height = rows * n
        self.pix = rows * cols
        self.total = self.pix * n
        self.shifted = [k for k in (1, 2, 3) if RATE * k < self.height]
        self.direct = [k for k in range(4) if k not in self.shifted]
        self.n_sh = len(self.shifted)
        self.vmem = (40 if self.n_sh == 1 else 50) * MIB
        self.together = n if self.n_sh == 1 else 1
        row = lambda k, a: [1 + 9 * (k - 1) + 3 * a + b for b in range(3)]
        still = [row(k, 1) for k in self.direct[1:]]
        self.loads = [[0] + (still[0] if still else [])] + still[1:]
        for k in self.shifted:
            self.loads += [row(k, a) for a in range(3)]
        self.units = 29
        self.unit_rows = c_in // n
        self.proj_rows = 5 * c_out // n
        self.cls_rows = c_out // n
        starts = [self.proj_rows * s // 128 * 128 for s in range(n)]
        ends = [-(-self.proj_rows * (s + 1) // 128) * 128 for s in range(n)]
        self.window = max(e - b for b, e in zip(starts, ends))
        self.starts = [min(b, 5 * c_out - self.window) for b in starts]
        tables = [self.table(s) for s in range(n)]
        self.n_slots = max(t[1] for t in tables)
        self.depth = max(t[2] for t in tables)
        self.tables = np.array([
            sum((c + [[0] * 6] * (self.depth - len(c)) for c in t[0]), []) for t in tables
        ], np.int32).reshape(n, -1)
        self.flags = self.tables.shape[1]
        self.tables = np.concatenate([
            self.tables,
            np.array([
                [len(c) for c in t[0]] + t[3] + [s, self.starts[s]]
                + sum(([len(h)] + h + [0] * (self.depth - len(h)) for h in t[4]), [])
                for s, t in enumerate(tables)
            ], np.int32),
        ], axis=1)

    def tap(self, t):
        if t == 0:
            return (0, 1, 1)
        if t == 28:
            return None
        k, rest = (t - 1) // 9 + 1, (t - 1) % 9
        a, b = rest // 3, rest % 3
        if a != 1 and k not in self.shifted:
            return "zero"
        return (k, a, b)

    def table(self, s):
        parts = [[] for _ in range(self.n)]
        here = range(s * self.units, (s + 1) * self.units)
        slots = {}
        for k in range(4):
            for b in ((1,) if k == 0 else range(3)):
                if any(
                    isinstance(self.tap(u // self.n), tuple)
                    and (self.tap(u // self.n)[0], self.tap(u // self.n)[2]) == (k, b)
                    for u in here
                ):
                    slots[(k, b)] = len(slots)
        for unit in here:
            c, tap = unit % self.n, self.tap(unit // self.n)
            local = unit - s * self.units
            if tap is None or tap == "zero":
                parts[c].append([0, 0, 0, 0, 1 if tap is None else 2, local])
                continue
            k, a, b = tap
            move = (a - 1) * RATE * k
            valid = [
                j for j in range(self.n)
                if any(0 <= self.rows * j + i - move < self.height for i in range(self.rows))
            ]
            entry = [slots[(k, b)], move, valid[0], valid[-1] + 1, 0, local]
            if b == 2 and len(parts[c]) > 1 and all(
                e[4] == 0 and e[:4] == [entry[0] - back] + entry[1:4]
                for back, e in ((1, parts[c][-1]), (2, parts[c][-2]))
            ):
                parts[c][-2][4] = 3
                parts[c][-1][4] = 4
                entry[4] = 4
            parts[c].append(entry)
        want = [slots.get((k, b), -1) for k in range(4) for b in range(3)]
        heads = [[i for i, e in enumerate(c) if e[4] != 4] for c in parts]
        return parts, len(slots), max(len(c) for c in parts), want, heads


def pack_kernel(pix, x_ref, lab_ref, out_ref):
    x = x_ref[...]
    out_ref[:pix, :] = x
    total = jnp.sum(x.astype(F32), axis=0, keepdims=True)
    head = total.astype(BF16).astype(F32)
    mid = (total - head).astype(BF16).astype(F32)
    row = lax.broadcasted_iota(jnp.int32, (EXTRA, x.shape[1]), 0)
    extra = jnp.zeros((EXTRA, x.shape[1]), F32)
    for at, value in enumerate((head, mid, total - head - mid, lab_ref[...])):
        extra = jnp.where(row == at, value, extra)
    out_ref[pix:, :] = extra.astype(BF16)


def block_kernel(plan, n_cand, n_slots, aliased, meta, *refs):
    rows, cols, c_in, c_out = plan.rows, plan.cols, plan.c_in, plan.c_out
    pix = plan.pix
    cands = refs[:n_cand]
    w_hbm = refs[n_cand]
    refs = refs[n_cand + 1 + (4 if aliased else 0):]
    xt_out, cat_out, s_out, aux_out = refs[:4]
    xin, wbuf, xtb, catb, sb, res, sem_x, sem_w, sem_o, sem_s = refs[4:]
    step = pl.program_id(0)
    block, field = meta[step, 1], meta[step, 2]
    now = lax.rem(step, 2)
    xbuf = xin.at[now, pl.ds(0, pix)]

    def fetch(at, slot):
        for c in range(n_cand):
            @pl.when(meta[at, 0] == c)
            def _(c=c):
                pltpu.make_async_copy(cands[c], xin.at[slot], sem_x.at[slot]).start()

    def weights(group, taps):
        return [
            pltpu.make_async_copy(
                w_hbm.at[tap], wbuf.at[group, :, pl.ds(i * c_out, c_out)], sem_w.at[group, i]
            )
            for i, tap in enumerate(taps)
        ]

    @pl.when(step == 0)
    def _():
        fetch(0, 0)
        for group, taps in enumerate(plan.loads):
            for copy in weights(group, taps):
                copy.start()
        res[:, :EDGE, :] = jnp.zeros((rows, EDGE, res.shape[2]), F32)
        res[:, EDGE + cols:, :] = jnp.zeros((rows, EDGE, res.shape[2]), F32)

    if n_slots > 1:
        @pl.when(step + 1 < n_slots)
        def _():
            fetch(step + 1, 1 - now)

    pltpu.make_async_copy(cands[0], xin.at[now], sem_x.at[now]).wait()
    aux_copy = pltpu.make_async_copy(
        xin.at[now, pl.ds(pix, EXTRA)], aux_out.at[field, block], sem_o.at[2]
    )
    aux_copy.start()
    eye = identity(256)
    for c in range(c_in // 256):
        part = slice(c * 256, (c + 1) * 256)
        xtb[part, :] = nt(eye, xbuf[:, part]).astype(BF16)
    xt_copy = pltpu.make_async_copy(xtb, xt_out.at[field, block], sem_o.at[0])
    xt_copy.start()

    def in_field(move):
        first = block * rows + move
        return jnp.logical_and(first + rows - 1 >= 0, first < plan.height)

    def loaded(group, taps):
        @pl.when(step == 0)
        def _():
            for copy in weights(group, taps):
                copy.wait()

    def columns(k, first):
        r = RATE * k
        part = [slice(first + i * c_out, first + (i + 1) * c_out) for i in range(3)]
        return (
            res[:, EDGE - r:EDGE - r + cols, part[0]]
            + res[:, EDGE:EDGE + cols, part[1]]
            + res[:, EDGE + r:EDGE + r + cols, part[2]]
        )

    def relu_to(k, value):
        at = plan.direct.index(k)
        catb[:, at * c_out:(at + 1) * c_out] = (
            jnp.maximum(value, 0.0).astype(BF16).reshape(pix, c_out)
        )

    def shifted_copy(at):
        return pltpu.make_async_copy(
            sb.at[at], s_out.at[at, field, pl.ds(block * rows, rows)], sem_s.at[at]
        )

    group = 0
    first = c_out
    loaded(0, plan.loads[0])
    width = len(plan.loads[0]) * c_out
    res[:, EDGE:EDGE + cols, :width] = nn(xbuf[...], wbuf[0, :, :width]).reshape(
        rows, cols, width
    )
    relu_to(0, res[:, EDGE:EDGE + cols, :c_out])
    group = 1
    for k in plan.direct[1:]:
        if first + 3 * c_out > width:
            loaded(group, plan.loads[group])
            width, first = 3 * c_out, 0
            res[:, EDGE:EDGE + cols, :width] = nn(xbuf[...], wbuf[group, :, :width]).reshape(
                rows, cols, width
            )
            group += 1
        relu_to(k, columns(k, first))
        first += 3 * c_out
    cat_copy = pltpu.make_async_copy(catb, cat_out.at[field, block], sem_o.at[1])
    cat_copy.start()
    width = 3 * c_out
    for at, k in enumerate(plan.shifted):
        for a in range(3):
            loaded(group + 3 * at + a, plan.loads[group + 3 * at + a])

        def one(a, _, k=k, at=at, base=group + 3 * at):
            @pl.when(in_field((1 - a) * RATE * k))
            def _():
                res[:, EDGE:EDGE + cols, :width] = nn(
                    xbuf[...], wbuf[base + a, :, :width]
                ).reshape(rows, cols, width)
                sb[3 * at + a] = columns(k, 0)
                shifted_copy(3 * at + a).start()
            return 0

        lax.fori_loop(0, 3, one, 0)
    aux_copy.wait()
    xt_copy.wait()
    cat_copy.wait()
    for at, k in enumerate(plan.shifted):
        for a in range(3):
            @pl.when(in_field((1 - a) * RATE * k))
            def _(at=at, a=a):
                shifted_copy(3 * at + a).wait()


def run_blocks(plan, slots, meta, w_in, state):
    arrays = [value for cands in slots for value in cands]
    n, rows, cols, pix = plan.n, plan.rows, plan.cols, plan.pix
    c_in, c_out, n_sh = plan.c_in, plan.c_out, plan.n_sh
    shapes = [
        jax.ShapeDtypeStruct((2, n, c_in, pix), BF16),
        jax.ShapeDtypeStruct((2, n, pix, len(plan.direct) * c_out), BF16),
        jax.ShapeDtypeStruct((3 * n_sh, 2, n * rows, cols, c_out), F32),
        jax.ShapeDtypeStruct((2, n, EXTRA, c_in), BF16),
    ]
    widest = max(len(g) for g in plan.loads) * c_out
    aliased = state is not None
    operands = [*arrays, w_in] + (list(state) if aliased else [])
    aliases = {1 + len(arrays) + 1 + i: i for i in range(4)} if aliased else {}
    return pl.pallas_call(
        functools.partial(block_kernel, plan, len(arrays), len(slots), aliased),
        grid_spec=pltpu.PrefetchScalarGridSpec(
            num_scalar_prefetch=1,
            grid=(len(slots),),
            in_specs=[pl.BlockSpec(memory_space=pl.ANY)] * len(operands),
            out_specs=[pl.BlockSpec(memory_space=pl.ANY)] * 4,
            scratch_shapes=[
                pltpu.VMEM((2, pix + EXTRA, c_in), BF16),
                pltpu.VMEM((len(plan.loads), c_in, widest), BF16),
                pltpu.VMEM((c_in, pix), BF16),
                pltpu.VMEM((pix, len(plan.direct) * c_out), BF16),
                pltpu.VMEM((3 * n_sh, rows, cols, c_out), F32),
                pltpu.VMEM((rows, cols + 2 * EDGE, widest), F32),
                pltpu.SemaphoreType.DMA((2,)),
                pltpu.SemaphoreType.DMA((len(plan.loads), 4)),
                pltpu.SemaphoreType.DMA((3,)),
                pltpu.SemaphoreType.DMA((3 * n_sh,)),
            ],
        ),
        out_shape=shapes,
        input_output_aliases=aliases,
        compiler_params=pltpu.CompilerParams(
            dimension_semantics=("arbitrary",), vmem_limit_bytes=plan.vmem
        ),
        cost_estimate=pl.CostEstimate(
            flops=len(slots) * 2 * pix * c_in * c_out * (10 + 6 * n_sh),
            bytes_accessed=20_000_000 + len(slots) * 20_000_000,
            transcendentals=0,
        ),
        name="block_forward",
    )(meta, *operands)


def field_kernel(plan, field, last, tab, *refs):
    n, rows, cols, pix = plan.n, plan.rows, plan.cols, plan.pix
    c_in, c_out, n_sh = plan.c_in, plan.c_out, plan.n_sh
    unit_rows, depth, flags = plan.unit_rows, plan.depth, plan.flags
    cat_ref = refs[0]
    mid_refs = refs[1:1 + n_sh]
    s_hbm = refs[1 + n_sh]
    refs = refs[2 + n_sh:]
    aux_ref, all_ref, w28_ref, wproj_ref, wturn_ref, wcls_ref, cw_ref, xt_hbm = refs[:8]
    refs = refs[8:]
    if last:
        prev_g, prev_p, prev_c = refs[:3]
        refs = refs[3:]
    g_out, p_out, c_ref_out = refs[:3]
    side_refs = refs[3:3 + 2 * n_sh]
    (dbuf, pad, mean, ybuf, lbuf, dybuf, gp, spool, pact, catall, acc, stage, xt_ref, sem_xt,
     sems, sem_s) = refs[3 + 2 * n_sh:]
    xt_copy = pltpu.make_async_copy(xt_hbm.at[field], xt_ref, sem_xt)
    step = pl.program_id(0)
    edge_rows = rows - 1
    nb, turns = plan.together, n // plan.together

    def finish(value, prev):
        grad = value.astype(BF16)
        if not last:
            return grad
        return (prev.astype(F32) + grad.astype(F32)) * 0.5

    def side_copies():
        copies = []
        for at, k in enumerate(plan.shifted):
            for side in range(2):
                first, count = side * RATE * k, plan.height - RATE * k
                copies.append(pltpu.make_async_copy(
                    s_hbm.at[3 * at + 2 * side, field, pl.ds(first, count)],
                    side_refs[2 * at + side], sem_s.at[2 * at + side],
                ))
        return copies

    @pl.when(step == 0)
    def _():
        for copy in side_copies():
            copy.start()
        xt_copy.start()
        zero = jnp.zeros((edge_rows, cols, dbuf.shape[2]), BF16)
        dbuf[:edge_rows] = zero
        dbuf[edge_rows + plan.height:] = zero
        pad[:, :EDGE, :] = jnp.zeros((nb * rows, EDGE, c_out), F32)
        pad[:, EDGE + cols:, :] = jnp.zeros((nb * rows, EDGE, c_out), F32)
        total = jnp.zeros((1, c_in), F32)
        for j in range(n):
            extra = all_ref[j].astype(F32)
            total = total + ((extra[2:3] + extra[1:2]) + extra[0:1])
        mean_in = (total / plan.total).astype(BF16)
        mean[...] = jnp.broadcast_to(mean_in.astype(F32), (16, c_in))
        pact[...] = nn(mean[...].astype(BF16), w28_ref[0])
        for copy in side_copies():
            copy.wait()

    @pl.when(step < turns)
    def _():
        cat5 = catall.at[step]
        for k in range(4):
            part = slice(k * c_out, (k + 1) * c_out)
            if k in plan.shifted:
                at = plan.shifted.index(k)
                r = RATE * k
                pre = mid_refs[at]
                for i in range(nb * rows):
                    h = step * nb * rows + i
                    line = pre[i]
                    for side, src in ((0, h - r), (1, h)):
                        last_row = plan.height - r - 1
                        ok = jnp.logical_and(src >= 0, src <= last_row)
                        got = side_refs[2 * at + side][jnp.clip(src, 0, last_row)]
                        line = line + jnp.where(ok, got, 0.0)
                    cat5[i * cols:(i + 1) * cols, part] = jnp.maximum(line, 0.0).astype(BF16)
            else:
                at = plan.direct.index(k)
                cat5[:, part] = cat_ref[:, :, at * c_out:(at + 1) * c_out].reshape(nb * pix, c_out)
        pool_act = jnp.maximum(pact[0:1, :], 0.0).astype(BF16)
        cat5[:, 4 * c_out:] = jnp.broadcast_to(pool_act, (nb * pix, c_out))
        y_pre = nn(cat5[...], wproj_ref[...])
        y_act = jnp.maximum(y_pre, 0.0).astype(BF16)
        ybuf[step] = y_act
        row = lax.broadcasted_iota(jnp.int32, (16, pix), 0)
        live = row < plan.classes
        for sub in range(nb):
            cells = slice(sub * pix, (sub + 1) * pix)
            logits = nt(wcls_ref[...], y_act[cells])
            expo = jnp.where(live, jnp.exp(logits), 0.0)
            prob = expo / jnp.sum(expo, axis=0, keepdims=True)
            label = jnp.broadcast_to(aux_ref[sub, 3:4, :pix].astype(F32), (16, pix))
            onehot = jnp.where(label == row.astype(F32), 1.0, 0.0)
            weight = jnp.zeros((16, pix), F32)
            for c in range(plan.classes):
                weight = jnp.where(label == float(c), cw_ref[c], weight)
            d_logits = jnp.where(
                live, (prob - onehot) * weight * (LOSS_SCALE / plan.total), 0.0
            ).astype(BF16)
            lbuf[step * nb + sub] = d_logits
            dybuf[step, cells] = jnp.where(
                y_pre[cells] > 0, tn(d_logits, wcls_ref[...]), 0.0
            ).astype(BF16)
        d_y = dybuf[step]
        for k in range(4):
            want = [tab[flags + n + 3 * k + b] for b in range(3)]
            part = slice(k * c_out, (k + 1) * c_out)

            @pl.when((want[0] >= 0) | (want[1] >= 0) | (want[2] >= 0))
            def _(k=k, want=want, part=part):
                d_cat = nn(d_y, wturn_ref[:, part])
                d_k = jnp.where(cat5[:, part] > 0, d_cat, 0.0).astype(BF16)
                d_k = d_k.reshape(nb * rows, cols, c_out)
                if k > 0:
                    pad[:, EDGE:EDGE + cols, :] = d_k.astype(F32)
                at = pl.ds(step * nb * rows + edge_rows, nb * rows)
                for b in range(3):
                    if k == 0 and b != 1:
                        continue

                    @pl.when(want[b] >= 0)
                    def _(b=b):
                        lanes = pl.ds(pl.multiple_of(jnp.maximum(want[b], 0) * c_out, c_out), c_out)
                        if b == 1:
                            dbuf[at, :, lanes] = d_k
                        else:
                            first = EDGE + (1 - b) * RATE * k
                            dbuf[at, :, lanes] = pad[:, first:first + cols, :].astype(BF16)

    @pl.when(step == turns - 1)
    def _():
        all_dy = dybuf[...].reshape(n * pix, c_out)
        pool = wproj_ref[4 * c_out:, :]
        rest = nn(jnp.ones((16, n * pix), BF16), all_dy)
        total = jnp.zeros(rest.shape, F32)
        for _i in range(3):
            head = rest.astype(BF16)
            total = total + nt(head, pool)
            rest = rest - head.astype(F32)
        spool[...] = jnp.where(pact[...] > 0, jnp.broadcast_to(total[0:1, :], total.shape), 0.0)
        window = pl.ds(pl.multiple_of(tab[flags + n + 13], 128), plan.window)
        g_proj = jnp.zeros((c_out, plan.window), F32)
        g_cls = jnp.zeros((16, c_out), F32)
        for j in range(turns):
            g_proj = g_proj + nn(
                nt(identity(c_out), dybuf[j]).astype(BF16), catall[j, :, window]
            )
        for j in range(n):
            cells = slice(j % nb * pix, (j % nb + 1) * pix)
            g_cls = g_cls + nn(lbuf[j], ybuf[j // nb, cells])
        gp[:plan.window, :] = g_proj.T
        index = tab[flags + n + 12]
        first = pl.multiple_of(index * plan.proj_rows - tab[flags + n + 13], 32)
        p_out[...] = finish(gp[pl.ds(first, plan.proj_rows), :], prev_p[...] if last else None)
        gp[:c_out, :128] = jnp.concatenate([g_cls, jnp.zeros((112, c_out), F32)], axis=0).T
        first = pl.multiple_of(index * plan.cls_rows, plan.cls_rows)
        mine = finish(gp[pl.ds(first, plan.cls_rows), :128], prev_c[...] if last else None)
        c_ref_out[...] = mine[:, :c_ref_out.shape[1]]

    def out_copy(part, slot, t):
        row = tab[(part * depth + t) * 6 + 5] * unit_rows
        return pltpu.make_async_copy(
            stage.at[slot, t],
            g_out.at[pl.ds(pl.multiple_of(row, unit_rows), unit_rows)],
            sems.at[slot, t],
        )

    @pl.when(step == turns)
    def _():
        xt_copy.wait()

    @pl.when(step >= turns)
    def _():
        part = step - turns
        parity = lax.rem(part, 2)
        mine = pl.ds(pl.multiple_of(part * unit_rows, unit_rows), unit_rows)

        heads = flags + n + 14 + part * (depth + 1)

        def one(i, _):
            t = tab[heads + 1 + i]
            base = (part * depth + t) * 6
            slot, move, low, high = tab[base], tab[base + 1], tab[base + 2], tab[base + 3]
            kind = tab[base + 4]

            def product(taps):
                width = taps * c_out
                lanes = pl.ds(pl.multiple_of(slot * c_out, c_out), width)

                def term(j):
                    first = j * rows - move + edge_rows
                    return nn(xt_ref[j, mine, :], dbuf[pl.ds(first, rows), :, lanes].reshape(pix, width))

                whole = jnp.logical_and(low == 0, high == n)

                @pl.when(whole)
                def _():
                    total = term(0)
                    for j in range(1, n):
                        total = total + term(j)
                    acc[:, :width] = total

                @pl.when(jnp.logical_not(whole))
                def _():
                    acc[:, :width] = jnp.zeros((unit_rows, width), F32)

                    def add(j, _):
                        acc[:, :width] += term(j)
                        return 0

                    lax.fori_loop(low, high, add, 0)

            @pl.when(kind == 3)
            def _():
                product(3)

            @pl.when(kind == 0)
            def _():
                product(1)

            @pl.when(kind == 2)
            def _():
                acc[:, :c_out] = jnp.zeros((unit_rows, c_out), F32)

            @pl.when(kind == 1)
            def _():
                first = pl.multiple_of(part * unit_rows, unit_rows)
                row = mean[0:1, pl.ds(first, unit_rows)]
                column = jnp.broadcast_to(row, (128, unit_rows)).T
                for c in range(c_out // 128):
                    lanes = slice(c * 128, (c + 1) * 128)
                    acc[:, lanes] = column * spool[0:1, lanes]

            def emit(at, lanes):
                if last:
                    stage[parity, at] = finish(acc[:, lanes], prev_g[at])
                    out_copy(part, parity, at).start()
                else:
                    g_out[at] = finish(acc[:, lanes], None)

            emit(t, slice(0, c_out))

            @pl.when(kind == 3)
            def _():
                for b in (1, 2):
                    emit(t + b, slice(b * c_out, (b + 1) * c_out))

            return 0

        lax.fori_loop(0, tab[heads], one, 0)

        if last:
            def drain(which, slot):
                def one(t, _):
                    out_copy(which, slot, t).wait()
                    return 0
                lax.fori_loop(0, tab[flags + which], one, 0)

            @pl.when(part > 0)
            def _():
                drain(part - 1, 1 - parity)

            @pl.when(part == n - 1)
            def _():
                drain(part, parity)


def run_field(plan, field, tab, state, w_in, w_proj, w_turn, wcls, cw, prev):
    n, rows, cols, pix = plan.n, plan.rows, plan.cols, plan.pix
    c_in, c_out, n_sh = plan.c_in, plan.c_out, plan.n_sh
    unit_rows, depth = plan.unit_rows, plan.depth
    last = prev is not None
    nb, turns = plan.together, n // plan.together
    xt, cat, s, aux = state

    def blk(i):
        return jnp.minimum(i, turns - 1)

    def part(i):
        return jnp.maximum(i - turns, 0)

    in_specs = [
        pl.BlockSpec(
            (None, nb, pix, len(plan.direct) * c_out), lambda i, t: (field, blk(i), 0, 0)
        ),
    ]
    operands = [cat]
    for at in range(n_sh):
        in_specs.append(pl.BlockSpec(
            (None, None, nb * rows, cols, c_out),
            lambda i, t, at=at: (3 * at + 1, field, blk(i), 0, 0),
        ))
        operands.append(s)
    in_specs.append(pl.BlockSpec(memory_space=pl.ANY))
    operands.append(s)
    in_specs += [
        pl.BlockSpec((None, nb, EXTRA, c_in), lambda i, t: (field, blk(i), 0, 0)),
        pl.BlockSpec((None, n, EXTRA, c_in), lambda i, t: (field, 0, 0, 0)),
        pl.BlockSpec((1, c_in, c_out), lambda i, t: (28, 0, 0)),
        pl.BlockSpec((5 * c_out, c_out), lambda i, t: (0, 0)),
        pl.BlockSpec((c_out, 4 * c_out), lambda i, t: (0, 0)),
        pl.BlockSpec((16, c_out), lambda i, t: (0, 0)),
        pl.BlockSpec(memory_space=pltpu.SMEM),
        pl.BlockSpec(memory_space=pl.ANY),
    ]
    operands += [aux, aux, w_in, w_proj, w_turn, wcls, cw, xt]
    kind = F32 if last else BF16
    out_lanes = plan.classes if last else 128
    inner = pl.BlockSpec((None, depth, unit_rows, c_out), lambda i, t: (part(i), 0, 0, 0))
    small = [
        pl.BlockSpec((plan.proj_rows, c_out), lambda i, t: (0, 0)),
        pl.BlockSpec((plan.cls_rows, 128), lambda i, t: (0, 0)),
    ]
    out_small = [small[0], pl.BlockSpec((plan.cls_rows, out_lanes), lambda i, t: (0, 0))]
    if last:
        in_specs += [inner] + small
        operands += list(prev)
        main_spec = pl.BlockSpec(memory_space=pl.ANY)
        main_shape = jax.ShapeDtypeStruct((plan.units * unit_rows, c_out), F32)
    else:
        main_spec = inner
        main_shape = jax.ShapeDtypeStruct((n, depth, unit_rows, c_out), BF16)
    return pl.pallas_call(
        functools.partial(field_kernel, plan, field, last),
        grid_spec=pltpu.PrefetchScalarGridSpec(
            num_scalar_prefetch=1,
            grid=(turns + n,),
            in_specs=in_specs,
            out_specs=[main_spec] + out_small,
            scratch_shapes=[
                pltpu.VMEM((plan.height - RATE * k, cols, c_out), F32)
                for k in plan.shifted for _ in range(2)
            ] + [
                pltpu.VMEM((plan.height + 2 * (rows - 1), cols, plan.n_slots * c_out), BF16),
                pltpu.VMEM((nb * rows, cols + 2 * EDGE, c_out), F32),
                pltpu.VMEM((16, c_in), F32),
                pltpu.VMEM((turns, nb * pix, c_out), BF16),
                pltpu.VMEM((n, 16, pix), BF16),
                pltpu.VMEM((turns, nb * pix, c_out), BF16),
                pltpu.VMEM((max(plan.window, c_out), c_out), F32),
                pltpu.VMEM((16, c_out), F32),
                pltpu.VMEM((16, c_out), F32),
                pltpu.VMEM((turns, nb * pix, 5 * c_out), BF16),
                pltpu.VMEM((unit_rows, 3 * c_out), F32),
                pltpu.VMEM((2, depth if last else 1, unit_rows, c_out), F32),
                pltpu.VMEM((n, c_in, pix), BF16),
                pltpu.SemaphoreType.DMA,
                pltpu.SemaphoreType.DMA((2, depth)),
                pltpu.SemaphoreType.DMA((2 * n_sh,)),
            ],
        ),
        out_shape=[
            main_shape,
            jax.ShapeDtypeStruct((plan.proj_rows, c_out), kind),
            jax.ShapeDtypeStruct((plan.cls_rows, out_lanes), kind),
        ],
        compiler_params=pltpu.CompilerParams(
            dimension_semantics=("arbitrary",), vmem_limit_bytes=plan.vmem
        ),
        cost_estimate=pl.CostEstimate(
            flops=10_000_000_000, bytes_accessed=90_000_000, transcendentals=0
        ),
        name="field_grads",
    )(tab, *operands)


def after(value, *others):
    return lax.optimization_barrier((value, *others))[0]


def per_device(plan, features, labels, w_in, w_proj, w_cls, class_weight, matching):
    n, reps, rows, pix, c_in = plan.n, plan.reps, plan.rows, plan.pix, plan.c_in
    names = jnp.pad(labels[0].reshape(1, pix).astype(F32), ((0, 0), (0, c_in - pix)))
    x = pl.pallas_call(
        functools.partial(pack_kernel, pix),
        out_shape=jax.ShapeDtypeStruct((pix + EXTRA, c_in), BF16),
        name="pack",
    )(features[0].reshape(pix, c_in), names)
    here = lax.axis_index("space")
    n_bits = reps.bit_length() - 1
    bits = [jnp.bitwise_and(jnp.right_shift(matching[0], b), 1) == 1 for b in range(n_bits)]
    top = jnp.int32(0)
    for at, b in enumerate(list(range(1, n_bits)) + [0]):
        top = jnp.where(bits[b], n_bits - 1 - at, top)
    tab = jnp.asarray(plan.tables)[here]
    wcls = jnp.pad(w_cls.T, ((0, 16 - plan.classes), (0, 0)))

    def along(value, way, step):
        pairs = [
            (i, i + way) for i in range(n)
            if 0 <= i + way < n and 0 <= i - way * (step - 1) < n
        ]
        return lax.ppermute(value, "space", pairs)

    def hop(value, b):
        return lax.ppermute(value, "rep", [(r, r ^ (1 << b)) for r in range(reps)])

    order = np.array(
        [sorted(range(n), key=lambda j: (abs(j - s), j)) for s in range(n)], np.int32
    )
    blocks = jnp.asarray(order)[here]

    def arrival(q, ups, downs):
        value = None
        for s in range(n):
            j = int(order[s, q])
            arrived = ups[s - j] if j < s else downs[j - s]
            value = arrived if value is None else jnp.where(here == s, arrived, value)
        return value

    w_turn = w_proj[:4 * plan.c_out].T
    hops = list(range(1, n_bits)) + [0]
    rounds = n + n_bits - 1
    ups, downs, raw = [x], [x], (x, x)
    turns = []
    for t in range(1, rounds + 1):
        turn = [(t - 1, 0)] if t - 1 < n else []
        if t == rounds:
            turn += [(q, 1) for q in range(max(0, n + 1 - n_bits), n)]
        elif t >= n_bits and t <= n:
            turn.append((t - n_bits, 1))
        turns.append(turn)
    metas = [
        jnp.stack([
            jnp.stack([(top if f else 0) + jnp.int32(n_bits * at if f and turn[0][1] else at),
                       blocks[q], jnp.int32(f)])
            for at, (q, f) in enumerate(turn)
        ]) if turn else None
        for turn in turns
    ]
    values, moves = {0: x}, {q: [] for q in range(n)}
    state, grads = None, None
    for t in range(1, rounds + 1):
        q = t - 1
        if 0 < q < n:
            values[q] = arrival(q, ups, downs)
        for i in range(1, n_bits):
            if 0 <= q - i < n:
                values[q - i] = jnp.where(bits[hops[i - 1]], moves[q - i][0], values[q - i])
        for i in reversed(range(n_bits)):
            if 0 <= q - i < n:
                moves[q - i].insert(0, hop(values[q - i], hops[i]))
        if t < n:
            raw = along(raw[0], 1, t), along(raw[1], -1, t)
            ups.append(raw[0])
            downs.append(raw[1])
        slots = [moves[at] if f else [values[at]] for at, f in turns[q]]
        if slots:
            state = run_blocks(plan, slots, metas[q], w_in, state)
        if q == min(n, rounds - 1):
            grads = tuple(run_field(
                plan, 0, tab, state, w_in, w_proj, w_turn, wcls, class_weight, None
            ))
        if t < rounds:
            live = (ups, downs, values, moves, state, grads, metas, tab, wcls, w_turn)
            live = lax.optimization_barrier(live)
            ups, downs, values, moves, state, grads, metas, tab, wcls, w_turn = live
    avg_in, avg_proj, avg_cls = run_field(
        plan, 1, tab, state, w_in, w_proj, w_turn, wcls, class_weight, grads
    )
    return avg_in[None], avg_proj[None], avg_cls[None]


def solution(mesh):
    n, reps = mesh.shape["space"], mesh.shape["rep"]

    def build(features, labels, w_in, w_proj, w_cls, class_weight, matching):
        _, rows, cols, c_in = features.shape
        plan = Plan(n, reps, rows // n, cols, c_in, w_proj.shape[1], w_cls.shape[1])
        return jax.shard_map(
            functools.partial(per_device, plan),
            mesh=mesh,
            in_specs=(P("rep", "space", None, None), P("rep", "space", None), P(), P(), P(), P(), P()),
            out_specs=(P("rep", "space", None), P("rep", "space", None), P("rep", "space", None)),
            check_vma=False,
        )(features, labels, w_in, w_proj, w_cls, class_weight, matching)

    return build
```
